512 devices in a mesh: dp: 16 (over z_lo, x, core), vocab: 32 (over z_hi, y).
Axes of the slice: x: 4, y: 8, z: 8 (z_hi: 4, z_lo: 2; z = z_hi * 2 + z_lo), core: 2. Of those that a mesh axis runs over, the one named last changes fastest.
Arguments:
- hidden: bfloat16 [4096, 1024], P(('dp', 'vocab')), may hold values from -8 to 8
- embed_grad: bfloat16 [4096, 1024], P(('dp', 'vocab')), may hold values from -6 to 6
- token_ids: int32 [4096], P(('dp', 'vocab')), may hold values from 0 to 126975
- lengths: int32 [32], P('dp'), may hold values from 32 to 128, as said below
- pool_index: int32 [32, 126976], P('dp', 'vocab'), may hold values from 0 to 127, as said below
- embedding: bfloat16 [1024, 126976], P('dp', 'vocab'), may hold values from -0.1875 to 0.1875
- head_bias: float32 [126976], P('vocab'), may hold values from -5 to 5
- pooled_grad: float32 [32, 126976], P('dp', 'vocab'), may hold values from -6 to 6
Outputs:
- hidden_grad: bfloat16 [4096, 1024], P(('dp', 'vocab'))
- embedding_grad: float32 [1024, 126976], P('dp', 'vocab')
- bias_grad: float32 [126976], P('vocab')
The draws below stay inside these ranges and needn't reach their ends.
Inputs may be any that keep to these rules, and one draw needn't show every extreme that they name: `lengths`: passage 0 has all 128 tokens live. pool_index[p, v] is below lengths[p]; pool_index[0, 0] = 127.
All inputs are finite; a program needn't handle non-finite values.
Results may differ from the reference program's by a relative error of at most 0.011.
Values may be sent and summed in bfloat16 or wider, within the bound.
No kernel may reach another device: no remote copies, remote signals or barrier semaphores. Data moves between devices by JAX's collectives and lax.ppermute only.
A program may use at most 64 MiB of HBM per device.

```python
import math
import jax
import jax.numpy as jnp
import numpy as np
from jax import lax

D = 1024
SEQ = 128
PASSAGES = 32
TOKENS = 4096
V = 126976


def passage_lengths(key):
    inner = jax.random.fold_in(key, 11)
    counts = jax.random.randint(inner, (PASSAGES,), SEQ // 4, SEQ + 1)
    return counts.at[0].set(SEQ)


def draw_lengths(key, part):
    return passage_lengths(key).astype(jnp.int32)


def draw_pool_index(key, part):
    counts = passage_lengths(key)
    key = jax.random.fold_in(key, 2)
    raw = jax.random.randint(key, (PASSAGES, V), 0, 65536)
    spots = raw % counts[:, None]
    return spots.at[0, 0].set(SEQ - 1).astype(jnp.int32)


def draw_hidden(key, part):
    key = jax.random.fold_in(key, 3)
    passage = jnp.arange(TOKENS) // SEQ
    ramp = 0.6 * jnp.power(3.0, passage.astype(jnp.float32) / max(PASSAGES - 1, 1))
    values = jnp.clip(jax.random.normal(key, (TOKENS, D), jnp.float32), -4.0, 4.0)
    return (values * ramp[:, None]).astype(jnp.bfloat16)


def set_ends(values, key, least, high):
    spot = [jax.random.randint(jax.random.fold_in(key, axis), (), 0, length) for axis, length in enumerate(values.shape)]
    main_axis = values.shape.index(max(values.shape))
    next_to = spot[:main_axis] + [(spot[main_axis] + 1) % values.shape[main_axis]] + spot[main_axis + 1:]
    return values.at[tuple(spot)].set(least).at[tuple(next_to)].set(high)


def level_of(own_key, shape, cuts, low, high):
    level = 1.0
    for axis_at, parts in cuts:
        draws = jax.random.uniform(jax.random.fold_in(jax.random.fold_in(own_key, 6), axis_at), (parts,), jnp.float32, low / len(cuts), high / len(cuts))
        level = level * jnp.repeat(jnp.exp(draws), shape[axis_at] // parts).reshape((-1,) + (1,) * (len(shape) - 1 - axis_at))
    return level


def skewed_wide(rng, dims, number_of, skew):
    portions = [min(1 << octave, number_of + 1 - (1 << octave)) * (1 << 20) // math.isqrt((1 << octave) ** skew) + 1 for octave in range((number_of + 1).bit_length()) if 1 << octave <= number_of]
    scale = 1 + sum(portions) // (1 << 30)
    table = np.cumsum(np.array([max(1, weight // scale) for weight in portions]))
    lot = jax.random.randint(jax.random.fold_in(rng, 1), dims, 0, int(table[len(portions) - 1]))
    start = jnp.left_shift(1, jnp.searchsorted(jnp.asarray(table, jnp.int32), lot, side="right").astype(jnp.int32))
    grade = start - 1 + jax.random.randint(jax.random.fold_in(rng, 4), dims, 0, 1 << 30) % jnp.minimum(start, number_of + 1 - start)
    return jax.random.permutation(jax.random.fold_in(rng, 2), number_of)[grade].astype(jnp.int32)


def scatter_about(key, extent, width, most, cuts=(), kind=jnp.bfloat16):
    array = jax.random.normal(key, extent, jnp.float32) * width
    if len(cuts) > 0:
        array = level_of(key, extent, cuts, -0.22, 0.18) * array
    return jnp.clip(array, min=-most, max=most).astype(kind)


def setup_inputs(seed: int = 0) -> dict:
    key_of = jax.random.split(jax.random.key(seed), 9)
    return {
        "hidden": draw_hidden(jax.random.fold_in(key_of[8], 71), 0),
        "embed_grad": scatter_about(key_of[1], (TOKENS, D), 1.0, 6.0, ((0, 512),)),
        "token_ids": set_ends(skewed_wide(key_of[2], (TOKENS,), V, 2), jax.random.fold_in(key_of[2], 3), 0, V - 1).astype(jnp.int32),
        "lengths": draw_lengths(jax.random.fold_in(key_of[8], 71), 0),
        "pool_index": draw_pool_index(jax.random.fold_in(key_of[8], 71), 0),
        "embedding": scatter_about(key_of[5], (D, V), D ** -0.5, 0.1875, ((0, 16), (1, 32))),
        "head_bias": scatter_about(key_of[6], (V,), 1.0, 5.0, ((0, 32),), jnp.float32),
        "pooled_grad": scatter_about(key_of[7], (PASSAGES, V), 1.0, 6.0, ((0, 16), (1, 32)), jnp.float32),
    }


def reference(hidden, embed_grad, token_ids, lengths, pool_index, embedding, head_bias, pooled_grad):
    table = jnp.transpose(embedding).astype(jnp.float32)
    grouped = hidden.reshape(PASSAGES, SEQ, D)

    def pick(pieces):
        passage_rows, chosen_spot = pieces
        chosen = jnp.take(passage_rows, chosen_spot, axis=0).astype(jnp.float32)
        return jnp.sum(chosen * table, axis=1)

    logits = lax.map(pick, (grouped, pool_index)) + head_bias[None, :]
    softened = jax.nn.softplus(logits)
    pooled = jnp.log1p(softened)
    slope = jax.nn.sigmoid(logits) / (1.0 + softened)
    mean_pooled = jnp.sum(pooled, axis=0) / PASSAGES
    logit_grad = ((pooled_grad + mean_pooled[None, :]) * slope).astype(jnp.bfloat16)
    weights = logit_grad.astype(jnp.float32)
    bias_grad = jnp.sum(weights, axis=0)

    def spread(pieces):
        weight_row, chosen_spot = pieces
        return jax.ops.segment_sum(weight_row[:, None] * table, chosen_spot, num_segments=SEQ)

    hidden_grad = lax.map(spread, (weights, pool_index)).reshape(TOKENS, D).astype(jnp.bfloat16)

    def collect(total, pieces):
        weight_row, chosen_spot, passage_rows = pieces
        chosen = jnp.take(passage_rows, chosen_spot, axis=0).astype(jnp.float32)
        return total + weight_row[:, None] * chosen, None

    decoder_grad, _ = lax.scan(collect, jnp.zeros((V, D), jnp.float32), (weights, pool_index, grouped))
    position = jnp.arange(TOKENS, dtype=jnp.int32) % SEQ
    live = position < jnp.repeat(lengths, SEQ)
    masked = jnp.where(live[:, None], embed_grad.astype(jnp.float32), 0.0)
    full_grad = decoder_grad + jax.ops.segment_sum(masked, token_ids, num_segments=V)
    return hidden_grad, jnp.transpose(full_grad), bias_grad
```

```python
import functools

import jax
import jax.numpy as jnp
from jax import lax
from jax.experimental import pallas as pl
from jax.experimental.pallas import tpu as pltpu
from jax.sharding import PartitionSpec as P

F32 = jnp.float32
BF16 = jnp.bfloat16
I16 = jnp.int16
I32 = jnp.int32
LANES = 128
PARAMS = pltpu.CompilerParams(vmem_limit_bytes=48 * 1024 * 1024)
SMEM = pl.BlockSpec(memory_space=pltpu.SMEM)
VMEM = pl.BlockSpec(memory_space=pltpu.VMEM)

GROUPS = 16
SHARDS = 32
SEQ = 128
PASSAGES = 32
COLS = 64
ROWS = 8
TILES = 31
VOC = TILES * LANES
CHUNK = 256


def lane_gather(table, index):
    numbers = lax.GatherDimensionNumbers(
        offset_dims=(),
        collapsed_slice_dims=(1,),
        start_index_map=(1,),
        operand_batching_dims=(0,),
        start_indices_batching_dims=(0,),
    )
    return lax.gather(
        table,
        index[..., None],
        numbers,
        (1, 1),
        mode=lax.GatherScatterMode.PROMISE_IN_BOUNDS,
    )


def pack_body(place_ref, lengths_ref, ids_ref, hidden_ref, grad_ref, index_ref, out_ref, rows):
    place = place_ref[0]
    limit = lengths_ref[place // (SEQ // ROWS)]
    spot = (place % (SEQ // ROWS)) * ROWS + lax.broadcasted_iota(I32, (ROWS, 1), 0)
    hidden = hidden_ref[...].astype(F32)
    masked = jnp.where(spot < limit, grad_ref[...].astype(F32), 0.0)
    row = lax.broadcasted_iota(I32, (ROWS, LANES), 0)
    lane = lax.broadcasted_iota(I32, (ROWS, LANES), 1)
    ids = jnp.zeros((ROWS, LANES), I32)
    for r in range(ROWS):
        ids = jnp.where(row == r, ids_ref[r], ids)
    digits = jnp.where(lane == 0, ids & 127, jnp.where(lane == 1, (ids >> 7) & 127, ids >> 14))
    digits = jnp.where(lane < 3, digits, 0).astype(F32)
    rows[...] = jnp.zeros_like(rows)
    for tile in range(TILES):
        rows[2 * tile : 2 * tile + 2, :] = index_ref[:, tile * LANES : (tile + 1) * LANES].astype(F32)
    spots = rows[...].astype(BF16)
    for g in range(GROUPS):
        own = jnp.concatenate(
            [hidden[:, g * COLS : (g + 1) * COLS], masked[:, g * COLS : (g + 1) * COLS]], axis=1
        )
        out_ref[g, 0:16, :] = jnp.concatenate([own, digits], axis=0).astype(BF16)
        out_ref[g, 16:80, :] = spots


def spread_body(got_ref, hidden_out, grad_out):
    hidden = []
    grads = []
    digits = []
    for g in range(GROUPS):
        block = got_ref[g, 0:16, :].astype(F32)
        hidden.append(block[0:8, 0:COLS])
        grads.append(block[0:8, COLS:])
        digits.append(block[8:16, :])
    hidden = jnp.concatenate(
        [jnp.concatenate([hidden[g], hidden[g + 1]], axis=1) for g in range(0, GROUPS, 2)], axis=0
    ).astype(BF16)
    grads = jnp.concatenate(
        [jnp.concatenate([grads[g], grads[g + 1]], axis=1) for g in range(0, GROUPS, 2)], axis=0
    ).astype(BF16)
    digits = jnp.concatenate(digits[0::2] + digits[1::2], axis=0).T[0:16, :].astype(BF16)
    for s in range(SHARDS):
        hidden_out[s] = hidden
        grad_out[s, 0:64, :] = grads
        grad_out[s, 64:80, :] = digits


def logits_body(hidden_ref, got_ref, embed_ref, pooled_ref, out_ref, table_ref, spots):
    for pair in range(4):
        for half in range(2):
            block = hidden_ref[half * 16 : half * 16 + 16, pair * 16 : pair * 16 + 16, :].astype(F32)
            for s in range(2):
                turned = block[:, s * 8 : s * 8 + 8, :].reshape(SEQ, LANES).T.astype(BF16)
                first = 4 * (2 * pair + s) + half
                table_ref[first] = turned[0:COLS]
                table_ref[first + 2] = turned[COLS:]
    for g in range(GROUPS):
        spots[g] = got_ref[g, 16:80, :].astype(I32)

    def one_tile(tile, carry):
        at = pl.multiple_of(tile * LANES, LANES)
        embed = embed_ref[:, pl.ds(at, LANES)].astype(F32)
        lane_at = pl.multiple_of((tile % 2) * LANES, LANES)
        for p in range(PASSAGES):
            index = spots[p // 2, pl.ds(2 * tile + p % 2, 1), :]
            index = jnp.broadcast_to(index, (16, LANES)).astype(I16)
            total = jnp.zeros((8, LANES), F32)
            for d in range(0, COLS, 16):
                picked = lane_gather(table_ref[p, d : d + 16, :], index).astype(F32)
                product = picked * embed[d : d + 16]
                total = total + product[0:8] + product[8:16]
            out_ref[tile // 2, p : p + 1, pl.ds(lane_at, LANES)] = jnp.sum(total, axis=0, keepdims=True)
        out_ref[tile // 2, 32:34, pl.ds(lane_at, LANES)] = pooled_ref[:, pl.ds(at, LANES)]
        return carry

    lax.fori_loop(0, TILES, one_tile, 0)
    out_ref[GROUPS - 1, :, LANES:] = jnp.zeros((40, LANES), F32)


def slope_body(part_ref, bias_ref, out_ref):
    total = part_ref[0, 0:32, :]
    for g in range(1, GROUPS):
        total = total + part_ref[g, 0:32, :]
    logits = total + bias_ref[...]
    softened = jnp.maximum(logits, 0.0) + jnp.log1p(jnp.exp(-jnp.abs(logits)))
    pooled = jnp.log1p(softened)
    sigmoid = 1.0 / (1.0 + jnp.exp(-logits))
    slope = sigmoid / (1.0 + softened)
    mean_pooled = jnp.sum(pooled, axis=0, keepdims=True) / PASSAGES
    upstream = jnp.concatenate([part_ref[g, 32:34, :] for g in range(GROUPS)], axis=0)
    grad = ((upstream + mean_pooled) * slope).astype(BF16)
    for g in range(GROUPS):
        out_ref[g] = grad


def hidden_body(grad_ref, got_ref, embed_ref, out_ref, spots, grads, total):
    for g in range(GROUPS):
        spots[g] = got_ref[g, 16:80, :].astype(I32)
    total[...] = jnp.zeros_like(total)
    here = lax.broadcasted_iota(I32, (SEQ, LANES), 0).astype(I16)
    zero = jnp.zeros((), BF16)

    def one_chunk(chunk, width):
        at = pl.multiple_of(chunk * CHUNK, CHUNK)
        embed = embed_ref[:, pl.ds(at, width)]
        blank = jnp.zeros((COLS, width), BF16)
        right = jnp.concatenate(
            [jnp.concatenate([embed, blank], axis=1), jnp.concatenate([blank, embed], axis=1)], axis=0
        )
        grads[...] = grad_ref[chunk].astype(F32)

        def weights(p):
            parts = []
            for tile in range(width // LANES):
                index = spots[p // 2, pl.ds(4 * chunk + 2 * tile + p % 2, 1), :]
                index = jnp.broadcast_to(index, (16, LANES)).astype(I16)
                value = grads[p : p + 1, tile * LANES : (tile + 1) * LANES]
                value = jnp.broadcast_to(value, (16, LANES)).astype(BF16)
                index = jnp.concatenate([index] * 8, axis=0)
                value = jnp.concatenate([value] * 8, axis=0)
                parts.append(jnp.where(index == here, value, zero))
            return parts

        for pair in range(8):
            for half in range(2):
                first = 4 * pair + half
                left = jnp.concatenate(weights(first) + weights(first + 2), axis=1)
                product = lax.dot_general(
                    left, right, (((1,), (1,)), ((), ())), preferred_element_type=F32
                )
                rows = (slice(half * 16, half * 16 + 16), slice(pair * 8, pair * 8 + 8))
                total[rows] += product.reshape(16, 8, LANES)

    def loop(chunk, carry):
        one_chunk(chunk, CHUNK)
        return carry

    lax.fori_loop(0, GROUPS - 1, loop, 0)
    one_chunk(GROUPS - 1, LANES)
    out_ref[...] = total[...].astype(BF16)


def token_body(place_ref, got_ref, out_ref, left, right):
    base = place_ref[0] * VOC
    low_row = lax.broadcasted_iota(I32, (512, LANES), 0)
    out_ref[...] = jnp.zeros_like(out_ref)

    def one_block(block, carry):
        for s in range(8):
            shard = block * 8 + s
            rows = got_ref[shard].astype(F32)
            digits = rows[64:72].astype(I32)
            local = (digits[2:3] << 14) + (digits[1:2] << 7) + digits[0:1] - base
            high = local >> 9
            low = local & 511
            turned = rows[0:64].T
            grads = jnp.concatenate([turned[0:COLS], turned[COLS:]], axis=1)
            lanes = slice(s * LANES, (s + 1) * LANES)
            for h in range(8):
                left[h * COLS : (h + 1) * COLS, lanes] = jnp.where(high == h, grads, 0.0).astype(BF16)
            right[:, lanes] = jnp.where(low_row == low, 1.0, 0.0).astype(BF16)
        for h in range(8):
            out_ref[:, h * 512 : (h + 1) * 512] += lax.dot_general(
                left[h * COLS : (h + 1) * COLS, :],
                right[...],
                (((1,), (1,)), ((), ())),
                preferred_element_type=F32,
            )
        return carry

    lax.fori_loop(0, 4, one_block, 0)


def embed_body(grad_ref, got_ref, table_ref, token_ref, out_ref, bias_ref, spots, grads):
    for g in range(GROUPS):
        spots[g] = got_ref[g, 16:80, :].astype(I32)
        grads[g] = grad_ref[g].astype(F32)

    def one_tile(tile, carry):
        at = pl.multiple_of(tile * LANES, LANES)
        lane_at = pl.multiple_of((tile % 2) * LANES, LANES)
        totals = [token_ref[d : d + 16, pl.ds(at, LANES)] for d in range(0, COLS, 16)]
        for p in range(PASSAGES):
            index = spots[p // 2, pl.ds(2 * tile + p % 2, 1), :]
            index = jnp.broadcast_to(index, (16, LANES)).astype(I16)
            value = grads[tile // 2, p : p + 1, pl.ds(lane_at, LANES)]
            for n in range(COLS // 16):
                picked = lane_gather(table_ref[p, n * 16 : n * 16 + 16, :], index).astype(F32)
                totals[n] = totals[n] + picked * value
        for n in range(COLS // 16):
            out_ref[n * 16 : n * 16 + 16, pl.ds(at, LANES)] = totals[n]
        bias_ref[:, pl.ds(at, LANES)] = jnp.sum(
            grads[tile // 2, :, pl.ds(lane_at, LANES)], axis=0, keepdims=True
        )
        return carry

    lax.fori_loop(0, TILES, one_tile, 0)


def sum_body(part_ref, out_ref):
    total = part_ref[0].astype(F32)
    for s in range(1, SHARDS):
        total = total + part_ref[s].astype(F32)
    for g in range(GROUPS):
        rows = total[(g // 2) * 8 : (g // 2) * 8 + 8, :]
        if g % 2:
            rows = jnp.concatenate([rows[:, COLS:], rows[:, :COLS]], axis=1)
        out_ref[g] = rows


def call(body, name, out, scratch=(), specs=None, flops=0, reads=0):
    return pl.pallas_call(
        body,
        out_shape=out,
        in_specs=specs,
        scratch_shapes=scratch,
        compiler_params=PARAMS,
        cost_estimate=pl.CostEstimate(flops=flops, bytes_accessed=reads, transcendentals=0),
        name=name,
    )


def shape(dims, dtype):
    return jax.ShapeDtypeStruct(dims, dtype)


def exchange(x, axis):
    return lax.all_to_all(x, axis, split_axis=0, concat_axis=0, tiled=True)


def on_device(
    hidden, embed_grad, token_ids, lengths, pool_index, embedding, head_bias, pooled_grad
):
    place = lax.axis_index("vocab").astype(I32).reshape(1)
    packed = call(
        pack_body,
        "pack",
        shape((GROUPS, 80, LANES), BF16),
        [pltpu.VMEM((64, LANES), F32)],
        [SMEM, SMEM, SMEM, VMEM, VMEM, VMEM],
    )(place, lengths, token_ids, hidden, embed_grad, pool_index)
    got = exchange(packed, "dp")
    hidden_rows, grad_rows = call(
        spread_body,
        "spread",
        (shape((SHARDS, 64, LANES), BF16), shape((SHARDS, 80, LANES), BF16)),
        specs=[VMEM],
    )(got)
    all_hidden = exchange(hidden_rows, "vocab")
    all_grads = exchange(grad_rows, "vocab")
    partial, table = call(
        logits_body,
        "logits",
        (shape((GROUPS, 40, CHUNK), F32), shape((PASSAGES, COLS, LANES), BF16)),
        [pltpu.VMEM((GROUPS, 64, LANES), I32)],
        [VMEM, VMEM, VMEM, VMEM],
    )(all_hidden, got, embedding, pooled_grad)
    parts = exchange(partial, "dp")
    bias = jnp.pad(head_bias, (0, GROUPS * CHUNK - VOC)).reshape(GROUPS, 1, CHUNK)
    bias = lax.dynamic_index_in_dim(bias, lax.axis_index("dp"), 0, keepdims=False)
    grad_block = call(
        slope_body, "slope", shape((GROUPS, PASSAGES, CHUNK), BF16), specs=[VMEM, VMEM]
    )(parts, bias)
    all_grad = exchange(grad_block, "dp")
    hidden_parts = call(
        hidden_body,
        "hidden_grad",
        shape((SHARDS, 64, LANES), BF16),
        [
            pltpu.VMEM((GROUPS, 64, LANES), I32),
            pltpu.VMEM((PASSAGES, CHUNK), F32),
            pltpu.VMEM((SHARDS, 64, LANES), F32),
        ],
        [VMEM, VMEM, VMEM],
    )(all_grad, got, embedding)
    hidden_got = exchange(hidden_parts, "vocab")
    token_grad = call(
        token_body,
        "token_grad",
        shape((COLS, 4096), F32),
        [pltpu.VMEM((512, 1024), BF16), pltpu.VMEM((512, 1024), BF16)],
        [SMEM, VMEM],
    )(place, all_grads)
    embedding_grad, bias_grad = call(
        embed_body,
        "embedding_grad",
        (shape((COLS, VOC), F32), shape((1, VOC), F32)),
        [pltpu.VMEM((GROUPS, 64, LANES), I32), pltpu.VMEM((GROUPS, PASSAGES, CHUNK), F32)],
        [VMEM, VMEM, VMEM, VMEM],
    )(all_grad, got, table, token_grad)
    hidden_sum = call(sum_body, "sum_shards", shape((GROUPS, ROWS, LANES), F32), specs=[VMEM])(
        hidden_got
    )
    blocks = exchange(hidden_sum, "dp")
    hidden_grad = blocks[:, :, :COLS].transpose(1, 0, 2).reshape(ROWS, GROUPS * COLS).astype(BF16)
    return hidden_grad, embedding_grad, bias_grad.reshape(VOC)


def solution(mesh):
    return jax.shard_map(
        on_device,
        mesh=mesh,
        in_specs=(
            P(("dp", "vocab"), None),
            P(("dp", "vocab"), None),
            P(("dp", "vocab")),
            P("dp"),
            P("dp", "vocab"),
            P("dp", "vocab"),
            P("vocab"),
            P("dp", "vocab"),
        ),
        out_specs=(P(("dp", "vocab"), None), P("dp", "vocab"), P("vocab")),
        check_vma=False,
    )
```

```python
import jax
import jax.numpy as jnp
from jax import lax
from jax.experimental import pallas as pl
from jax.experimental.pallas import tpu as pltpu
from jax.sharding import Mesh, PartitionSpec as P

F32 = jnp.float32
BF16 = jnp.bfloat16
I16 = jnp.int16
I32 = jnp.int32
LANES = 128
PARAMS = pltpu.CompilerParams(vmem_limit_bytes=48 * 1024 * 1024)
SMEM = pl.BlockSpec(memory_space=pltpu.SMEM)
VMEM = pl.BlockSpec(memory_space=pltpu.VMEM)

GROUP = ("zl", "x", "core")
SHARD = ("zh", "y")
PLANE = ("zl", "zh", "y")
ROW = ("x", "core")
GROUPS = 16
SHARDS = 32
PEERS = 8
SEQ = 128
PASSAGES = 32
COLS = 64
HALF = 512
ROWS = 8
TILES = 31
VOC = TILES * LANES
PAD = 4096


def lane_gather(table, index):
    numbers = lax.GatherDimensionNumbers(
        offset_dims=(),
        collapsed_slice_dims=(1,),
        start_index_map=(1,),
        operand_batching_dims=(0,),
        start_indices_batching_dims=(0,),
    )
    return lax.gather(
        table,
        index[..., None],
        numbers,
        (1, 1),
        mode=lax.GatherScatterMode.PROMISE_IN_BOUNDS,
    )


def pack_body(
    place_ref, lengths_ref, ids_ref, hidden_ref, grad_ref, index_ref, pooled_ref, hidden_out, grad_out, side_out
):
    place = place_ref[0]
    limit = lengths_ref[place // (SEQ // ROWS)]
    spot = (place % (SEQ // ROWS)) * ROWS + lax.broadcasted_iota(I32, (ROWS, 1), 0)
    hidden = hidden_ref[...]
    masked = jnp.where(spot < limit, grad_ref[...].astype(F32), 0.0)
    row = lax.broadcasted_iota(I32, (ROWS, LANES), 0)
    lane = lax.broadcasted_iota(I32, (ROWS, LANES), 1)
    ids = jnp.zeros((ROWS, LANES), I32)
    for r in range(ROWS):
        ids = jnp.where(row == r, ids_ref[r], ids)
    digits = jnp.where(lane == 0, ids & 127, jnp.where(lane == 1, (ids >> 7) & 127, ids >> 14))
    digits = jnp.where(lane < 3, digits, 0).astype(F32)
    for half in range(2):
        cols = slice(half * HALF, (half + 1) * HALF)
        own = hidden[:, cols]
        rest = jnp.concatenate([masked[:, cols], digits], axis=1).astype(BF16)
        for s in range(SHARDS):
            hidden_out[half * SHARDS + s] = own
            grad_out[half * SHARDS + s] = rest
    side = jnp.concatenate([pooled_ref[...], index_ref[...].astype(F32)], axis=0)
    for g in range(GROUPS):
        side_out[g, :, 0:VOC] = side
        side_out[g, :, VOC:] = jnp.zeros((4, PAD - VOC), F32)


def logits_body(place_ref, hidden_ref, side_ref, embed_ref, out_ref):
    row = place_ref[1]
    here = lax.broadcasted_iota(I32, (SEQ, 1), 0).astype(F32)

    def one_chunk(at, width):
        dense = jnp.dot(
            hidden_ref[...], embed_ref[:, pl.ds(at, width)], preferred_element_type=F32
        )
        picked = []
        for n in range(4):
            index = side_ref[(n // 2) * PEERS + row, 2 + n % 2 : 3 + n % 2, pl.ds(at, width)]
            scores = dense[n * SEQ : (n + 1) * SEQ]
            picked.append(jnp.sum(jnp.where(index == here, scores, 0.0), axis=0, keepdims=True))
        picked = jnp.concatenate(picked, axis=0)
        for g in range(GROUPS):
            out_ref[g, :, pl.ds(at, width)] = picked

    def loop(chunk, carry):
        one_chunk(pl.multiple_of(chunk * 256, 256), 256)
        return carry

    lax.fori_loop(0, VOC // 256, loop, 0)
    one_chunk(VOC - 128, 128)


def hidden_body(
    place_ref, part_ref, side_ref, bias_ref, embed_ref, out_ref, grad_ref, bias_out, total, left
):
    row = place_ref[1]
    here = lax.broadcasted_iota(I32, (SEQ, LANES), 0).astype(I16)
    zero = jnp.zeros((), BF16)
    total[...] = jnp.zeros_like(total)

    def slopes(at, width):
        lanes = pl.ds(at, width)
        logits = jnp.concatenate(
            [part_ref[x, :, lanes] + part_ref[PEERS + x, :, lanes] for x in range(PEERS)], axis=0
        )
        upstream = jnp.concatenate(
            [side_ref[z * PEERS + x, 0:2, lanes] for x in range(PEERS) for z in range(2)], axis=0
        )
        logits = logits + bias_ref[:, lanes]
        softened = jnp.maximum(logits, 0.0) + jnp.log1p(jnp.exp(-jnp.abs(logits)))
        pooled = jnp.log1p(softened)
        sigmoid = 1.0 / (1.0 + jnp.exp(-logits))
        slope = sigmoid / (1.0 + softened)
        mean_pooled = jnp.sum(pooled, axis=0, keepdims=True) / PASSAGES
        grad = ((upstream + mean_pooled) * slope).astype(BF16).astype(F32)
        for x in range(PEERS):
            grad_ref[x, :, lanes] = grad[4 * x : 4 * x + 4]
        bias_out[:, lanes] = jnp.sum(grad, axis=0, keepdims=True)

    def one_chunk(at, width):
        slopes(at, width)
        for n in range(4):
            for tile in range(width // LANES):
                lanes = pl.ds(at + tile * LANES, LANES)
                index = side_ref[(n // 2) * PEERS + row, 2 + n % 2 : 3 + n % 2, lanes]
                index = jnp.broadcast_to(index, (16, LANES)).astype(I32).astype(I16)
                value = grad_ref[row, n : n + 1, lanes]
                value = jnp.broadcast_to(value, (16, LANES)).astype(BF16)
                index = jnp.concatenate([index] * 8, axis=0)
                value = jnp.concatenate([value] * 8, axis=0)
                left[n * SEQ : (n + 1) * SEQ, tile * LANES : (tile + 1) * LANES] = jnp.where(
                    index == here, value, zero
                )
        total[...] += lax.dot_general(
            left[:, 0:width],
            embed_ref[:, pl.ds(at, width)],
            (((1,), (1,)), ((), ())),
            preferred_element_type=F32,
        )

    def loop(chunk, carry):
        one_chunk(pl.multiple_of(chunk * 512, 512), 512)
        return carry

    lax.fori_loop(0, 7, loop, 0)
    one_chunk(7 * 512, VOC - 7 * 512)
    out_ref[...] = total[...].astype(BF16)


def turn_body(hidden_ref, grad_ref, out_ref):
    digits = []
    for n in range(4):
        rows = slice(n * SEQ, (n + 1) * SEQ)
        hidden = hidden_ref[rows, :].astype(F32).T.astype(BF16)
        grads = grad_ref[rows, :].astype(F32)
        digits.append(grads[:, HALF:].T[0:8])
        grads = grads[:, 0:HALF].T.astype(BF16)
        for x in range(PEERS):
            out_ref[x, n * SEQ : n * SEQ + COLS, :] = hidden[x * COLS : (x + 1) * COLS]
            out_ref[x, n * SEQ + COLS : (n + 1) * SEQ, :] = grads[x * COLS : (x + 1) * COLS]
    digits = jnp.concatenate(digits, axis=0).astype(BF16)
    for x in range(PEERS):
        out_ref[x, HALF:, :] = digits


def embed_body(place_ref, grad_ref, side_ref, got_ref, out_ref, left, right, total):
    base = place_ref[0] * VOC
    low_row = lax.broadcasted_iota(I32, (HALF, LANES), 0).astype(I16)
    zero = jnp.zeros((), BF16)
    one = jnp.ones((), BF16)
    total[...] = jnp.zeros_like(total)

    def one_block(block, carry):
        for s in range(8):
            peer = block * 2 + s // 4
            n = s % 4
            digits = got_ref[peer, HALF + (n // 2) * 16 : HALF + (n // 2) * 16 + 16, :].astype(F32).astype(I32)
            digits = digits[(n % 2) * 8 : (n % 2) * 8 + 8]
            local = (digits[2:3] << 14) + (digits[1:2] << 7) + digits[0:1] - base
            inside = (local >= 0) & (local < VOC)
            high = jnp.where(inside, local >> 9, 15)
            high = jnp.broadcast_to(high, (16, LANES)).astype(I16)
            low = jnp.broadcast_to(local & 511, (16, LANES)).astype(I16)
            high = jnp.concatenate([high] * 4, axis=0)
            low = jnp.concatenate([low] * 32, axis=0)
            grads = got_ref[peer, n * SEQ + COLS : (n + 1) * SEQ, :]
            lanes = slice(s * LANES, (s + 1) * LANES)
            for h in range(8):
                left[h * COLS : (h + 1) * COLS, lanes] = jnp.where(high == jnp.int16(h), grads, zero)
            right[:, lanes] = jnp.where(low_row == low, one, zero)
        total[...] += lax.dot_general(
            left[...], right[...], (((1,), (1,)), ((), ())), preferred_element_type=F32
        )
        return carry

    lax.fori_loop(0, 4, one_block, 0)
    for h in range(8):
        width = min(HALF, VOC - h * HALF)
        out_ref[:, h * HALF : h * HALF + width] = total[h * COLS : (h + 1) * COLS, 0:width]

    def one_tile(tile, carry):
        lanes = pl.ds(pl.multiple_of(tile * LANES, LANES), LANES)
        totals = [out_ref[d : d + 16, lanes] for d in range(0, COLS, 16)]
        for q in range(PASSAGES):
            x, z, n = q // 4, (q // 2) % 2, q % 2
            index = side_ref[z * PEERS + x, 2 + n : 3 + n, lanes]
            index = jnp.broadcast_to(index, (16, LANES)).astype(I32).astype(I16)
            value = grad_ref[x, q % 4 : q % 4 + 1, lanes]
            for d in range(COLS // 16):
                at = (q % 4) * SEQ + d * 16
                picked = lane_gather(got_ref[x, at : at + 16, :], index).astype(F32)
                totals[d] = totals[d] + picked * value
        for d in range(COLS // 16):
            out_ref[d * 16 : d * 16 + 16, lanes] = totals[d]
        return carry

    lax.fori_loop(0, TILES, one_tile, 0)


def sum_body(part_ref, out_ref):
    for half in range(2):
        total = part_ref[half * SHARDS].astype(F32)
        for s in range(1, SHARDS):
            total = total + part_ref[half * SHARDS + s].astype(F32)
        out_ref[:, half * HALF : (half + 1) * HALF] = total.astype(BF16)


def call(body, name, out, scratch=(), specs=None, us=1):
    return pl.pallas_call(
        body,
        out_shape=out,
        in_specs=specs,
        scratch_shapes=scratch,
        compiler_params=PARAMS,
        cost_estimate=pl.CostEstimate(flops=0, bytes_accessed=3_700_000 * us, transcendentals=0),
        name=name,
    )


def shape(dims, dtype):
    return jax.ShapeDtypeStruct(dims, dtype)


def exchange(x, axis):
    return lax.all_to_all(x, axis, split_axis=0, concat_axis=0, tiled=True)


def on_device(
    hidden, embed_grad, token_ids, lengths, pool_index, embedding, head_bias, pooled_grad
):
    place = jnp.stack([lax.axis_index(SHARD), lax.axis_index(ROW)]).astype(I32)
    embed = lax.all_gather(embedding, ROW, axis=0, tiled=True)
    hidden_rows, grad_rows, side = call(
        pack_body,
        "pack",
        (
            shape((2 * SHARDS, ROWS, HALF), BF16),
            shape((2 * SHARDS, ROWS, HALF + LANES), BF16),
            shape((GROUPS, 4, PAD), F32),
        ),
        specs=[SMEM, SMEM, SMEM, VMEM, VMEM, VMEM, VMEM],
    )(place, lengths, token_ids, hidden, embed_grad, pool_index, pooled_grad)
    all_hidden = exchange(hidden_rows, PLANE).reshape(4 * SEQ, HALF)
    all_side = exchange(side, GROUP)
    all_grads = exchange(grad_rows, PLANE).reshape(4 * SEQ, HALF + LANES)
    partial = call(
        logits_body,
        "logits",
        shape((GROUPS, 4, VOC), F32),
        specs=[SMEM, VMEM, VMEM, VMEM],
        us=5,
    )(place, all_hidden, all_side, embed)
    parts = exchange(partial, GROUP)
    turned = call(
        turn_body,
        "turn",
        shape((PEERS, HALF + 32, LANES), BF16),
        specs=[VMEM, VMEM],
        us=3,
    )(all_hidden, all_grads)
    got = exchange(turned, ROW)
    hidden_parts, all_grad, bias_grad = call(
        hidden_body,
        "hidden_grad",
        (shape((4 * SEQ, HALF), BF16), shape((PEERS, 4, VOC), F32), shape((1, VOC), F32)),
        [pltpu.VMEM((4 * SEQ, HALF), F32), pltpu.VMEM((4 * SEQ, HALF), BF16)],
        [SMEM, VMEM, VMEM, VMEM, VMEM],
        us=8,
    )(place, parts, all_side, head_bias.reshape(1, VOC), embed)
    hidden_got = exchange(hidden_parts.reshape(2 * SHARDS, ROWS, HALF), PLANE)
    embedding_grad = call(
        embed_body,
        "embedding_grad",
        shape((COLS, VOC), F32),
        [
            pltpu.VMEM((HALF, 1024), BF16),
            pltpu.VMEM((HALF, 1024), BF16),
            pltpu.VMEM((HALF, HALF), F32),
        ],
        [SMEM, VMEM, VMEM, VMEM],
        us=16,
    )(place, all_grad, all_side, got)
    hidden_grad = call(sum_body, "sum_shards", shape((ROWS, 2 * HALF), BF16), specs=[VMEM])(
        hidden_got
    )
    return hidden_grad, embedding_grad, bias_grad.reshape(VOC)


def solution(mesh):
    fine = Mesh(mesh.devices.reshape(2, 4, 2, 4, 8), GROUP + SHARD)
    every = P(GROUP + SHARD, None)
    split = P(GROUP, SHARD)
    return jax.shard_map(
        on_device,
        mesh=fine,
        in_specs=(every, every, P(GROUP + SHARD), P(GROUP), split, split, P(SHARD), split),
        out_specs=(every, split, P(SHARD)),
        check_vma=False,
    )
```

```python
import jax
import jax.numpy as jnp
from jax import lax
from jax.experimental import pallas as pl
from jax.experimental.pallas import tpu as pltpu
from jax.sharding import Mesh, PartitionSpec as P

F32 = jnp.float32
BF16 = jnp.bfloat16
I16 = jnp.int16
I32 = jnp.int32
LANES = 128
SMEM = pl.BlockSpec(memory_space=pltpu.SMEM)
VMEM = pl.BlockSpec(memory_space=pltpu.VMEM)

GROUP = ("zl", "x", "core")
SHARD = ("zh", "y")
PLANE = ("zl", "zh", "y")
ROW = ("x", "core")
GROUPS = 16
SHARDS = 32
PEERS = 8
SEQ = 128
PASSAGES = 32
COLS = 64
HALF = 512
ROWS = 8
TILES = 31
VOC = TILES * LANES
PAD = 4096
ROOM = 56
STEP = 512
STEPS = 8


def lane_gather(table, index):
    numbers = lax.GatherDimensionNumbers(
        offset_dims=(),
        collapsed_slice_dims=(1,),
        start_index_map=(1,),
        operand_batching_dims=(0,),
        start_indices_batching_dims=(0,),
    )
    return lax.gather(
        table,
        index[..., None],
        numbers,
        (1, 1),
        mode=lax.GatherScatterMode.PROMISE_IN_BOUNDS,
    )


def pack_body(place_ref, lengths, ids, hidden, grad, index, pooled, row_out, side_out, *scratch):
    held, sem = scratch[:-1], scratch[-1]
    copies = [
        pltpu.make_async_copy(source, target, sem.at[n])
        for n, (source, target) in enumerate(zip((lengths, ids, hidden, grad, index, pooled), held))
    ]
    for copy in copies:
        copy.start()
    for copy in copies:
        copy.wait()
    lengths_ref, ids_ref, hidden_ref, grad_ref, index_ref, pooled_ref = held
    place = place_ref[0]
    limit = lengths_ref[place // (SEQ // ROWS)]
    spot = (place % (SEQ // ROWS)) * ROWS + lax.broadcasted_iota(I32, (ROWS, 1), 0)
    masked = jnp.where(spot < limit, grad_ref[...].astype(F32), 0.0).astype(BF16)
    row = lax.broadcasted_iota(I32, (ROWS, LANES), 0)
    lane = lax.broadcasted_iota(I32, (ROWS, LANES), 1)
    ids = jnp.zeros((ROWS, LANES), I32)
    for r in range(ROWS):
        ids = jnp.where(row == r, ids_ref[r], ids)
    digits = jnp.where(lane == 0, ids & 127, jnp.where(lane == 1, (ids >> 7) & 127, ids >> 14))
    digits = jnp.where(lane < 3, digits, 0).astype(F32).astype(BF16)
    for half in range(2):
        cols = slice(half * HALF, (half + 1) * HALF)
        own = jnp.concatenate([hidden_ref[:, cols], masked[:, cols], digits], axis=1)
        for s in range(SHARDS):
            row_out[half * SHARDS + s] = own
    side_out[:, 0:VOC] = jnp.concatenate([pooled_ref[...], index_ref[...].astype(F32)], axis=0)
    side_out[:, VOC:] = jnp.zeros((4, PAD - VOC), F32)


def logits_body(hidden_ref, index_ref, embed_ref, out_ref):
    here = lax.broadcasted_iota(I32, (SEQ, 1), 0)
    dense = jnp.dot(hidden_ref[...], embed_ref[...], preferred_element_type=F32)
    picked = []
    for n in range(4):
        scores = dense[n * SEQ : (n + 1) * SEQ]
        hit = index_ref[n : n + 1, :] == here
        picked.append(jnp.sum(jnp.where(hit, scores, 0.0), axis=0, keepdims=True))
    picked = jnp.concatenate(picked, axis=0)
    for g in range(GROUPS):
        out_ref[g] = picked


def hidden_body(
    place_ref, part_ref, side_ref, index_ref, bias_ref, embed_ref, out_ref, grad_ref, bias_out, total, left
):
    row = place_ref[1]
    step = pl.program_id(0)
    here = lax.broadcasted_iota(I32, (SEQ, LANES), 0).astype(I16)
    zero = jnp.zeros((), BF16)

    logits = jnp.concatenate([part_ref[x] + part_ref[PEERS + x] for x in range(PEERS)], axis=0)
    upstream = jnp.concatenate(
        [side_ref[z * PEERS + x, 0:2, :] for x in range(PEERS) for z in range(2)], axis=0
    )
    logits = logits + bias_ref[...]
    softened = jnp.maximum(logits, 0.0) + jnp.log1p(jnp.exp(-jnp.abs(logits)))
    pooled = jnp.log1p(softened)
    sigmoid = 1.0 / (1.0 + jnp.exp(-logits))
    slope = sigmoid / (1.0 + softened)
    mean_pooled = jnp.sum(pooled, axis=0, keepdims=True) / PASSAGES
    grad = ((upstream + mean_pooled) * slope).astype(BF16).astype(F32)
    for x in range(PEERS):
        grad_ref[x] = grad[4 * x : 4 * x + 4]
    bias_out[...] = jnp.sum(grad, axis=0, keepdims=True)

    def scatter(width):
        for n in range(4):
            for tile in range(width // LANES):
                lanes = slice(tile * LANES, (tile + 1) * LANES)
                index = jnp.broadcast_to(index_ref[n : n + 1, lanes], (16, LANES)).astype(I16)
                value = jnp.broadcast_to(grad_ref[row, n : n + 1, lanes], (16, LANES)).astype(BF16)
                index = jnp.concatenate([index] * 8, axis=0)
                value = jnp.concatenate([value] * 8, axis=0)
                left[n * SEQ : (n + 1) * SEQ, lanes] = jnp.where(index == here, value, zero)
        return lax.dot_general(
            left[:, 0:width],
            embed_ref[:, 0:width],
            (((1,), (1,)), ((), ())),
            preferred_element_type=F32,
        )

    @pl.when(step == 0)
    def first():
        total[...] = scatter(STEP)

    @pl.when((step > 0) & (step < STEPS - 1))
    def middle():
        total[...] += scatter(STEP)

    @pl.when(step == STEPS - 1)
    def last():
        out_ref[...] = (total[...] + scatter(VOC - (STEPS - 1) * STEP)).astype(BF16)


def turn_body(rows_ref, out_ref):
    digits = []
    for n in range(4):
        rows = rows_ref[n * SEQ : (n + 1) * SEQ, :].astype(F32)
        digits.append(rows[:, 2 * HALF :].T[0:8])
        hidden = rows[:, 0:HALF].T.astype(BF16)
        grads = rows[:, HALF : 2 * HALF].T.astype(BF16)
        for x in range(PEERS):
            out_ref[x, n * SEQ : n * SEQ + COLS, :] = hidden[x * COLS : (x + 1) * COLS]
            out_ref[x, n * SEQ + COLS : (n + 1) * SEQ, :] = grads[x * COLS : (x + 1) * COLS]
    digits = jnp.concatenate(digits, axis=0).astype(BF16)
    for x in range(PEERS):
        out_ref[x, HALF:, :] = digits


def embed_body(place_ref, grad_ref, side_ref, got_ref, out_ref, left, right, total):
    base = place_ref[0] * VOC
    low_row = lax.broadcasted_iota(I32, (HALF, LANES), 0).astype(I16)
    zero = jnp.zeros((), BF16)
    one = jnp.ones((), BF16)
    total[...] = jnp.zeros_like(total)

    def one_block(block, carry):
        for s in range(8):
            peer = block * 2 + s // 4
            n = s % 4
            digits = got_ref[peer, HALF + (n // 2) * 16 : HALF + (n // 2) * 16 + 16, :].astype(F32).astype(I32)
            digits = digits[(n % 2) * 8 : (n % 2) * 8 + 8]
            local = (digits[2:3] << 14) + (digits[1:2] << 7) + digits[0:1] - base
            inside = (local >= 0) & (local < VOC)
            high = jnp.where(inside, local >> 9, 15)
            high = jnp.broadcast_to(high, (16, LANES)).astype(I16)
            low = jnp.broadcast_to(local & 511, (16, LANES)).astype(I16)
            high = jnp.concatenate([high] * 4, axis=0)
            low = jnp.concatenate([low] * 32, axis=0)
            grads = got_ref[peer, n * SEQ + COLS : (n + 1) * SEQ, :]
            lanes = slice(s * LANES, (s + 1) * LANES)
            for h in range(8):
                left[h * COLS : (h + 1) * COLS, lanes] = jnp.where(high == jnp.int16(h), grads, zero)
            right[:, lanes] = jnp.where(low_row == low, one, zero)
        total[...] += lax.dot_general(
            left[...], right[...], (((1,), (1,)), ((), ())), preferred_element_type=F32
        )
        return carry

    lax.fori_loop(0, 4, one_block, 0)
    for h in range(8):
        width = min(HALF, VOC - h * HALF)
        out_ref[:, h * HALF : h * HALF + width] = total[h * COLS : (h + 1) * COLS, 0:width]

    def one_tile(tile, carry):
        lanes = pl.ds(pl.multiple_of(tile * LANES, LANES), LANES)
        totals = [out_ref[d : d + 16, lanes] for d in range(0, COLS, 16)]
        for q in range(PASSAGES):
            x, z, n = q // 4, (q // 2) % 2, q % 2
            index = side_ref[z * PEERS + x, 2 + n : 3 + n, lanes]
            index = jnp.broadcast_to(index, (16, LANES)).astype(I32).astype(I16)
            value = grad_ref[x, q % 4 : q % 4 + 1, lanes]
            for d in range(COLS // 16):
                at = (q % 4) * SEQ + d * 16
                picked = lane_gather(got_ref[x, at : at + 16, :], index).astype(F32)
                totals[d] = totals[d] + picked * value
        for d in range(COLS // 16):
            out_ref[d * 16 : d * 16 + 16, lanes] = totals[d]
        return carry

    lax.fori_loop(0, TILES, one_tile, 0)


def sum_body(part_ref, out_ref):
    for half in range(2):
        total = part_ref[half * SHARDS].astype(F32)
        for s in range(1, SHARDS):
            total = total + part_ref[half * SHARDS + s].astype(F32)
        out_ref[:, half * HALF : (half + 1) * HALF] = total.astype(BF16)


def call(body, name, out, scratch=(), specs=None, us=1, grid=(), out_specs=None, room=ROOM):
    extra = {key: value for key, value in (("grid", grid), ("out_specs", out_specs)) if value}
    return pl.pallas_call(
        body,
        out_shape=out,
        in_specs=specs,
        scratch_shapes=scratch,
        compiler_params=pltpu.CompilerParams(vmem_limit_bytes=room * 1024 * 1024),
        cost_estimate=pl.CostEstimate(flops=0, bytes_accessed=3_700_000 * us, transcendentals=0),
        name=name,
        **extra,
    )


def shape(dims, dtype):
    return jax.ShapeDtypeStruct(dims, dtype)


def chunk(*dims):
    return pl.BlockSpec(dims + (STEP,), lambda i: (0,) * len(dims) + (i,))


def whole(*dims):
    return pl.BlockSpec(dims, lambda i: (0,) * len(dims))


def exchange(x, axis):
    return lax.all_to_all(x, axis, split_axis=0, concat_axis=0, tiled=True)


def on_device(
    hidden, embed_grad, token_ids, lengths, pool_index, embedding, head_bias, pooled_grad
):
    place = jnp.stack([lax.axis_index(SHARD), lax.axis_index(ROW)]).astype(I32)
    width = 2 * HALF + LANES
    rows, side = call(
        pack_body,
        "pack",
        (shape((2 * SHARDS, ROWS, width), BF16), shape((4, PAD), F32)),
        [
            pltpu.SMEM((2,), I32),
            pltpu.SMEM((ROWS,), I32),
            pltpu.VMEM((ROWS, 2 * HALF), BF16),
            pltpu.VMEM((ROWS, 2 * HALF), BF16),
            pltpu.VMEM((2, VOC), I32),
            pltpu.VMEM((2, VOC), F32),
            pltpu.SemaphoreType.DMA((6,)),
        ],
        [SMEM] + [pl.BlockSpec(memory_space=pl.ANY)] * 6,
        room=ROOM,
    )(place, lengths, token_ids, hidden, embed_grad, pool_index, pooled_grad)
    embedding, rows = lax.optimization_barrier((embedding, rows))
    embed = lax.all_gather(embedding, ROW, axis=0, tiled=True)
    all_rows = exchange(rows, PLANE).reshape(4 * SEQ, width)
    index = lax.all_gather(pool_index, "zl", axis=0, tiled=True)
    side, embed = lax.optimization_barrier((side, embed))
    all_side = lax.all_gather(side, GROUP, axis=0, tiled=False)
    turned = call(
        turn_body,
        "turn",
        shape((PEERS, HALF + 32, LANES), BF16),
        specs=[VMEM],
        us=2,
    )(all_rows)
    got = exchange(turned, ROW)
    partial = call(
        logits_body,
        "logits",
        shape((GROUPS, 4, VOC), F32),
        specs=[whole(4 * SEQ, HALF), chunk(4), chunk(HALF)],
        out_specs=chunk(GROUPS, 4),
        grid=(STEPS,),
        us=6,
    )(all_rows, index, embed)
    partial, got = lax.optimization_barrier((partial, got))
    parts = exchange(partial, GROUP)
    hidden_parts, all_grad, bias_grad = call(
        hidden_body,
        "hidden_grad",
        (shape((4 * SEQ, HALF), BF16), shape((PEERS, 4, VOC), F32), shape((1, VOC), F32)),
        [pltpu.VMEM((4 * SEQ, HALF), F32), pltpu.VMEM((4 * SEQ, STEP), BF16)],
        [SMEM, chunk(GROUPS, 4), chunk(GROUPS, 4), chunk(4), chunk(1), chunk(HALF)],
        out_specs=(whole(4 * SEQ, HALF), chunk(PEERS, 4), chunk(1)),
        grid=(STEPS,),
        us=7,
    )(place, parts, all_side, index, head_bias.reshape(1, VOC), embed)
    hidden_got = exchange(hidden_parts.reshape(2 * SHARDS, ROWS, HALF), PLANE)
    embedding_grad = call(
        embed_body,
        "embedding_grad",
        shape((COLS, VOC), F32),
        [
            pltpu.VMEM((HALF, 1024), BF16),
            pltpu.VMEM((HALF, 1024), BF16),
            pltpu.VMEM((HALF, HALF), F32),
        ],
        [SMEM, VMEM, VMEM, VMEM],
        us=16,
    )(place, all_grad, all_side, got)
    hidden_grad = call(sum_body, "sum_shards", shape((ROWS, 2 * HALF), BF16), specs=[VMEM])(
        hidden_got
    )
    return hidden_grad, embedding_grad, bias_grad.reshape(VOC)


def solution(mesh):
    fine = Mesh(mesh.devices.reshape(2, 4, 2, 4, 8), GROUP + SHARD)
    every = P(GROUP + SHARD, None)
    split = P(GROUP, SHARD)
    return jax.shard_map(
        on_device,
        mesh=fine,
        in_specs=(every, every, P(GROUP + SHARD), P(GROUP), split, split, P(SHARD), split),
        out_specs=(every, split, P(SHARD)),
        check_vma=False,
    )
```

```python
import jax
import jax.numpy as jnp
from jax import lax
from jax.experimental import pallas as pl
from jax.experimental.pallas import tpu as pltpu
from jax.sharding import Mesh, PartitionSpec as P

F32 = jnp.float32
BF16 = jnp.bfloat16
I16 = jnp.int16
I32 = jnp.int32
LANES = 128
SMEM = pl.BlockSpec(memory_space=pltpu.SMEM)
VMEM = pl.BlockSpec(memory_space=pltpu.VMEM)
ANY = pl.BlockSpec(memory_space=pl.ANY)

GROUP = ("zl", "x", "core")
SHARD = ("zh", "y")
HOME = ("zl", "x", "zh", "y")
GROUPS = 16
SHARDS = 32
CHIPS = 8
SEQ = 128
PASSAGES = 32
OWN = 16
COLS = 64
PAIR = 128
WIDTH = 8 * PAIR
ROWS = 8
TILES = 31
VOC = TILES * LANES
CHUNK = 256
STEP = 512
STEPS = 8
ROOM = 56
CARRY = 4 * 2 * PAIR + LANES


def lane_gather(table, index):
    numbers = lax.GatherDimensionNumbers(
        offset_dims=(),
        collapsed_slice_dims=(1,),
        start_index_map=(1,),
        operand_batching_dims=(0,),
        start_indices_batching_dims=(0,),
    )
    return lax.gather(
        table,
        index[..., None],
        numbers,
        (1, 1),
        mode=lax.GatherScatterMode.PROMISE_IN_BOUNDS,
    )


def slot(place_ref, m):
    return ((m // 4) ^ place_ref[2]) * 4 + ((place_ref[3] - m % 4) & 3)


def turned_spot(index):
    return ((index & 3) << 5) | (index >> 2)


def pack_body(place_ref, lengths, ids, hidden, grad, out_ref, *scratch):
    held, block, sem, out_sem = scratch[:4], scratch[4], scratch[5], scratch[6]
    copies = [
        pltpu.make_async_copy(source, target, sem.at[n])
        for n, (source, target) in enumerate(zip((lengths, ids, hidden, grad), held))
    ]
    for copy in copies:
        copy.start()
    for copy in copies:
        copy.wait()
    lengths_ref, ids_ref, hidden_ref, grad_ref = held
    place = place_ref[0]
    swap = place_ref[1] == 1
    limit = lengths_ref[place // (SEQ // ROWS)]
    spot = (place % (SEQ // ROWS)) * ROWS + lax.broadcasted_iota(I32, (ROWS, 1), 0)
    rows = [hidden_ref[...].astype(F32), jnp.where(spot < limit, grad_ref[...].astype(F32), 0.0)]
    row = lax.broadcasted_iota(I32, (2, LANES), 0)
    lane = lax.broadcasted_iota(I32, (2, LANES), 1)
    digits = jnp.zeros((2, LANES), I32)
    for r in range(ROWS):
        for d in range(3):
            here = (row == r // 4) & (lane == (r % 4) * 8 + d)
            digits = jnp.where(here, (ids_ref[r] >> (7 * d)) & 127, digits)
    digits = digits.astype(F32)
    for m in range(CHIPS):
        parts = []
        for q in range(4):
            for array in rows:
                two = jnp.concatenate(
                    [array[r : r + 1, m * PAIR : (m + 1) * PAIR] for r in (q, 4 + q)], axis=0
                )
                other = jnp.concatenate([two[:, COLS:], two[:, :COLS]], axis=1)
                parts.append(jnp.where(swap, other, two))
        block[m] = jnp.concatenate(parts + [digits], axis=1).astype(BF16)
    copies = [
        pltpu.make_async_copy(block, out_ref.at[:, s], out_sem.at[s]) for s in range(SHARDS)
    ]
    for copy in copies:
        copy.start()
    for copy in copies:
        copy.wait()


def turn_body(rows_ref, hidden_out, keep_out, send_out):
    for p in range(OWN):
        rows = rows_ref[p * 32 : (p + 1) * 32, :].astype(F32)
        tokens = jnp.concatenate([rows[:, q * CHUNK : (q + 1) * CHUNK] for q in range(4)], axis=0)
        hidden_out[p * SEQ : (p + 1) * SEQ, :] = tokens[:, 0:PAIR].astype(BF16)
        turned = tokens.T.astype(BF16)
        digits = rows[:, 4 * CHUNK :].T
        digits = jnp.concatenate([digits[q * 8 : q * 8 + 8] for q in range(4)], axis=1)
        digits = jnp.concatenate([digits, jnp.zeros((8, SEQ), F32)], axis=0).astype(BF16)
        for n, out in enumerate((keep_out, send_out)):
            out[p, 0:COLS, :] = turned[n * COLS : (n + 1) * COLS]
            out[p, COLS:PAIR, :] = turned[PAIR + n * COLS : PAIR + (n + 1) * COLS]
            out[p, PAIR:, :] = digits


def logits_body(place_ref, hidden_ref, index_ref, own_ref, other_ref, pooled_ref, out_ref):
    here = lax.broadcasted_iota(I32, (SEQ, 1), 0)
    inside = pl.program_id(0) * STEP + lax.broadcasted_iota(I32, (1, STEP), 1) < VOC
    embed = jnp.concatenate([own_ref[...], other_ref[...]], axis=0)
    picked = []
    for p in range(OWN):
        scores = jnp.dot(
            hidden_ref[p * SEQ : (p + 1) * SEQ, :], embed, preferred_element_type=F32
        )
        index = turned_spot(index_ref[slot(place_ref, p // 2), p % 2 : p % 2 + 1, :])
        picked.append(jnp.sum(jnp.where(index == here, scores, 0.0), axis=0, keepdims=True))
    picked = jnp.concatenate(picked + [pooled_ref[...], jnp.zeros((6, STEP), F32)], axis=0)
    picked = jnp.where(inside, picked, 0.0)
    for n in range(2):
        out_ref[n] = picked[:, n * CHUNK : (n + 1) * CHUNK]


def slope_body(part_ref, bias_ref, out_ref):
    logits = []
    upstream = []
    for c in range(2):
        total = part_ref[c, 0:OWN, :]
        for m in range(1, CHIPS):
            total = total + part_ref[2 * m + c, 0:OWN, :]
        logits.append(total)
        upstream += [part_ref[2 * m + c, OWN : OWN + 2, :] for m in range(CHIPS)]
    logits = jnp.concatenate(logits, axis=0) + bias_ref[...]
    upstream = jnp.concatenate(upstream, axis=0)
    softened = jnp.maximum(logits, 0.0) + jnp.log1p(jnp.exp(-jnp.abs(logits)))
    pooled = jnp.log1p(softened)
    sigmoid = 1.0 / (1.0 + jnp.exp(-logits))
    slope = sigmoid / (1.0 + softened)
    mean_pooled = jnp.sum(pooled, axis=0, keepdims=True) / PASSAGES
    grad = ((upstream + mean_pooled) * slope).astype(BF16)
    for g in range(GROUPS):
        out_ref[g] = grad


def hidden_body(place_ref, grad_ref, index_ref, own_ref, other_ref, out_ref, total, grads):
    step = pl.program_id(0)
    here = lax.broadcasted_iota(I32, (SEQ, LANES), 0).astype(I16)
    zero = jnp.zeros((), BF16)
    first_core = place_ref[1] == 0
    for n in range(2):
        both = grad_ref[n].astype(F32)
        grads[:, n * CHUNK : (n + 1) * CHUNK] = jnp.where(first_core, both[0:OWN], both[OWN:])

    def scatter(width, p):
        parts = []
        for tile in range(width // LANES):
            lanes = slice(tile * LANES, (tile + 1) * LANES)
            index = index_ref[slot(place_ref, p // 2), p % 2 : p % 2 + 1, lanes]
            index = jnp.broadcast_to(index, (16, LANES)).astype(I16)
            value = jnp.broadcast_to(grads[p : p + 1, lanes], (16, LANES)).astype(BF16)
            index = jnp.concatenate([index] * 8, axis=0)
            value = jnp.concatenate([value] * 8, axis=0)
            parts.append(jnp.where(index == here, value, zero))
        embed = jnp.concatenate([own_ref[:, 0:width], other_ref[:, 0:width]], axis=0)
        return lax.dot_general(
            jnp.concatenate(parts, axis=1),
            embed,
            (((1,), (1,)), ((), ())),
            preferred_element_type=F32,
        )

    def rows(p):
        return slice(p * SEQ, (p + 1) * SEQ)

    @pl.when(step == 0)
    def first():
        for p in range(OWN):
            total[rows(p), :] = scatter(STEP, p)

    @pl.when((step > 0) & (step < STEPS - 1))
    def middle():
        for p in range(OWN):
            total[rows(p), :] += scatter(STEP, p)

    @pl.when(step == STEPS - 1)
    def last():
        for p in range(OWN):
            out_ref[rows(p), :] = (total[rows(p), :] + scatter(VOC - (STEPS - 1) * STEP, p)).astype(BF16)


def embed_body(
    place_ref, grad_ref, own_index, other_index, keep_ref, got_ref, out_ref, bias_ref, left, right, total, grads
):
    base = place_ref[0] * VOC
    first_core = place_ref[1] == 0
    low_row = lax.broadcasted_iota(I32, (512, LANES), 0).astype(I16)
    zero = jnp.zeros((), BF16)
    one = jnp.ones((), BF16)
    total[...] = jnp.zeros_like(total)

    def token_block(table_ref, block):
        for s in range(8):
            p = block * 8 + s
            digits = table_ref[p, PAIR:, :].astype(F32).astype(I32)
            local = (digits[2:3] << 14) + (digits[1:2] << 7) + digits[0:1] - base
            inside = (local >= 0) & (local < VOC)
            high = jnp.where(inside, local >> 9, 15)
            high = jnp.broadcast_to(high, (16, LANES)).astype(I16)
            low = jnp.broadcast_to(local & 511, (16, LANES)).astype(I16)
            high = jnp.concatenate([high] * 4, axis=0)
            low = jnp.concatenate([low] * 32, axis=0)
            cotangents = table_ref[p, COLS:PAIR, :]
            lanes = slice(s * LANES, (s + 1) * LANES)
            for h in range(8):
                left[h * COLS : (h + 1) * COLS, lanes] = jnp.where(
                    high == jnp.int16(h), cotangents, zero
                )
            right[:, lanes] = jnp.where(low_row == low, one, zero)
        total[...] += lax.dot_general(
            left[...], right[...], (((1,), (1,)), ((), ())), preferred_element_type=F32
        )

    for table_ref in (keep_ref, got_ref):

        def one_block(block, carry, table_ref=table_ref):
            token_block(table_ref, block)
            return carry

        lax.fori_loop(0, 2, one_block, 0)
    for h in range(8):
        width = min(512, VOC - h * 512)
        out_ref[:, h * 512 : h * 512 + width] = total[h * COLS : (h + 1) * COLS, 0:width]
    for g in range(GROUPS):
        both = grad_ref[g].astype(F32)
        grads[g] = jnp.where(first_core, both, jnp.concatenate([both[OWN:], both[:OWN]], axis=0))

    def one_tile(tile, carry):
        lanes = pl.ds(pl.multiple_of(tile * LANES, LANES), LANES)
        half = pl.ds(pl.multiple_of((tile % 2) * LANES, LANES), LANES)
        totals = [out_ref[d : d + 16, lanes] for d in range(0, COLS, 16)]
        for n, (table_ref, index_ref) in enumerate(((keep_ref, own_index), (got_ref, other_index))):
            for p in range(OWN):
                index = turned_spot(index_ref[slot(place_ref, p // 2), p % 2 : p % 2 + 1, lanes])
                index = jnp.broadcast_to(index, (16, LANES)).astype(I16)
                value = grads[tile // 2, n * OWN + p : n * OWN + p + 1, half]
                for d in range(COLS // 16):
                    picked = lane_gather(table_ref[p, d * 16 : d * 16 + 16, :], index).astype(F32)
                    totals[d] = totals[d] + picked * value
        for d in range(COLS // 16):
            out_ref[d * 16 : d * 16 + 16, lanes] = totals[d]
        bias_ref[:, lanes] = jnp.sum(grads[tile // 2, :, half], axis=0, keepdims=True)
        return carry

    lax.fori_loop(0, TILES, one_tile, 0)


def sum_body(place_ref, part_ref, out_ref):
    swap = place_ref[1] == 1
    for m in range(CHIPS):
        total = part_ref[m * SHARDS].astype(F32)
        for s in range(1, SHARDS):
            total = total + part_ref[m * SHARDS + s].astype(F32)
        other = jnp.concatenate([total[:, COLS:], total[:, :COLS]], axis=1)
        out_ref[:, m * PAIR : (m + 1) * PAIR] = jnp.where(swap, other, total).astype(BF16)


def call(body, name, out, scratch=(), specs=None, us=1, grid=(), out_specs=None):
    extra = {key: value for key, value in (("grid", grid), ("out_specs", out_specs)) if value}
    return pl.pallas_call(
        body,
        out_shape=out,
        in_specs=specs,
        scratch_shapes=scratch,
        compiler_params=pltpu.CompilerParams(vmem_limit_bytes=ROOM * 1024 * 1024),
        cost_estimate=pl.CostEstimate(flops=0, bytes_accessed=3_700_000 * us, transcendentals=0),
        name=name,
        **extra,
    )


def shape(dims, dtype):
    return jax.ShapeDtypeStruct(dims, dtype)


def lanes_of(*dims):
    return pl.BlockSpec(dims + (STEP,), lambda i: (0,) * len(dims) + (i,))


def chunks_of(*dims):
    return pl.BlockSpec((2,) + dims, lambda i: (i,) + (0,) * len(dims))


def whole(*dims):
    return pl.BlockSpec(dims, lambda i: (0,) * len(dims))


def exchange(x, axis):
    return lax.all_to_all(x, axis, split_axis=0, concat_axis=0, tiled=True)


def swap_over(x, axis):
    return lax.ppermute(x, axis, [(0, 1), (1, 0)])


def on_device(
    hidden, embed_grad, token_ids, lengths, pool_index, embedding, head_bias, pooled_grad
):
    place = jnp.stack([lax.axis_index(name) for name in (SHARD, "core", "zl", "x")]).astype(I32)
    rows = call(
        pack_body,
        "pack",
        shape((CHIPS, SHARDS, 2, CARRY), BF16),
        [
            pltpu.SMEM((2,), I32),
            pltpu.SMEM((ROWS,), I32),
            pltpu.VMEM((ROWS, WIDTH), BF16),
            pltpu.VMEM((ROWS, WIDTH), BF16),
            pltpu.VMEM((CHIPS, 2, CARRY), BF16),
            pltpu.SemaphoreType.DMA((4,)),
            pltpu.SemaphoreType.DMA((SHARDS,)),
        ],
        [SMEM] + [ANY] * 4,
        out_specs=ANY,
    )(place, lengths, token_ids, hidden, embed_grad)
    all_rows = exchange(rows.reshape(CHIPS * SHARDS, 2, CARRY), HOME).reshape(-1, CARRY)
    other_embed = swap_over(embedding, "core")
    index = jnp.stack([pool_index, swap_over(pool_index, "zl")])
    shifts = [
        lax.ppermute(index, "x", [(k, (k + s) % 4) for k in range(4)]) for s in range(1, 4)
    ]
    own_index = jnp.stack([index] + shifts, axis=1).reshape(CHIPS, 2, VOC)
    other_index = swap_over(own_index, "core")
    hidden_rows, keep, send = call(
        turn_body,
        "turn",
        (
            shape((OWN * SEQ, PAIR), BF16),
            shape((OWN, PAIR + 16, SEQ), BF16),
            shape((OWN, PAIR + 16, SEQ), BF16),
        ),
        specs=[VMEM],
        us=2,
    )(all_rows)
    got = swap_over(send, "core")
    partial = call(
        logits_body,
        "logits",
        shape((GROUPS, 24, CHUNK), F32),
        specs=[
            SMEM,
            whole(OWN * SEQ, PAIR),
            lanes_of(CHIPS, 2),
            lanes_of(COLS),
            lanes_of(COLS),
            lanes_of(2),
        ],
        out_specs=chunks_of(24, CHUNK),
        grid=(STEPS,),
        us=6,
    )(place, hidden_rows, own_index, embedding, other_embed, pooled_grad)
    parts = exchange(partial, GROUP)
    bias = jnp.pad(head_bias, (0, GROUPS * CHUNK - VOC)).reshape(GROUPS, 1, CHUNK)
    bias = lax.dynamic_index_in_dim(bias, lax.axis_index(GROUP), 0, keepdims=False)
    grad_block = call(
        slope_body, "slope", shape((GROUPS, PASSAGES, CHUNK), BF16), specs=[VMEM, VMEM]
    )(parts, bias)
    all_grad = exchange(grad_block, GROUP)
    hidden_parts = call(
        hidden_body,
        "hidden_grad",
        shape((OWN * SEQ, PAIR), BF16),
        [pltpu.VMEM((OWN * SEQ, PAIR), F32), pltpu.VMEM((OWN, STEP), F32)],
        [SMEM, chunks_of(PASSAGES, CHUNK), lanes_of(CHIPS, 2), lanes_of(COLS), lanes_of(COLS)],
        out_specs=whole(OWN * SEQ, PAIR),
        grid=(STEPS,),
        us=7,
    )(place, all_grad, own_index, embedding, other_embed)
    hidden_got = exchange(hidden_parts.reshape(CHIPS * SHARDS, ROWS, PAIR), HOME)
    embedding_grad, bias_grad = call(
        embed_body,
        "embedding_grad",
        (shape((COLS, VOC), F32), shape((1, VOC), F32)),
        [
            pltpu.VMEM((512, 1024), BF16),
            pltpu.VMEM((512, 1024), BF16),
            pltpu.VMEM((512, 512), F32),
            pltpu.VMEM((GROUPS, PASSAGES, CHUNK), F32),
        ],
        [SMEM] + [VMEM] * 5,
        us=16,
    )(place, all_grad, own_index, other_index, keep, got)
    hidden_grad = call(
        sum_body, "sum_shards", shape((ROWS, WIDTH), BF16), specs=[SMEM, VMEM]
    )(place, hidden_got)
    return hidden_grad, embedding_grad, bias_grad.reshape(VOC)


def solution(mesh):
    fine = Mesh(mesh.devices.reshape(2, 4, 2, 4, 8), GROUP + SHARD)
    every = P(GROUP + SHARD, None)
    split = P(GROUP, SHARD)
    return jax.shard_map(
        on_device,
        mesh=fine,
        in_specs=(every, every, P(GROUP + SHARD), P(GROUP), split, split, P(SHARD), split),
        out_specs=(every, split, P(SHARD)),
        check_vma=False,
    )
```

```python
import jax
import jax.numpy as jnp
from jax import lax
from jax.experimental import pallas as pl
from jax.experimental.pallas import tpu as pltpu
from jax.sharding import Mesh, PartitionSpec as P

F32 = jnp.float32
BF16 = jnp.bfloat16
I16 = jnp.int16
I32 = jnp.int32
LANES = 128
SMEM = pl.BlockSpec(memory_space=pltpu.SMEM)
VMEM = pl.BlockSpec(memory_space=pltpu.VMEM)
ANY = pl.BlockSpec(memory_space=pl.ANY)

GROUP = ("zl", "x", "core")
SHARD = ("zh", "y")
HOME = ("zl", "x", "zh", "y")
GROUPS = 16
SHARDS = 32
CHIPS = 8
SEQ = 128
PASSAGES = 32
OWN = 16
COLS = 64
PAIR = 128
WIDTH = 8 * PAIR
ROWS = 8
TILES = 31
VOC = TILES * LANES
CHUNK = 256
STEP = 512
STEPS = 8
CARRY = 4 * 2 * PAIR + LANES


def lane_gather(table, index):
    numbers = lax.GatherDimensionNumbers(
        offset_dims=(),
        collapsed_slice_dims=(1,),
        start_index_map=(1,),
        operand_batching_dims=(0,),
        start_indices_batching_dims=(0,),
    )
    return lax.gather(
        table,
        index[..., None],
        numbers,
        (1, 1),
        mode=lax.GatherScatterMode.PROMISE_IN_BOUNDS,
    )


def slot(place_ref, m):
    return ((m // 4) ^ place_ref[2]) * 4 + ((place_ref[3] - m % 4) & 3)


def turned_spot(index):
    return ((index & 3) << 5) | (index >> 2)


def pack_body(place_ref, lengths, ids, hidden, grad, out_ref, *scratch):
    held, block, sem, out_sem = scratch[:4], scratch[4], scratch[5], scratch[6]
    copies = [
        pltpu.make_async_copy(source, target, sem.at[n])
        for n, (source, target) in enumerate(zip((lengths, ids, hidden, grad), held))
    ]
    for copy in copies:
        copy.start()
    for copy in copies:
        copy.wait()
    lengths_ref, ids_ref, hidden_ref, grad_ref = held
    place = place_ref[0]
    swap = place_ref[1] == 1
    limit = lengths_ref[place // (SEQ // ROWS)]
    spot = (place % (SEQ // ROWS)) * ROWS + lax.broadcasted_iota(I32, (ROWS, 1), 0)
    rows = [hidden_ref[...].astype(F32), jnp.where(spot < limit, grad_ref[...].astype(F32), 0.0)]
    row = lax.broadcasted_iota(I32, (2, LANES), 0)
    lane = lax.broadcasted_iota(I32, (2, LANES), 1)
    digits = jnp.zeros((2, LANES), I32)
    for r in range(ROWS):
        for d in range(3):
            here = (row == r // 4) & (lane == (r % 4) * 8 + d)
            digits = jnp.where(here, (ids_ref[r] >> (7 * d)) & 127, digits)
    digits = digits.astype(F32)
    for m in range(CHIPS):
        parts = []
        for q in range(4):
            for array in rows:
                two = jnp.concatenate(
                    [array[r : r + 1, m * PAIR : (m + 1) * PAIR] for r in (q, 4 + q)], axis=0
                )
                other = jnp.concatenate([two[:, COLS:], two[:, :COLS]], axis=1)
                parts.append(jnp.where(swap, other, two))
        block[m] = jnp.concatenate(parts + [digits], axis=1).astype(BF16)
    copies = [
        pltpu.make_async_copy(block, out_ref.at[:, s], out_sem.at[s]) for s in range(SHARDS)
    ]
    for copy in copies:
        copy.start()
    for copy in copies:
        copy.wait()


def turn_body(rows_ref, keep_out, send_out):
    for p in range(OWN):
        rows = rows_ref[p * 32 : (p + 1) * 32, :].astype(F32)
        tokens = jnp.concatenate([rows[:, q * CHUNK : (q + 1) * CHUNK] for q in range(4)], axis=0)
        turned = tokens.T.astype(BF16)
        digits = rows[:, 4 * CHUNK :].T
        digits = jnp.concatenate([digits[q * 8 : q * 8 + 8] for q in range(4)], axis=1)
        digits = jnp.concatenate([digits, jnp.zeros((8, SEQ), F32)], axis=0).astype(BF16)
        for n, out in enumerate((keep_out, send_out)):
            out[p, 0:COLS, :] = turned[n * COLS : (n + 1) * COLS]
            out[p, COLS:PAIR, :] = turned[PAIR + n * COLS : PAIR + (n + 1) * COLS]
            out[p, PAIR:, :] = digits


def logits_body(place_ref, rows_ref, index_ref, own_ref, other_ref, pooled_ref, out_ref, hidden_ref):
    @pl.when(pl.program_id(0) == 0)
    def unfold():
        for p in range(OWN):
            for q in range(4):
                at = p * SEQ + q * 32
                hidden_ref[at : at + 32, :] = rows_ref[p * 32 : p * 32 + 32, q * CHUNK : q * CHUNK + PAIR]

    here = lax.broadcasted_iota(I32, (SEQ, 1), 0)
    inside = pl.program_id(0) * STEP + lax.broadcasted_iota(I32, (1, STEP), 1) < VOC
    embed = jnp.concatenate([own_ref[...], other_ref[...]], axis=0)
    picked = []
    for p in range(OWN):
        scores = jnp.dot(
            hidden_ref[p * SEQ : (p + 1) * SEQ, :], embed, preferred_element_type=F32
        )
        index = turned_spot(index_ref[slot(place_ref, p // 2), p % 2 : p % 2 + 1, :])
        picked.append(jnp.sum(jnp.where(index == here, scores, 0.0), axis=0, keepdims=True))
    picked = jnp.concatenate(picked + [pooled_ref[...], jnp.zeros((6, STEP), F32)], axis=0)
    picked = jnp.where(inside, picked, 0.0)
    for n in range(2):
        out_ref[n] = picked[:, n * CHUNK : (n + 1) * CHUNK]


def slope_body(part_ref, bias_ref, out_ref):
    logits = []
    upstream = []
    for c in range(2):
        total = part_ref[c, 0:OWN, :]
        for m in range(1, CHIPS):
            total = total + part_ref[2 * m + c, 0:OWN, :]
        logits.append(total)
        upstream += [part_ref[2 * m + c, OWN : OWN + 2, :] for m in range(CHIPS)]
    logits = jnp.concatenate(logits, axis=0) + bias_ref[...]
    upstream = jnp.concatenate(upstream, axis=0)
    softened = jnp.maximum(logits, 0.0) + jnp.log1p(jnp.exp(-jnp.abs(logits)))
    pooled = jnp.log1p(softened)
    sigmoid = 1.0 / (1.0 + jnp.exp(-logits))
    slope = sigmoid / (1.0 + softened)
    mean_pooled = jnp.sum(pooled, axis=0, keepdims=True) / PASSAGES
    grad = ((upstream + mean_pooled) * slope).astype(BF16)
    for g in range(GROUPS):
        out_ref[g] = grad


def hidden_body(place_ref, grad_ref, index_ref, own_ref, other_ref, out_ref, total, grads):
    step = pl.program_id(0)
    here = lax.broadcasted_iota(I32, (SEQ, LANES), 0).astype(I16)
    zero = jnp.zeros((), BF16)
    first_core = place_ref[1] == 0
    for n in range(2):
        both = grad_ref[n].astype(F32)
        grads[:, n * CHUNK : (n + 1) * CHUNK] = jnp.where(first_core, both[0:OWN], both[OWN:])

    def scatter(width, p):
        parts = []
        for tile in range(width // LANES):
            lanes = slice(tile * LANES, (tile + 1) * LANES)
            index = index_ref[slot(place_ref, p // 2), p % 2 : p % 2 + 1, lanes]
            index = jnp.broadcast_to(index, (16, LANES)).astype(I16)
            value = jnp.broadcast_to(grads[p : p + 1, lanes], (16, LANES)).astype(BF16)
            index = jnp.concatenate([index] * 8, axis=0)
            value = jnp.concatenate([value] * 8, axis=0)
            parts.append(jnp.where(index == here, value, zero))
        embed = jnp.concatenate([own_ref[:, 0:width], other_ref[:, 0:width]], axis=0)
        return lax.dot_general(
            jnp.concatenate(parts, axis=1),
            embed,
            (((1,), (1,)), ((), ())),
            preferred_element_type=F32,
        )

    def rows(p):
        return slice(p * SEQ, (p + 1) * SEQ)

    @pl.when(step == 0)
    def first():
        for p in range(OWN):
            total[rows(p), :] = scatter(STEP, p)

    @pl.when((step > 0) & (step < STEPS - 1))
    def middle():
        for p in range(OWN):
            total[rows(p), :] += scatter(STEP, p)

    @pl.when(step == STEPS - 1)
    def last():
        for p in range(OWN):
            out_ref[rows(p), :] = (total[rows(p), :] + scatter(VOC - (STEPS - 1) * STEP, p)).astype(BF16)


def token_body(place_ref, keep_ref, got_ref, out_ref, left, right, total):
    base = place_ref[0] * VOC
    low_row = lax.broadcasted_iota(I32, (512, LANES), 0).astype(I16)
    zero = jnp.zeros((), BF16)
    one = jnp.ones((), BF16)
    total[...] = jnp.zeros_like(total)

    def token_block(table_ref, block):
        for s in range(8):
            p = block * 8 + s
            digits = table_ref[p, PAIR:, :].astype(F32).astype(I32)
            local = (digits[2:3] << 14) + (digits[1:2] << 7) + digits[0:1] - base
            inside = (local >= 0) & (local < VOC)
            high = jnp.where(inside, local >> 9, 15)
            high = jnp.broadcast_to(high, (16, LANES)).astype(I16)
            low = jnp.broadcast_to(local & 511, (16, LANES)).astype(I16)
            high = jnp.concatenate([high] * 4, axis=0)
            low = jnp.concatenate([low] * 32, axis=0)
            cotangents = table_ref[p, COLS:PAIR, :]
            lanes = slice(s * LANES, (s + 1) * LANES)
            for h in range(8):
                left[h * COLS : (h + 1) * COLS, lanes] = jnp.where(
                    high == jnp.int16(h), cotangents, zero
                )
            right[:, lanes] = jnp.where(low_row == low, one, zero)
        total[...] += lax.dot_general(
            left[...], right[...], (((1,), (1,)), ((), ())), preferred_element_type=F32
        )

    for table_ref in (keep_ref, got_ref):

        def one_block(block, carry, table_ref=table_ref):
            token_block(table_ref, block)
            return carry

        lax.fori_loop(0, 2, one_block, 0)
    for h in range(8):
        out_ref[:, h * 512 : (h + 1) * 512] = total[h * COLS : (h + 1) * COLS, :]


def embed_body(
    place_ref, token_ref, grad_ref, own_index, other_index, keep_ref, got_ref, out_ref, bias_ref, grads
):
    first_core = place_ref[1] == 0
    for g in range(GROUPS):
        both = grad_ref[g].astype(F32)
        grads[g] = jnp.where(first_core, both, jnp.concatenate([both[OWN:], both[:OWN]], axis=0))

    def one_tile(tile, carry):
        lanes = pl.ds(pl.multiple_of(tile * LANES, LANES), LANES)
        half = pl.ds(pl.multiple_of((tile % 2) * LANES, LANES), LANES)
        totals = [token_ref[d : d + 16, lanes] for d in range(0, COLS, 16)]
        for n, (table_ref, index_ref) in enumerate(((keep_ref, own_index), (got_ref, other_index))):
            for p in range(OWN):
                index = turned_spot(index_ref[slot(place_ref, p // 2), p % 2 : p % 2 + 1, lanes])
                index = jnp.broadcast_to(index, (16, LANES)).astype(I16)
                value = grads[tile // 2, n * OWN + p : n * OWN + p + 1, half]
                for d in range(COLS // 16):
                    picked = lane_gather(table_ref[p, d * 16 : d * 16 + 16, :], index).astype(F32)
                    totals[d] = totals[d] + picked * value
        for d in range(COLS // 16):
            out_ref[d * 16 : d * 16 + 16, lanes] = totals[d]
        bias_ref[:, lanes] = jnp.sum(grads[tile // 2, :, half], axis=0, keepdims=True)
        return carry

    lax.fori_loop(0, TILES, one_tile, 0)


def sum_body(place_ref, part_ref, out_ref):
    swap = place_ref[1] == 1
    for m in range(CHIPS):
        total = part_ref[m * SHARDS].astype(F32)
        for s in range(1, SHARDS):
            total = total + part_ref[m * SHARDS + s].astype(F32)
        other = jnp.concatenate([total[:, COLS:], total[:, :COLS]], axis=1)
        out_ref[:, m * PAIR : (m + 1) * PAIR] = jnp.where(swap, other, total).astype(BF16)


def call(body, name, out, scratch=(), specs=None, us=1, grid=(), out_specs=None, room=56):
    extra = {key: value for key, value in (("grid", grid), ("out_specs", out_specs)) if value}
    return pl.pallas_call(
        body,
        out_shape=out,
        in_specs=specs,
        scratch_shapes=scratch,
        compiler_params=pltpu.CompilerParams(vmem_limit_bytes=room * 1024 * 1024),
        cost_estimate=pl.CostEstimate(flops=0, bytes_accessed=3_700_000 * us, transcendentals=0),
        name=name,
        **extra,
    )


def shape(dims, dtype):
    return jax.ShapeDtypeStruct(dims, dtype)


def lanes_of(*dims):
    return pl.BlockSpec(dims + (STEP,), lambda i: (0,) * len(dims) + (i,))


def chunks_of(*dims):
    return pl.BlockSpec((2,) + dims, lambda i: (i,) + (0,) * len(dims))


def whole(*dims):
    return pl.BlockSpec(dims, lambda i: (0,) * len(dims))


def exchange(x, axis):
    return lax.all_to_all(x, axis, split_axis=0, concat_axis=0, tiled=True)


def swap_over(x, axis):
    return lax.ppermute(x, axis, [(0, 1), (1, 0)])


def on_device(
    hidden, embed_grad, token_ids, lengths, pool_index, embedding, head_bias, pooled_grad
):
    place = jnp.stack([lax.axis_index(name) for name in (SHARD, "core", "zl", "x")]).astype(I32)
    rows = call(
        pack_body,
        "pack",
        shape((CHIPS, SHARDS, 2, CARRY), BF16),
        [
            pltpu.SMEM((2,), I32),
            pltpu.SMEM((ROWS,), I32),
            pltpu.VMEM((ROWS, WIDTH), BF16),
            pltpu.VMEM((ROWS, WIDTH), BF16),
            pltpu.VMEM((CHIPS, 2, CARRY), BF16),
            pltpu.SemaphoreType.DMA((4,)),
            pltpu.SemaphoreType.DMA((SHARDS,)),
        ],
        [SMEM] + [ANY] * 4,
        out_specs=ANY,
    )(place, lengths, token_ids, hidden, embed_grad)
    all_rows = exchange(rows.reshape(CHIPS * SHARDS, 2, CARRY), HOME).reshape(-1, CARRY)
    other_embed = swap_over(embedding, "core")
    index = [pool_index]
    for slot_at in range(1, CHIPS):
        pairs = [(m, ((m // 4) ^ (slot_at // 4)) * 4 + (m + slot_at) % 4) for m in range(CHIPS)]
        index.append(lax.ppermute(pool_index, ("zl", "x"), pairs))
    own_index = jnp.stack(index)
    partial = call(
        logits_body,
        "logits",
        shape((GROUPS, 24, CHUNK), F32),
        [pltpu.VMEM((OWN * SEQ, PAIR), BF16)],
        specs=[
            SMEM,
            whole(OWN * SEQ // 4, CARRY),
            lanes_of(CHIPS, 2),
            lanes_of(COLS),
            lanes_of(COLS),
            lanes_of(2),
        ],
        out_specs=chunks_of(24, CHUNK),
        grid=(STEPS,),
        us=7,
    )(place, all_rows, own_index, embedding, other_embed, pooled_grad)
    keep, send = call(
        turn_body,
        "turn",
        (shape((OWN, PAIR + 16, SEQ), BF16), shape((OWN, PAIR + 16, SEQ), BF16)),
        specs=[VMEM],
        us=3,
    )(all_rows)
    got = swap_over(send, "core")
    other_index = swap_over(own_index, "core")
    parts = exchange(partial, GROUP)
    bias = jnp.pad(head_bias, (0, GROUPS * CHUNK - VOC)).reshape(GROUPS, 1, CHUNK)
    bias = lax.dynamic_index_in_dim(bias, lax.axis_index(GROUP), 0, keepdims=False)
    grad_block = call(
        slope_body, "slope", shape((GROUPS, PASSAGES, CHUNK), BF16), specs=[VMEM, VMEM], room=8
    )(parts, bias)
    all_grad = exchange(grad_block, GROUP)
    token_grad = call(
        token_body,
        "token_grad",
        shape((COLS, 4096), F32),
        [
            pltpu.VMEM((512, 1024), BF16),
            pltpu.VMEM((512, 1024), BF16),
            pltpu.VMEM((512, 512), F32),
        ],
        [SMEM, VMEM, VMEM],
        us=5,
        room=24,
    )(place, keep, got)
    all_grad, token_grad, other_index = lax.optimization_barrier((all_grad, token_grad, other_index))
    hidden_parts = call(
        hidden_body,
        "hidden_grad",
        shape((OWN * SEQ, PAIR), BF16),
        [pltpu.VMEM((OWN * SEQ, PAIR), F32), pltpu.VMEM((OWN, STEP), F32)],
        [SMEM, chunks_of(PASSAGES, CHUNK), lanes_of(CHIPS, 2), lanes_of(COLS), lanes_of(COLS)],
        out_specs=whole(OWN * SEQ, PAIR),
        grid=(STEPS,),
        us=7,
    )(place, all_grad, own_index, embedding, other_embed)
    hidden_got = exchange(hidden_parts.reshape(CHIPS * SHARDS, ROWS, PAIR), HOME)
    embedding_grad, bias_grad = call(
        embed_body,
        "embedding_grad",
        (shape((COLS, VOC), F32), shape((1, VOC), F32)),
        [pltpu.VMEM((GROUPS, PASSAGES, CHUNK), F32)],
        [SMEM] + [VMEM] * 6,
        us=11,
        room=24,
    )(place, token_grad, all_grad, own_index, other_index, keep, got)
    hidden_grad = call(
        sum_body, "sum_shards", shape((ROWS, WIDTH), BF16), specs=[SMEM, VMEM], room=8
    )(place, hidden_got)
    return hidden_grad, embedding_grad, bias_grad.reshape(VOC)


def solution(mesh):
    fine = Mesh(mesh.devices.reshape(2, 4, 2, 4, 8), GROUP + SHARD)
    every = P(GROUP + SHARD, None)
    split = P(GROUP, SHARD)
    return jax.shard_map(
        on_device,
        mesh=fine,
        in_specs=(every, every, P(GROUP + SHARD), P(GROUP), split, split, P(SHARD), split),
        out_specs=(every, split, P(SHARD)),
        check_vma=False,
    )
```

```python
import jax
import jax.numpy as jnp
from jax import lax
from jax.experimental import pallas as pl
from jax.experimental.pallas import tpu as pltpu
from jax.sharding import Mesh, PartitionSpec as P

F32 = jnp.float32
BF16 = jnp.bfloat16
I16 = jnp.int16
I32 = jnp.int32
LANES = 128
SMEM = pl.BlockSpec(memory_space=pltpu.SMEM)
VMEM = pl.BlockSpec(memory_space=pltpu.VMEM)
ANY = pl.BlockSpec(memory_space=pl.ANY)

GROUP = ("zl", "x", "core")
SHARD = ("zh", "y")
HOME = ("zl", "x", "zh", "y")
GROUPS = 16
SHARDS = 32
CHIPS = 8
SEQ = 128
PASSAGES = 32
OWN = 16
COLS = 64
PAIR = 128
WIDTH = 8 * PAIR
ROWS = 8
TILES = 31
VOC = TILES * LANES
CHUNK = 256
CARRY = 4 * 2 * PAIR + LANES


def lane_gather(table, index):
    numbers = lax.GatherDimensionNumbers(
        offset_dims=(),
        collapsed_slice_dims=(1,),
        start_index_map=(1,),
        operand_batching_dims=(0,),
        start_indices_batching_dims=(0,),
    )
    return lax.gather(
        table,
        index[..., None],
        numbers,
        (1, 1),
        mode=lax.GatherScatterMode.PROMISE_IN_BOUNDS,
    )


def turned_spot(index):
    return ((index & 3) << 5) | (index >> 2)


def pack_body(place_ref, lengths, ids, hidden, grad, out_ref, *scratch):
    held, block, sem, out_sem = scratch[:4], scratch[4], scratch[5], scratch[6]
    copies = [
        pltpu.make_async_copy(source, target, sem.at[n])
        for n, (source, target) in enumerate(zip((lengths, ids, hidden, grad), held))
    ]
    for copy in copies:
        copy.start()
    for copy in copies:
        copy.wait()
    lengths_ref, ids_ref, hidden_ref, grad_ref = held
    place = place_ref[0]
    swap = place_ref[1] == 1
    limit = lengths_ref[place // (SEQ // ROWS)]
    spot = (place % (SEQ // ROWS)) * ROWS + lax.broadcasted_iota(I32, (ROWS, 1), 0)
    rows = [hidden_ref[...].astype(F32), jnp.where(spot < limit, grad_ref[...].astype(F32), 0.0)]
    row = lax.broadcasted_iota(I32, (2, LANES), 0)
    lane = lax.broadcasted_iota(I32, (2, LANES), 1)
    digits = jnp.zeros((2, LANES), I32)
    for r in range(ROWS):
        for d in range(3):
            here = (row == r // 4) & (lane == (r % 4) * 8 + d)
            digits = jnp.where(here, (ids_ref[r] >> (7 * d)) & 127, digits)
    digits = digits.astype(F32)
    for m in range(CHIPS):
        parts = []
        for q in range(4):
            for array in rows:
                two = jnp.concatenate(
                    [array[r : r + 1, m * PAIR : (m + 1) * PAIR] for r in (q, 4 + q)], axis=0
                )
                other = jnp.concatenate([two[:, COLS:], two[:, :COLS]], axis=1)
                parts.append(jnp.where(swap, other, two))
        block[m] = jnp.concatenate(parts + [digits], axis=1).astype(BF16)
    copies = [
        pltpu.make_async_copy(block, out_ref.at[:, s], out_sem.at[s]) for s in range(SHARDS)
    ]
    for copy in copies:
        copy.start()
    for copy in copies:
        copy.wait()


def turn_body(rows_ref, keep_out, send_out):
    for p in range(OWN):
        rows = rows_ref[p * 32 : (p + 1) * 32, :].astype(F32)
        tokens = jnp.concatenate([rows[:, q * CHUNK : (q + 1) * CHUNK] for q in range(4)], axis=0)
        turned = tokens.T.astype(BF16)
        digits = rows[:, 4 * CHUNK :].T
        digits = jnp.concatenate([digits[q * 8 : q * 8 + 8] for q in range(4)], axis=1)
        digits = jnp.concatenate([digits, jnp.zeros((8, SEQ), F32)], axis=0).astype(BF16)
        for n, out in enumerate((keep_out, send_out)):
            out[p, 0:COLS, :] = turned[n * COLS : (n + 1) * COLS]
            out[p, COLS:PAIR, :] = turned[PAIR + n * COLS : PAIR + (n + 1) * COLS]
            out[p, PAIR:, :] = digits


def over_terms(step, one_chunk):
    full = VOC // step

    def loop(i, carry):
        one_chunk(pl.multiple_of(i * step, step), step)
        return carry

    lax.fori_loop(0, full, loop, 0)
    one_chunk(full * step, VOC - full * step)


def logits_body(rows_ref, index_ref, own_ref, other_ref, pooled_ref, out_ref, hidden_ref, embed_ref):
    here = lax.broadcasted_iota(I32, (SEQ, 1), 0)
    embed_ref[0:COLS, :] = own_ref[...]
    embed_ref[COLS:, :] = other_ref[...]
    for p in range(OWN):
        for q in range(4):
            at = p * SEQ + q * 32
            hidden_ref[at : at + 32, :] = rows_ref[p * 32 : p * 32 + 32, q * CHUNK : q * CHUNK + PAIR]

    def one_chunk(first, width):
        lanes = pl.ds(first, width)
        embed = embed_ref[:, lanes]
        for p in range(OWN):
            scores = jnp.dot(
                hidden_ref[p * SEQ : (p + 1) * SEQ, :], embed, preferred_element_type=F32
            )
            index = turned_spot(index_ref[p // 2, p % 2 : p % 2 + 1, lanes])
            picked = jnp.sum(jnp.where(index == here, scores, 0.0), axis=0, keepdims=True)
            for at in range(0, width, CHUNK):
                some = min(CHUNK, width - at)
                out_ref[first // CHUNK + at // CHUNK, p : p + 1, 0:some] = picked[:, at : at + some]
        for at in range(0, width, CHUNK):
            some = min(CHUNK, width - at)
            upstream = pooled_ref[:, pl.ds(first + at, some)]
            out_ref[first // CHUNK + at // CHUNK, OWN : OWN + 2, 0:some] = upstream

    over_terms(1024, one_chunk)
    out_ref[:, OWN + 2 :, :] = jnp.zeros((GROUPS, 6, CHUNK), F32)
    out_ref[GROUPS - 1, :, LANES:] = jnp.zeros((24, CHUNK - LANES), F32)


def slope_body(part_ref, bias_ref, out_ref):
    logits = []
    upstream = []
    for c in range(2):
        total = part_ref[c, 0:OWN, :]
        for m in range(1, CHIPS):
            total = total + part_ref[2 * m + c, 0:OWN, :]
        logits.append(total)
        upstream += [part_ref[2 * m + c, OWN : OWN + 2, :] for m in range(CHIPS)]
    logits = jnp.concatenate(logits, axis=0) + bias_ref[...]
    upstream = jnp.concatenate(upstream, axis=0)
    softened = jnp.maximum(logits, 0.0) + jnp.log1p(jnp.exp(-jnp.abs(logits)))
    pooled = jnp.log1p(softened)
    sigmoid = 1.0 / (1.0 + jnp.exp(-logits))
    slope = sigmoid / (1.0 + softened)
    mean_pooled = jnp.sum(pooled, axis=0, keepdims=True) / PASSAGES
    grad = ((upstream + mean_pooled) * slope).astype(BF16)
    for g in range(GROUPS):
        out_ref[g] = grad


def hidden_body(
    place_ref, grad_ref, index_ref, own_ref, other_ref, out_ref, total, left, embed_ref, grads
):
    here = lax.broadcasted_iota(I32, (SEQ, LANES), 0).astype(I16)
    zero = jnp.zeros((), BF16)
    first_core = place_ref[1] == 0
    embed_ref[0:COLS, :] = own_ref[...]
    embed_ref[COLS:, :] = other_ref[...]
    total[...] = jnp.zeros_like(total)

    def one_chunk(first, width):
        for at in range(0, width, CHUNK):
            both = grad_ref[first // CHUNK + at // CHUNK].astype(F32)
            grads[:, at : at + CHUNK] = jnp.where(first_core, both[0:OWN], both[OWN:])
        embed = embed_ref[:, pl.ds(first, width)]
        for group in range(0, OWN, 4):
            for p in range(group, group + 4):
                for tile in range(width // LANES):
                    lanes = slice(tile * LANES, (tile + 1) * LANES)
                    index = index_ref[p // 2, p % 2 : p % 2 + 1, pl.ds(first + tile * LANES, LANES)]
                    index = jnp.broadcast_to(index, (16, LANES)).astype(I16)
                    value = jnp.broadcast_to(grads[p : p + 1, lanes], (16, LANES)).astype(BF16)
                    index = jnp.concatenate([index] * 8, axis=0)
                    value = jnp.concatenate([value] * 8, axis=0)
                    left[p * SEQ : (p + 1) * SEQ, lanes] = jnp.where(index == here, value, zero)
            rows = slice(group * SEQ, (group + 4) * SEQ)
            total[rows, :] += lax.dot_general(
                left[rows, 0:width], embed, (((1,), (1,)), ((), ())), preferred_element_type=F32
            )

    over_terms(1024, one_chunk)
    out_ref[...] = total[...].astype(BF16)


def token_body(place_ref, keep_ref, got_ref, out_ref, left, right, total):
    base = place_ref[0] * VOC
    low_row = lax.broadcasted_iota(I32, (512, LANES), 0).astype(I16)
    zero = jnp.zeros((), BF16)
    one = jnp.ones((), BF16)
    total[...] = jnp.zeros_like(total)

    def token_block(table_ref, block):
        for s in range(8):
            p = block * 8 + s
            digits = table_ref[p, PAIR:, :].astype(F32).astype(I32)
            local = (digits[2:3] << 14) + (digits[1:2] << 7) + digits[0:1] - base
            inside = (local >= 0) & (local < VOC)
            high = jnp.where(inside, local >> 9, 15)
            high = jnp.broadcast_to(high, (16, LANES)).astype(I16)
            low = jnp.broadcast_to(local & 511, (16, LANES)).astype(I16)
            high = jnp.concatenate([high] * 4, axis=0)
            low = jnp.concatenate([low] * 32, axis=0)
            cotangents = table_ref[p, COLS:PAIR, :]
            lanes = slice(s * LANES, (s + 1) * LANES)
            for h in range(8):
                left[h * COLS : (h + 1) * COLS, lanes] = jnp.where(
                    high == jnp.int16(h), cotangents, zero
                )
            right[:, lanes] = jnp.where(low_row == low, one, zero)
        total[...] += lax.dot_general(
            left[...], right[...], (((1,), (1,)), ((), ())), preferred_element_type=F32
        )

    for table_ref in (keep_ref, got_ref):

        def one_block(block, carry, table_ref=table_ref):
            token_block(table_ref, block)
            return carry

        lax.fori_loop(0, 2, one_block, 0)
    for h in range(8):
        out_ref[:, h * 512 : (h + 1) * 512] = total[h * COLS : (h + 1) * COLS, :]


def embed_body(
    place_ref, token_ref, grad_ref, own_index, other_index, keep_ref, got_ref, out_ref, bias_ref, grads
):
    first_core = place_ref[1] == 0
    for g in range(GROUPS):
        both = grad_ref[g].astype(F32)
        grads[g] = jnp.where(first_core, both, jnp.concatenate([both[OWN:], both[:OWN]], axis=0))

    def one_tile(tile, carry):
        lanes = pl.ds(pl.multiple_of(tile * LANES, LANES), LANES)
        half = pl.ds(pl.multiple_of((tile % 2) * LANES, LANES), LANES)
        totals = [token_ref[d : d + 16, lanes] for d in range(0, COLS, 16)]
        for n, (table_ref, index_ref) in enumerate(((keep_ref, own_index), (got_ref, other_index))):
            for p in range(OWN):
                index = turned_spot(index_ref[p // 2, p % 2 : p % 2 + 1, lanes])
                index = jnp.broadcast_to(index, (16, LANES)).astype(I16)
                value = grads[tile // 2, n * OWN + p : n * OWN + p + 1, half]
                for d in range(COLS // 16):
                    picked = lane_gather(table_ref[p, d * 16 : d * 16 + 16, :], index).astype(F32)
                    totals[d] = totals[d] + picked * value
        for d in range(COLS // 16):
            out_ref[d * 16 : d * 16 + 16, lanes] = totals[d]
        bias_ref[:, lanes] = jnp.sum(grads[tile // 2, :, half], axis=0, keepdims=True)
        return carry

    lax.fori_loop(0, TILES, one_tile, 0)


def sum_body(place_ref, part_ref, out_ref):
    swap = place_ref[1] == 1
    for m in range(CHIPS):
        total = part_ref[m * SHARDS].astype(F32)
        for s in range(1, SHARDS):
            total = total + part_ref[m * SHARDS + s].astype(F32)
        other = jnp.concatenate([total[:, COLS:], total[:, :COLS]], axis=1)
        out_ref[:, m * PAIR : (m + 1) * PAIR] = jnp.where(swap, other, total).astype(BF16)


def call(body, name, out, scratch=(), specs=None, us=1, out_specs=None, room=56):
    extra = {} if out_specs is None else {"out_specs": out_specs}
    return pl.pallas_call(
        body,
        out_shape=out,
        in_specs=specs,
        scratch_shapes=scratch,
        compiler_params=pltpu.CompilerParams(vmem_limit_bytes=room * 1024 * 1024),
        cost_estimate=pl.CostEstimate(flops=0, bytes_accessed=3_700_000 * us, transcendentals=0),
        name=name,
        **extra,
    )


def shape(dims, dtype):
    return jax.ShapeDtypeStruct(dims, dtype)


def exchange(x, axis):
    return lax.all_to_all(x, axis, split_axis=0, concat_axis=0, tiled=True)


def swap_over(x, axis):
    return lax.ppermute(x, axis, [(0, 1), (1, 0)])


def on_device(
    hidden, embed_grad, token_ids, lengths, pool_index, embedding, head_bias, pooled_grad
):
    place = jnp.stack([lax.axis_index(name) for name in (SHARD, "core", "zl", "x")]).astype(I32)
    own_index = exchange(jnp.broadcast_to(pool_index, (CHIPS, 2, VOC)), ("zl", "x"))
    rows = call(
        pack_body,
        "pack",
        shape((CHIPS, SHARDS, 2, CARRY), BF16),
        [
            pltpu.SMEM((2,), I32),
            pltpu.SMEM((ROWS,), I32),
            pltpu.VMEM((ROWS, WIDTH), BF16),
            pltpu.VMEM((ROWS, WIDTH), BF16),
            pltpu.VMEM((CHIPS, 2, CARRY), BF16),
            pltpu.SemaphoreType.DMA((4,)),
            pltpu.SemaphoreType.DMA((SHARDS,)),
        ],
        [SMEM] + [ANY] * 4,
        out_specs=ANY,
        us=4,
    )(place, lengths, token_ids, hidden, embed_grad)
    rows, own_index = lax.optimization_barrier((rows, own_index))
    all_rows = exchange(rows.reshape(CHIPS * SHARDS, 2, CARRY), HOME).reshape(-1, CARRY)
    other_embed = swap_over(embedding, "core")
    partial = call(
        logits_body,
        "logits",
        shape((GROUPS, 24, CHUNK), F32),
        [pltpu.VMEM((OWN * SEQ, PAIR), BF16), pltpu.VMEM((PAIR, VOC), BF16)],
        [VMEM] * 5,
        us=6,
    )(all_rows, own_index, embedding, other_embed, pooled_grad)
    keep, send = call(
        turn_body,
        "turn",
        (shape((OWN, PAIR + 16, SEQ), BF16), shape((OWN, PAIR + 16, SEQ), BF16)),
        specs=[VMEM],
        us=3,
    )(all_rows)
    got = swap_over(send, "core")
    other_index = swap_over(own_index, "core")
    parts = exchange(partial, GROUP)
    bias = jnp.pad(head_bias, (0, GROUPS * CHUNK - VOC)).reshape(GROUPS, 1, CHUNK)
    bias = lax.dynamic_index_in_dim(bias, lax.axis_index(GROUP), 0, keepdims=False)
    grad_block = call(
        slope_body, "slope", shape((GROUPS, PASSAGES, CHUNK), BF16), specs=[VMEM, VMEM], room=8
    )(parts, bias)
    all_grad = exchange(grad_block, GROUP)
    token_grad = call(
        token_body,
        "token_grad",
        shape((COLS, 4096), F32),
        [
            pltpu.VMEM((512, 1024), BF16),
            pltpu.VMEM((512, 1024), BF16),
            pltpu.VMEM((512, 512), F32),
        ],
        [SMEM, VMEM, VMEM],
        us=5,
        room=24,
    )(place, keep, got)
    all_grad, token_grad, other_index = lax.optimization_barrier((all_grad, token_grad, other_index))
    hidden_parts = call(
        hidden_body,
        "hidden_grad",
        shape((OWN * SEQ, PAIR), BF16),
        [
            pltpu.VMEM((OWN * SEQ, PAIR), F32),
            pltpu.VMEM((OWN * SEQ, 1024), BF16),
            pltpu.VMEM((PAIR, VOC), BF16),
            pltpu.VMEM((OWN, 1024), F32),
        ],
        [SMEM] + [VMEM] * 4,
        us=6,
    )(place, all_grad, own_index, embedding, other_embed)
    hidden_got = exchange(hidden_parts.reshape(CHIPS * SHARDS, ROWS, PAIR), HOME)
    embedding_grad, bias_grad = call(
        embed_body,
        "embedding_grad",
        (shape((COLS, VOC), F32), shape((1, VOC), F32)),
        [pltpu.VMEM((GROUPS, PASSAGES, CHUNK), F32)],
        [SMEM] + [VMEM] * 6,
        us=11,
        room=24,
    )(place, token_grad, all_grad, own_index, other_index, keep, got)
    hidden_grad = call(
        sum_body, "sum_shards", shape((ROWS, WIDTH), BF16), specs=[SMEM, VMEM], room=8
    )(place, hidden_got)
    return hidden_grad, embedding_grad, bias_grad.reshape(VOC)


def solution(mesh):
    fine = Mesh(mesh.devices.reshape(2, 4, 2, 4, 8), GROUP + SHARD)
    every = P(GROUP + SHARD, None)
    split = P(GROUP, SHARD)
    return jax.shard_map(
        on_device,
        mesh=fine,
        in_specs=(every, every, P(GROUP + SHARD), P(GROUP), split, split, P(SHARD), split),
        out_specs=(every, split, P(SHARD)),
        check_vma=False,
    )
```

```python
import jax
import jax.numpy as jnp
from jax import lax
from jax.experimental import pallas as pl
from jax.experimental.pallas import tpu as pltpu
from jax.sharding import Mesh, PartitionSpec as P

F32 = jnp.float32
BF16 = jnp.bfloat16
I16 = jnp.int16
I32 = jnp.int32
LANES = 128
SMEM = pl.BlockSpec(memory_space=pltpu.SMEM)
VMEM = pl.BlockSpec(memory_space=pltpu.VMEM)
ANY = pl.BlockSpec(memory_space=pl.ANY)

GROUP = ("zl", "x", "core")
SHARD = ("zh", "y")
HOME = ("zl", "x", "zh", "y")
GROUPS = 16
SHARDS = 32
CHIPS = 8
SEQ = 128
PASSAGES = 32
OWN = 16
COLS = 64
PAIR = 128
WIDTH = 8 * PAIR
ROWS = 8
TILES = 31
VOC = TILES * LANES
CHUNK = 256
IDS = 16


def lane_gather(table, index):
    numbers = lax.GatherDimensionNumbers(
        offset_dims=(),
        collapsed_slice_dims=(1,),
        start_index_map=(1,),
        operand_batching_dims=(0,),
        start_indices_batching_dims=(0,),
    )
    return lax.gather(
        table,
        index[..., None],
        numbers,
        (1, 1),
        mode=lax.GatherScatterMode.PROMISE_IN_BOUNDS,
    )


def load_spots(got_ref, spots):
    for m in range(CHIPS):
        spots[m] = got_ref[m, IDS + 16 :, :].astype(F32).astype(I32)


def spot_row(spots, p, tile):
    return spots[p // 2, pl.ds(2 * tile + p % 2, 1), :]


def pack_body(place_ref, lengths, ids, hidden, grad, index, out_ref, *scratch):
    held, spots, sem = scratch[:5], scratch[5], scratch[6]
    copies = [
        pltpu.make_async_copy(source, target, sem.at[n])
        for n, (source, target) in enumerate(zip((lengths, ids, hidden, grad, index), held))
    ]
    for copy in copies:
        copy.start()
    for copy in copies:
        copy.wait()
    lengths_ref, ids_ref, hidden_ref, grad_ref, index_ref = held
    place = place_ref[0]
    swap = place_ref[1] == 1
    limit = lengths_ref[place // (SEQ // ROWS)]
    spot = (place % (SEQ // ROWS)) * ROWS + lax.broadcasted_iota(I32, (ROWS, 1), 0)
    arrays = [hidden_ref[...].astype(F32), jnp.where(spot < limit, grad_ref[...].astype(F32), 0.0)]
    row = lax.broadcasted_iota(I32, (16, LANES), 0)
    lane = lax.broadcasted_iota(I32, (16, LANES), 1)
    digits = jnp.zeros((16, LANES), I32)
    for r in range(ROWS):
        digits = jnp.where(row == r, ids_ref[r], digits)
    digits = jnp.where(lane == 0, digits & 127, jnp.where(lane == 1, (digits >> 7) & 127, digits >> 14))
    digits = jnp.where(lane < 3, digits, 0).astype(F32).astype(BF16)
    spots[...] = jnp.zeros_like(spots)
    for tile in range(TILES):
        spots[2 * tile : 2 * tile + 2, :] = index_ref[:, tile * LANES : (tile + 1) * LANES].astype(F32)
    positions = spots[...].astype(BF16)
    for m in range(CHIPS):
        parts = []
        for array in arrays:
            pair = array[:, m * PAIR : (m + 1) * PAIR]
            other = jnp.concatenate([pair[:, COLS:], pair[:, :COLS]], axis=1)
            parts.append(jnp.where(swap, other, pair))
        out_ref[m, 0:IDS, :] = jnp.concatenate(parts, axis=0).astype(BF16)
        out_ref[m, IDS : IDS + 16, :] = digits
        out_ref[m, IDS + 16 :, :] = positions


def spread_body(got_ref, out_ref, block, sem):
    hidden = []
    cotangents = []
    digits = []
    for m in range(CHIPS):
        rows = got_ref[m, 0:IDS, :].astype(F32)
        hidden.append(rows[0:ROWS])
        cotangents.append(rows[ROWS:])
        digits.append(got_ref[m, IDS : IDS + 16, :].astype(F32)[0:ROWS])
    block[0:64, :] = jnp.concatenate(hidden, axis=0).astype(BF16)
    block[64:128, :] = jnp.concatenate(cotangents, axis=0).astype(BF16)
    digits = jnp.concatenate(digits + [jnp.zeros((64, LANES), F32)], axis=0).T
    block[128:144, :] = digits[0:16].astype(BF16)
    copies = [pltpu.make_async_copy(block, out_ref.at[s], sem.at[s]) for s in range(SHARDS)]
    for copy in copies:
        copy.start()
    for copy in copies:
        copy.wait()


def turn_body(rows_ref, keep_out, send_out):
    for two in range(CHIPS // 2):
        for h in range(2):
            rows = rows_ref[h * 16 : h * 16 + 16, two * 16 : two * 16 + 16, :].astype(F32)
            for s in range(2):
                p = (2 * two + s) * 2 + h
                turned = rows[:, s * ROWS : (s + 1) * ROWS, :].reshape(SEQ, PAIR).T.astype(BF16)
                keep_out[p, 0:COLS, :] = turned[:COLS]
                send_out[p, 0:COLS, :] = turned[COLS:]
    for pair in range(SHARDS // 2):
        rows = [rows_ref[2 * pair + s, 64:144, :].astype(F32) for s in range(2)]
        turned = jnp.concatenate([r[0:64] for r in rows], axis=0).T.astype(BF16)
        digits = jnp.concatenate([r[64:80, 0:64] for r in rows], axis=1).astype(BF16)
        for out, part in ((keep_out, turned[:COLS]), (send_out, turned[COLS:])):
            out[pair, COLS:PAIR, :] = part
            out[pair, PAIR:, :] = digits


def over_terms(step, one_chunk):
    full = VOC // step

    def loop(i, carry):
        one_chunk(pl.multiple_of(i * step, step), step)
        return carry

    lax.fori_loop(0, full, loop, 0)
    one_chunk(full * step, VOC - full * step)


def logits_body(
    rows_ref, got_ref, own_ref, other_ref, pooled_ref, out_ref, hidden_ref, embed_ref, spots
):
    here = lax.broadcasted_iota(I32, (SEQ, 1), 0)
    embed_ref[0:COLS, :] = own_ref[...]
    embed_ref[COLS:, :] = other_ref[...]
    load_spots(got_ref, spots)
    for two in range(CHIPS // 2):
        for h in range(2):
            rows = rows_ref[h * 16 : h * 16 + 16, two * 16 : two * 16 + 16, :].astype(F32)
            for s in range(2):
                p = (2 * two + s) * 2 + h
                tokens = rows[:, s * ROWS : (s + 1) * ROWS, :].reshape(SEQ, PAIR)
                hidden_ref[p * SEQ : (p + 1) * SEQ, :] = tokens.astype(BF16)

    def one_chunk(first, width):
        lanes = pl.ds(first, width)
        embed = embed_ref[:, lanes]
        for p in range(OWN):
            scores = jnp.dot(
                hidden_ref[p * SEQ : (p + 1) * SEQ, :], embed, preferred_element_type=F32
            )
            index = jnp.concatenate(
                [spot_row(spots, p, first // LANES + n) for n in range(width // LANES)], axis=1
            )
            picked = jnp.sum(jnp.where(index == here, scores, 0.0), axis=0, keepdims=True)
            for at in range(0, width, CHUNK):
                some = min(CHUNK, width - at)
                out_ref[first // CHUNK + at // CHUNK, p : p + 1, 0:some] = picked[:, at : at + some]
        for at in range(0, width, CHUNK):
            some = min(CHUNK, width - at)
            upstream = pooled_ref[:, pl.ds(first + at, some)]
            out_ref[first // CHUNK + at // CHUNK, OWN : OWN + 2, 0:some] = upstream

    over_terms(1024, one_chunk)
    out_ref[:, OWN + 2 :, :] = jnp.zeros((GROUPS, 6, CHUNK), F32)
    out_ref[GROUPS - 1, :, LANES:] = jnp.zeros((24, CHUNK - LANES), F32)


def slope_body(part_ref, bias_ref, out_ref):
    logits = []
    upstream = []
    for c in range(2):
        total = part_ref[c, 0:OWN, :]
        for m in range(1, CHIPS):
            total = total + part_ref[2 * m + c, 0:OWN, :]
        logits.append(total)
        upstream += [part_ref[2 * m + c, OWN : OWN + 2, :] for m in range(CHIPS)]
    logits = jnp.concatenate(logits, axis=0) + bias_ref[...]
    upstream = jnp.concatenate(upstream, axis=0)
    softened = jnp.maximum(logits, 0.0) + jnp.log1p(jnp.exp(-jnp.abs(logits)))
    pooled = jnp.log1p(softened)
    sigmoid = 1.0 / (1.0 + jnp.exp(-logits))
    slope = sigmoid / (1.0 + softened)
    mean_pooled = jnp.sum(pooled, axis=0, keepdims=True) / PASSAGES
    grad = ((upstream + mean_pooled) * slope).astype(BF16)
    for g in range(GROUPS):
        out_ref[g] = grad


def hidden_body(
    place_ref, grad_ref, got_ref, own_ref, other_ref, out_ref, total, left, embed_ref, grads, spots
):
    here = lax.broadcasted_iota(I32, (SEQ, LANES), 0).astype(I16)
    zero = jnp.zeros((), BF16)
    first_core = place_ref[1] == 0
    load_spots(got_ref, spots)
    embed_ref[0:COLS, :] = own_ref[...]
    embed_ref[COLS:, :] = other_ref[...]
    total[...] = jnp.zeros_like(total)

    def one_chunk(first, width):
        for at in range(0, width, CHUNK):
            both = grad_ref[first // CHUNK + at // CHUNK].astype(F32)
            grads[:, at : at + CHUNK] = jnp.where(first_core, both[0:OWN], both[OWN:])
        embed = embed_ref[:, pl.ds(first, width)]
        for group in range(0, OWN, 4):
            for p in range(group, group + 4):
                for tile in range(width // LANES):
                    lanes = slice(tile * LANES, (tile + 1) * LANES)
                    index = spot_row(spots, p, first // LANES + tile)
                    index = jnp.broadcast_to(index, (16, LANES)).astype(I16)
                    value = jnp.broadcast_to(grads[p : p + 1, lanes], (16, LANES)).astype(BF16)
                    index = jnp.concatenate([index] * 8, axis=0)
                    value = jnp.concatenate([value] * 8, axis=0)
                    left[p * SEQ : (p + 1) * SEQ, lanes] = jnp.where(index == here, value, zero)
            rows = slice(group * SEQ, (group + 4) * SEQ)
            total[rows, :] += lax.dot_general(
                left[rows, 0:width], embed, (((1,), (1,)), ((), ())), preferred_element_type=F32
            )

    over_terms(1024, one_chunk)
    out_ref[...] = total[...].astype(BF16)


def token_body(place_ref, keep_ref, got_ref, out_ref, left, right, total):
    base = place_ref[0] * VOC
    low_row = lax.broadcasted_iota(I32, (512, LANES), 0).astype(I16)
    zero = jnp.zeros((), BF16)
    one = jnp.ones((), BF16)
    total[...] = jnp.zeros_like(total)

    def token_block(table_ref, block):
        for s in range(8):
            p = block * 8 + s
            digits = table_ref[p, PAIR:, :].astype(F32).astype(I32)
            local = (digits[2:3] << 14) + (digits[1:2] << 7) + digits[0:1] - base
            inside = (local >= 0) & (local < VOC)
            high = jnp.where(inside, local >> 9, 15)
            high = jnp.broadcast_to(high, (16, LANES)).astype(I16)
            low = jnp.broadcast_to(local & 511, (16, LANES)).astype(I16)
            high = jnp.concatenate([high] * 4, axis=0)
            low = jnp.concatenate([low] * 32, axis=0)
            cotangents = table_ref[p, COLS:PAIR, :]
            lanes = slice(s * LANES, (s + 1) * LANES)
            for h in range(8):
                left[h * COLS : (h + 1) * COLS, lanes] = jnp.where(
                    high == jnp.int16(h), cotangents, zero
                )
            right[:, lanes] = jnp.where(low_row == low, one, zero)
        total[...] += lax.dot_general(
            left[...], right[...], (((1,), (1,)), ((), ())), preferred_element_type=F32
        )

    for table_ref in (keep_ref, got_ref):

        def one_block(block, carry, table_ref=table_ref):
            token_block(table_ref, block)
            return carry

        lax.fori_loop(0, 2, one_block, 0)
    for h in range(8):
        out_ref[:, h * 512 : (h + 1) * 512] = total[h * COLS : (h + 1) * COLS, :]


def embed_body(
    place_ref, token_ref, grad_ref, own_index, other_index, keep_ref, got_ref, out_ref, bias_ref, grads, own_spots, other_spots
):
    first_core = place_ref[1] == 0
    load_spots(own_index, own_spots)
    load_spots(other_index, other_spots)
    for g in range(GROUPS):
        both = grad_ref[g].astype(F32)
        grads[g] = jnp.where(first_core, both, jnp.concatenate([both[OWN:], both[:OWN]], axis=0))

    def one_tile(tile, carry):
        lanes = pl.ds(pl.multiple_of(tile * LANES, LANES), LANES)
        half = pl.ds(pl.multiple_of((tile % 2) * LANES, LANES), LANES)
        totals = [token_ref[d : d + 16, lanes] for d in range(0, COLS, 16)]
        for n, (table_ref, spots) in enumerate(((keep_ref, own_spots), (got_ref, other_spots))):
            for p in range(OWN):
                index = spot_row(spots, p, tile)
                index = jnp.broadcast_to(index, (16, LANES)).astype(I16)
                value = grads[tile // 2, n * OWN + p : n * OWN + p + 1, half]
                for d in range(COLS // 16):
                    picked = lane_gather(table_ref[p, d * 16 : d * 16 + 16, :], index).astype(F32)
                    totals[d] = totals[d] + picked * value
        for d in range(COLS // 16):
            out_ref[d * 16 : d * 16 + 16, lanes] = totals[d]
        bias_ref[:, lanes] = jnp.sum(grads[tile // 2, :, half], axis=0, keepdims=True)
        return carry

    lax.fori_loop(0, TILES, one_tile, 0)


def sum_body(place_ref, part_ref, out_ref):
    swap = place_ref[1] == 1
    for m in range(CHIPS):
        total = part_ref[m * SHARDS].astype(F32)
        for s in range(1, SHARDS):
            total = total + part_ref[m * SHARDS + s].astype(F32)
        other = jnp.concatenate([total[:, COLS:], total[:, :COLS]], axis=1)
        out_ref[:, m * PAIR : (m + 1) * PAIR] = jnp.where(swap, other, total).astype(BF16)


def call(body, name, out, scratch=(), specs=None, us=1, out_specs=None, room=56):
    extra = {} if out_specs is None else {"out_specs": out_specs}
    return pl.pallas_call(
        body,
        out_shape=out,
        in_specs=specs,
        scratch_shapes=scratch,
        compiler_params=pltpu.CompilerParams(vmem_limit_bytes=room * 1024 * 1024),
        cost_estimate=pl.CostEstimate(flops=0, bytes_accessed=3_700_000 * us, transcendentals=0),
        name=name,
        **extra,
    )


def shape(dims, dtype):
    return jax.ShapeDtypeStruct(dims, dtype)


def exchange(x, axis):
    return lax.all_to_all(x, axis, split_axis=0, concat_axis=0, tiled=True)


def swap_over(x, axis):
    return lax.ppermute(x, axis, [(0, 1), (1, 0)])


def on_device(
    hidden, embed_grad, token_ids, lengths, pool_index, embedding, head_bias, pooled_grad
):
    place = jnp.stack([lax.axis_index(name) for name in (SHARD, "core", "zl", "x")]).astype(I32)
    packed = call(
        pack_body,
        "pack",
        shape((CHIPS, IDS + 80, LANES), BF16),
        [
            pltpu.SMEM((2,), I32),
            pltpu.SMEM((ROWS,), I32),
            pltpu.VMEM((ROWS, WIDTH), BF16),
            pltpu.VMEM((ROWS, WIDTH), BF16),
            pltpu.VMEM((2, VOC), I32),
            pltpu.VMEM((64, LANES), F32),
            pltpu.SemaphoreType.DMA((5,)),
        ],
        [SMEM] + [ANY] * 5,
    )(place, lengths, token_ids, hidden, embed_grad, pool_index)
    own_index = exchange(packed, ("zl", "x"))
    rows = call(
        spread_body,
        "spread",
        shape((SHARDS, 144, LANES), BF16),
        [pltpu.VMEM((144, LANES), BF16), pltpu.SemaphoreType.DMA((SHARDS,))],
        [VMEM],
        out_specs=ANY,
        room=8,
    )(own_index)
    all_rows = exchange(rows, SHARD)
    other_embed = swap_over(embedding, "core")
    partial = call(
        logits_body,
        "logits",
        shape((GROUPS, 24, CHUNK), F32),
        [
            pltpu.VMEM((OWN * SEQ, PAIR), BF16),
            pltpu.VMEM((PAIR, VOC), BF16),
            pltpu.VMEM((CHIPS, 64, LANES), I32),
        ],
        [VMEM] * 5,
        us=6,
    )(all_rows, own_index, embedding, other_embed, pooled_grad)
    keep, send = call(
        turn_body,
        "turn",
        (shape((OWN, PAIR + 16, SEQ), BF16), shape((OWN, PAIR + 16, SEQ), BF16)),
        specs=[VMEM],
        us=3,
    )(all_rows)
    got = swap_over(send, "core")
    other_index = swap_over(own_index, "core")
    parts = exchange(partial, GROUP)
    bias = jnp.pad(head_bias, (0, GROUPS * CHUNK - VOC)).reshape(GROUPS, 1, CHUNK)
    bias = lax.dynamic_index_in_dim(bias, lax.axis_index(GROUP), 0, keepdims=False)
    grad_block = call(
        slope_body, "slope", shape((GROUPS, PASSAGES, CHUNK), BF16), specs=[VMEM, VMEM], room=8
    )(parts, bias)
    all_grad = exchange(grad_block, GROUP)
    token_grad = call(
        token_body,
        "token_grad",
        shape((COLS, 4096), F32),
        [
            pltpu.VMEM((512, 1024), BF16),
            pltpu.VMEM((512, 1024), BF16),
            pltpu.VMEM((512, 512), F32),
        ],
        [SMEM, VMEM, VMEM],
        us=5,
        room=24,
    )(place, keep, got)
    all_grad, token_grad, other_index = lax.optimization_barrier((all_grad, token_grad, other_index))
    hidden_parts = call(
        hidden_body,
        "hidden_grad",
        shape((OWN * SEQ, PAIR), BF16),
        [
            pltpu.VMEM((OWN * SEQ, PAIR), F32),
            pltpu.VMEM((OWN * SEQ, 1024), BF16),
            pltpu.VMEM((PAIR, VOC), BF16),
            pltpu.VMEM((OWN, 1024), F32),
            pltpu.VMEM((CHIPS, 64, LANES), I32),
        ],
        [SMEM] + [VMEM] * 4,
        us=6,
    )(place, all_grad, own_index, embedding, other_embed)
    hidden_got = exchange(hidden_parts.reshape(CHIPS * SHARDS, ROWS, PAIR), HOME)
    embedding_grad, bias_grad = call(
        embed_body,
        "embedding_grad",
        (shape((COLS, VOC), F32), shape((1, VOC), F32)),
        [
            pltpu.VMEM((GROUPS, PASSAGES, CHUNK), F32),
            pltpu.VMEM((CHIPS, 64, LANES), I32),
            pltpu.VMEM((CHIPS, 64, LANES), I32),
        ],
        [SMEM] + [VMEM] * 6,
        us=11,
        room=24,
    )(place, token_grad, all_grad, own_index, other_index, keep, got)
    hidden_grad = call(
        sum_body, "sum_shards", shape((ROWS, WIDTH), BF16), specs=[SMEM, VMEM], room=8
    )(place, hidden_got)
    return hidden_grad, embedding_grad, bias_grad.reshape(VOC)


def solution(mesh):
    fine = Mesh(mesh.devices.reshape(2, 4, 2, 4, 8), GROUP + SHARD)
    every = P(GROUP + SHARD, None)
    split = P(GROUP, SHARD)
    return jax.shard_map(
        on_device,
        mesh=fine,
        in_specs=(every, every, P(GROUP + SHARD), P(GROUP), split, split, P(SHARD), split),
        out_specs=(every, split, P(SHARD)),
        check_vma=False,
    )
```

```python
import jax
import jax.numpy as jnp
from jax import lax
from jax.experimental import pallas as pl
from jax.experimental.pallas import tpu as pltpu
from jax.sharding import Mesh, PartitionSpec as P

F32 = jnp.float32
BF16 = jnp.bfloat16
I16 = jnp.int16
I32 = jnp.int32
LANES = 128
SMEM = pl.BlockSpec(memory_space=pltpu.SMEM)
VMEM = pl.BlockSpec(memory_space=pltpu.VMEM)
ANY = pl.BlockSpec(memory_space=pl.ANY)

GROUP = ("zl", "xh", "xl", "core")
FAR = ("zl", "xh")
NEAR = ("xl", "core")
SHARD = ("zh", "y")
GROUPS = 16
SHARDS = 32
QUADS = 4
SEQ = 128
PASSAGES = 32
OWN = 8
COLS = 64
PAIR = 128
QUAD = 256
WIDTH = 4 * QUAD
ROWS = 8
TILES = 31
VOC = TILES * LANES
CHUNK = 256
TOKENS = 32
SPOTS = 48
CARRY = SPOTS + 64


def lane_gather(table, index):
    numbers = lax.GatherDimensionNumbers(
        offset_dims=(),
        collapsed_slice_dims=(1,),
        start_index_map=(1,),
        operand_batching_dims=(0,),
        start_indices_batching_dims=(0,),
    )
    return lax.gather(
        table,
        index[..., None],
        numbers,
        (1, 1),
        mode=lax.GatherScatterMode.PROMISE_IN_BOUNDS,
    )


def load_spots(got_ref, spots):
    for a in range(QUADS):
        spots[a] = got_ref[a, SPOTS:, :].astype(F32).astype(I32)


def spot_row(spots, p, tile):
    return spots[p // 2, pl.ds(2 * tile + p % 2, 1), :]


def by_distance(place_ref, x, axis, unit):
    place = place_ref[1]
    blocks = [lax.slice_in_dim(x, n * unit, (n + 1) * unit, axis=axis) for n in range(4)]
    blocks = [jnp.where(place % 2 == 1, blocks[n ^ 1], blocks[n]) for n in range(4)]
    blocks = [jnp.where(place // 2 == 1, blocks[n ^ 2], blocks[n]) for n in range(4)]
    return jnp.concatenate(blocks, axis=axis)


def pack_body(place_ref, lengths, ids, hidden, grad, index, out_ref, *scratch):
    held, spots, sem = scratch[:5], scratch[5], scratch[6]
    copies = [
        pltpu.make_async_copy(source, target, sem.at[n])
        for n, (source, target) in enumerate(zip((lengths, ids, hidden, grad, index), held))
    ]
    for copy in copies:
        copy.start()
    for copy in copies:
        copy.wait()
    lengths_ref, ids_ref, hidden_ref, grad_ref, index_ref = held
    place = place_ref[0]
    limit = lengths_ref[place // (SEQ // ROWS)]
    spot = (place % (SEQ // ROWS)) * ROWS + lax.broadcasted_iota(I32, (ROWS, 1), 0)
    arrays = [hidden_ref[...].astype(F32), jnp.where(spot < limit, grad_ref[...].astype(F32), 0.0)]
    row = lax.broadcasted_iota(I32, (16, LANES), 0)
    lane = lax.broadcasted_iota(I32, (16, LANES), 1)
    digits = jnp.zeros((16, LANES), I32)
    for r in range(ROWS):
        digits = jnp.where(row == r, ids_ref[r], digits)
    digits = jnp.where(lane == 0, digits & 127, jnp.where(lane == 1, (digits >> 7) & 127, digits >> 14))
    digits = jnp.where(lane < 3, digits, 0).astype(F32).astype(BF16)
    spots[...] = jnp.zeros_like(spots)
    for tile in range(TILES):
        spots[2 * tile : 2 * tile + 2, :] = index_ref[:, tile * LANES : (tile + 1) * LANES].astype(F32)
    positions = spots[...].astype(BF16)
    for a in range(QUADS):
        parts = []
        for array in arrays:
            quad = by_distance(place_ref, array[:, a * QUAD : (a + 1) * QUAD], 1, COLS)
            parts += [quad[:, 0:PAIR], quad[:, PAIR:]]
        out_ref[a, 0:TOKENS, :] = jnp.concatenate(parts, axis=0).astype(BF16)
        out_ref[a, TOKENS:SPOTS, :] = digits
        out_ref[a, SPOTS:, :] = positions


def spread_body(got_ref, out_ref, block, sem):
    quads = [got_ref[a, 0:TOKENS, :].astype(F32) for a in range(QUADS)]
    for n in range(4):
        rows = jnp.concatenate([q[n * ROWS : (n + 1) * ROWS] for q in quads], axis=0)
        block[n * 32 : (n + 1) * 32, :] = rows.astype(BF16)
    digits = [got_ref[a, TOKENS:SPOTS, :].astype(F32)[0:ROWS] for a in range(QUADS)]
    digits = jnp.concatenate(digits + [jnp.zeros((96, LANES), F32)], axis=0).T
    block[128:144, :] = digits[0:16].astype(BF16)
    copies = [pltpu.make_async_copy(block, out_ref.at[s], sem.at[s]) for s in range(SHARDS)]
    for copy in copies:
        copy.start()
    for copy in copies:
        copy.wait()


def token_tiles(rows_ref, half):
    tiles = {}
    for two in range(QUADS // 2):
        for h in range(2):
            at = half * 32 + two * 16
            rows = rows_ref[h * 16 : h * 16 + 16, at : at + 16, :].astype(F32)
            for s in range(2):
                p = (2 * two + s) * 2 + h
                tiles[p] = rows[:, s * ROWS : (s + 1) * ROWS, :].reshape(SEQ, PAIR)
    return tiles


def turn_body(rows_ref, *outs):
    for half in range(2):
        for p, tokens in token_tiles(rows_ref, half).items():
            turned = tokens.T.astype(BF16)
            outs[2 * half][p, 0:COLS, :] = turned[:COLS]
            outs[2 * half + 1][p, 0:COLS, :] = turned[COLS:]
    for four in range(SHARDS // 4):
        rows = [rows_ref[4 * four + s, 64:144, :].astype(F32) for s in range(4)]
        digits = jnp.concatenate([r[64:80, 0:32] for r in rows], axis=1).astype(BF16)
        for half in range(2):
            turned = jnp.concatenate([r[half * 32 : half * 32 + 32] for r in rows], axis=0).T.astype(BF16)
            outs[2 * half][four, COLS:PAIR, :] = turned[:COLS]
            outs[2 * half + 1][four, COLS:PAIR, :] = turned[COLS:]
        for out in outs:
            out[four, PAIR:, :] = digits


def load_embedding(embed_ref, embed_0, embed_1, embed_23):
    embed_ref[0:COLS, :] = embed_0[...]
    embed_ref[COLS:PAIR, :] = embed_1[...]
    embed_ref[PAIR : PAIR + COLS, :] = embed_23[0]
    embed_ref[PAIR + COLS :, :] = embed_23[1]


def over_terms(step, one_chunk):
    full = VOC // step

    def loop(i, carry):
        one_chunk(pl.multiple_of(i * step, step), step)
        return carry

    lax.fori_loop(0, full, loop, 0)
    one_chunk(full * step, VOC - full * step)


def logits_body(
    rows_ref, got_ref, embed_0, embed_1, embed_23, pooled_ref, out_ref, hidden_ref, embed_ref, spots
):
    here = lax.broadcasted_iota(I32, (SEQ, 1), 0)
    load_embedding(embed_ref, embed_0, embed_1, embed_23)
    load_spots(got_ref, spots)
    for half in range(2):
        for p, tokens in token_tiles(rows_ref, half).items():
            hidden_ref[p * SEQ : (p + 1) * SEQ, half * PAIR : (half + 1) * PAIR] = tokens.astype(BF16)

    def one_chunk(first, width):
        lanes = pl.ds(first, width)
        embed = embed_ref[:, lanes]
        for p in range(OWN):
            scores = jnp.dot(
                hidden_ref[p * SEQ : (p + 1) * SEQ, :], embed, preferred_element_type=F32
            )
            index = jnp.concatenate(
                [spot_row(spots, p, first // LANES + n) for n in range(width // LANES)], axis=1
            )
            picked = jnp.sum(jnp.where(index == here, scores, 0.0), axis=0, keepdims=True)
            for at in range(0, width, CHUNK):
                some = min(CHUNK, width - at)
                out_ref[first // CHUNK + at // CHUNK, p : p + 1, 0:some] = picked[:, at : at + some]
        for at in range(0, width, CHUNK):
            some = min(CHUNK, width - at)
            upstream = pooled_ref[:, pl.ds(first + at, some)]
            out_ref[first // CHUNK + at // CHUNK, OWN : OWN + 2, 0:some] = upstream

    over_terms(1024, one_chunk)
    out_ref[:, OWN + 2 :, :] = jnp.zeros((GROUPS, 6, CHUNK), F32)
    out_ref[GROUPS - 1, :, LANES:] = jnp.zeros((16, CHUNK - LANES), F32)


def slope_body(part_ref, bias_ref, out_ref):
    logits = []
    upstream = []
    for b in range(4):
        total = part_ref[b, 0:OWN, :]
        for a in range(1, QUADS):
            total = total + part_ref[4 * a + b, 0:OWN, :]
        logits.append(total)
        upstream += [part_ref[4 * a + b, OWN : OWN + 2, :] for a in range(QUADS)]
    logits = jnp.concatenate(logits, axis=0) + bias_ref[...]
    upstream = jnp.concatenate(upstream, axis=0)
    softened = jnp.maximum(logits, 0.0) + jnp.log1p(jnp.exp(-jnp.abs(logits)))
    pooled = jnp.log1p(softened)
    sigmoid = 1.0 / (1.0 + jnp.exp(-logits))
    slope = sigmoid / (1.0 + softened)
    mean_pooled = jnp.sum(pooled, axis=0, keepdims=True) / PASSAGES
    grad = ((upstream + mean_pooled) * slope).astype(BF16)
    for g in range(GROUPS):
        out_ref[g] = grad


def hidden_body(
    place_ref, grad_ref, got_ref, embed_0, embed_1, embed_23, out_ref, total, left, embed_ref, grads, spots
):
    here = lax.broadcasted_iota(I32, (SEQ, LANES), 0).astype(I16)
    zero = jnp.zeros((), BF16)
    load_spots(got_ref, spots)
    load_embedding(embed_ref, embed_0, embed_1, embed_23)
    total[...] = jnp.zeros_like(total)

    def one_chunk(first, width):
        for at in range(0, width, CHUNK):
            every = grad_ref[first // CHUNK + at // CHUNK].astype(F32)
            grads[:, at : at + CHUNK] = by_distance(place_ref, every, 0, OWN)[0:OWN]
        embed = embed_ref[:, pl.ds(first, width)]
        for group in range(0, OWN, 4):
            for p in range(group, group + 4):
                for tile in range(width // LANES):
                    lanes = slice(tile * LANES, (tile + 1) * LANES)
                    index = spot_row(spots, p, first // LANES + tile)
                    index = jnp.broadcast_to(index, (16, LANES)).astype(I16)
                    value = jnp.broadcast_to(grads[p : p + 1, lanes], (16, LANES)).astype(BF16)
                    index = jnp.concatenate([index] * 8, axis=0)
                    value = jnp.concatenate([value] * 8, axis=0)
                    left[p * SEQ : (p + 1) * SEQ, lanes] = jnp.where(index == here, value, zero)
            rows = slice(group * SEQ, (group + 4) * SEQ)
            total[rows, :] += lax.dot_general(
                left[rows, 0:width], embed, (((1,), (1,)), ((), ())), preferred_element_type=F32
            )

    over_terms(1024, one_chunk)
    out_ref[...] = total[...].astype(BF16)


def token_body(place_ref, table_0, table_1, table_2, table_3, out_ref, left, right, total):
    base = place_ref[0] * VOC
    low_row = lax.broadcasted_iota(I32, (512, LANES), 0).astype(I16)
    zero = jnp.zeros((), BF16)
    one = jnp.ones((), BF16)
    total[...] = jnp.zeros_like(total)

    def token_block(table_ref):
        for p in range(OWN):
            digits = table_ref[p, PAIR:, :].astype(F32).astype(I32)
            local = (digits[2:3] << 14) + (digits[1:2] << 7) + digits[0:1] - base
            inside = (local >= 0) & (local < VOC)
            high = jnp.where(inside, local >> 9, 15)
            high = jnp.broadcast_to(high, (16, LANES)).astype(I16)
            low = jnp.broadcast_to(local & 511, (16, LANES)).astype(I16)
            high = jnp.concatenate([high] * 4, axis=0)
            low = jnp.concatenate([low] * 32, axis=0)
            cotangents = table_ref[p, COLS:PAIR, :]
            lanes = slice(p * LANES, (p + 1) * LANES)
            for h in range(8):
                left[h * COLS : (h + 1) * COLS, lanes] = jnp.where(
                    high == jnp.int16(h), cotangents, zero
                )
            right[:, lanes] = jnp.where(low_row == low, one, zero)
        total[...] += lax.dot_general(
            left[...], right[...], (((1,), (1,)), ((), ())), preferred_element_type=F32
        )

    for table_ref in (table_0, table_1, table_2, table_3):
        token_block(table_ref)
    for h in range(8):
        out_ref[:, h * 512 : (h + 1) * 512] = total[h * COLS : (h + 1) * COLS, :]


def embed_body(place_ref, token_ref, grad_ref, *refs):
    indices, tables = refs[0:4], refs[4:8]
    out_ref, bias_ref, grads = refs[8:11]
    spots = refs[11:15]
    for n in range(4):
        load_spots(indices[n], spots[n])
    for g in range(GROUPS):
        grads[g] = by_distance(place_ref, grad_ref[g].astype(F32), 0, OWN)

    def one_tile(tile, carry):
        lanes = pl.ds(pl.multiple_of(tile * LANES, LANES), LANES)
        half = pl.ds(pl.multiple_of((tile % 2) * LANES, LANES), LANES)
        totals = [token_ref[d : d + 16, lanes] for d in range(0, COLS, 16)]
        for n in range(4):
            for p in range(OWN):
                index = spot_row(spots[n], p, tile)
                index = jnp.broadcast_to(index, (16, LANES)).astype(I16)
                value = grads[tile // 2, n * OWN + p : n * OWN + p + 1, half]
                for d in range(COLS // 16):
                    picked = lane_gather(tables[n][p, d * 16 : d * 16 + 16, :], index).astype(F32)
                    totals[d] = totals[d] + picked * value
        for d in range(COLS // 16):
            out_ref[d * 16 : d * 16 + 16, lanes] = totals[d]
        bias_ref[:, lanes] = jnp.sum(grads[tile // 2, :, half], axis=0, keepdims=True)
        return carry

    lax.fori_loop(0, TILES, one_tile, 0)


def sum_body(place_ref, part_ref, out_ref):
    for a in range(QUADS):
        total = part_ref[a * SHARDS].astype(F32)
        for s in range(1, SHARDS):
            total = total + part_ref[a * SHARDS + s].astype(F32)
        out_ref[:, a * QUAD : (a + 1) * QUAD] = by_distance(place_ref, total, 1, COLS).astype(BF16)


def call(body, name, out, scratch=(), specs=None, us=1, out_specs=None, room=56):
    extra = {} if out_specs is None else {"out_specs": out_specs}
    return pl.pallas_call(
        body,
        out_shape=out,
        in_specs=specs,
        scratch_shapes=scratch,
        compiler_params=pltpu.CompilerParams(vmem_limit_bytes=room * 1024 * 1024),
        cost_estimate=pl.CostEstimate(flops=0, bytes_accessed=3_700_000 * us, transcendentals=0),
        name=name,
        **extra,
    )


def shape(dims, dtype):
    return jax.ShapeDtypeStruct(dims, dtype)


def exchange(x, axis):
    return lax.all_to_all(x, axis, split_axis=0, concat_axis=0, tiled=True)


def from_near(x, n):
    return lax.ppermute(x, NEAR, [(b, b ^ n) for b in range(4)])


def on_device(
    hidden, embed_grad, token_ids, lengths, pool_index, embedding, head_bias, pooled_grad
):
    place = jnp.stack([lax.axis_index(SHARD), lax.axis_index(NEAR)]).astype(I32)
    packed = call(
        pack_body,
        "pack",
        shape((QUADS, CARRY, LANES), BF16),
        [
            pltpu.SMEM((2,), I32),
            pltpu.SMEM((ROWS,), I32),
            pltpu.VMEM((ROWS, WIDTH), BF16),
            pltpu.VMEM((ROWS, WIDTH), BF16),
            pltpu.VMEM((2, VOC), I32),
            pltpu.VMEM((64, LANES), F32),
            pltpu.SemaphoreType.DMA((5,)),
        ],
        [SMEM] + [ANY] * 5,
    )(place, lengths, token_ids, hidden, embed_grad, pool_index)
    got = exchange(packed, FAR)
    rows = call(
        spread_body,
        "spread",
        shape((SHARDS, 144, LANES), BF16),
        [pltpu.VMEM((144, LANES), BF16), pltpu.SemaphoreType.DMA((SHARDS,))],
        [VMEM],
        out_specs=ANY,
        room=8,
    )(got)
    all_rows = exchange(rows, SHARD)
    embed_1 = from_near(embedding, 1)
    embed_23 = from_near(jnp.stack([embedding, embed_1]), 2)
    spots = [got] + [from_near(got, n) for n in range(1, 4)]
    all_rows, embed_1, embed_23, *spots = lax.optimization_barrier((all_rows, embed_1, embed_23, *spots))
    embed = (embedding, embed_1, embed_23)
    partial = call(
        logits_body,
        "logits",
        shape((GROUPS, 16, CHUNK), F32),
        [
            pltpu.VMEM((OWN * SEQ, QUAD), BF16),
            pltpu.VMEM((QUAD, VOC), BF16),
            pltpu.VMEM((QUADS, 64, LANES), I32),
        ],
        [VMEM] * 6,
        us=5,
    )(all_rows, spots[0], *embed, pooled_grad)
    tables = call(
        turn_body,
        "turn",
        (shape((OWN, PAIR + 16, SEQ), BF16),) * 4,
        specs=[VMEM],
        us=3,
    )(all_rows)
    tables = [tables[0]] + [from_near(tables[n], n) for n in range(1, 4)]
    parts = exchange(partial, GROUP)
    bias = jnp.pad(head_bias, (0, GROUPS * CHUNK - VOC)).reshape(GROUPS, 1, CHUNK)
    bias = lax.dynamic_index_in_dim(bias, lax.axis_index(GROUP), 0, keepdims=False)
    grad_block = call(
        slope_body, "slope", shape((GROUPS, PASSAGES, CHUNK), BF16), specs=[VMEM, VMEM], room=8
    )(parts, bias)
    all_grad = exchange(grad_block, GROUP)
    token_grad = call(
        token_body,
        "token_grad",
        shape((COLS, 4096), F32),
        [
            pltpu.VMEM((512, 1024), BF16),
            pltpu.VMEM((512, 1024), BF16),
            pltpu.VMEM((512, 512), F32),
        ],
        [SMEM] + [VMEM] * 4,
        us=5,
        room=24,
    )(place, *tables)
    all_grad, token_grad = lax.optimization_barrier((all_grad, token_grad))
    hidden_parts = call(
        hidden_body,
        "hidden_grad",
        shape((OWN * SEQ, QUAD), BF16),
        [
            pltpu.VMEM((OWN * SEQ, QUAD), F32),
            pltpu.VMEM((OWN * SEQ, 1024), BF16),
            pltpu.VMEM((QUAD, VOC), BF16),
            pltpu.VMEM((OWN, 1024), F32),
            pltpu.VMEM((QUADS, 64, LANES), I32),
        ],
        [SMEM] + [VMEM] * 5,
        us=5,
    )(place, all_grad, spots[0], *embed)
    hidden_got = exchange(hidden_parts.reshape(QUADS * SHARDS, ROWS, QUAD), FAR + SHARD)
    embedding_grad, bias_grad = call(
        embed_body,
        "embedding_grad",
        (shape((COLS, VOC), F32), shape((1, VOC), F32)),
        [pltpu.VMEM((GROUPS, PASSAGES, CHUNK), F32)] + [pltpu.VMEM((QUADS, 64, LANES), I32)] * 4,
        [SMEM] + [VMEM] * 10,
        us=11,
        room=24,
    )(place, token_grad, all_grad, *spots, *tables)
    hidden_grad = call(
        sum_body, "sum_shards", shape((ROWS, WIDTH), BF16), specs=[SMEM, VMEM], room=8
    )(place, hidden_got)
    return hidden_grad, embedding_grad, bias_grad.reshape(VOC)


def solution(mesh):
    fine = Mesh(mesh.devices.reshape(2, 2, 2, 2, 4, 8), GROUP + SHARD)
    every = P(GROUP + SHARD, None)
    split = P(GROUP, SHARD)
    return jax.shard_map(
        on_device,
        mesh=fine,
        in_specs=(every, every, P(GROUP + SHARD), P(GROUP), split, split, P(SHARD), split),
        out_specs=(every, split, P(SHARD)),
        check_vma=False,
    )
```

```python
import jax
import jax.numpy as jnp
from jax import lax
from jax.experimental import pallas as pl
from jax.experimental.pallas import tpu as pltpu
from jax.sharding import Mesh, PartitionSpec as P

F32 = jnp.float32
BF16 = jnp.bfloat16
I16 = jnp.int16
I32 = jnp.int32
LANES = 128
SMEM = pl.BlockSpec(memory_space=pltpu.SMEM)
VMEM = pl.BlockSpec(memory_space=pltpu.VMEM)
ANY = pl.BlockSpec(memory_space=pl.ANY)

GROUP = ("zl", "x", "core")
SHARD = ("zh", "y")
HOME = ("zl", "x", "zh", "y")
GROUPS = 16
SHARDS = 32
CHIPS = 8
SEQ = 128
PASSAGES = 32
OWN = 16
COLS = 64
PAIR = 128
WIDTH = 8 * PAIR
ROWS = 8
TILES = 31
VOC = TILES * LANES
CHUNK = 256
IDS = 16


def lane_gather(table, index):
    numbers = lax.GatherDimensionNumbers(
        offset_dims=(),
        collapsed_slice_dims=(1,),
        start_index_map=(1,),
        operand_batching_dims=(0,),
        start_indices_batching_dims=(0,),
    )
    return lax.gather(
        table,
        index[..., None],
        numbers,
        (1, 1),
        mode=lax.GatherScatterMode.PROMISE_IN_BOUNDS,
    )


def load_spots(got_ref, spots):
    for m in range(CHIPS):
        spots[m] = got_ref[m, IDS + 16 :, :].astype(F32).astype(I32)


def spot_row(spots, p, tile):
    return spots[p // 2, pl.ds(2 * tile + p % 2, 1), :]


def pack_body(lengths, ids, hidden, grad, index, out_ref, *scratch):
    held, spots, sem = scratch[:5], scratch[5], scratch[6]
    copies = [
        pltpu.make_async_copy(source, target, sem.at[n])
        for n, (source, target) in enumerate(zip((lengths, ids, hidden, grad, index), held))
    ]
    for copy in copies:
        copy.start()
    for copy in copies:
        copy.wait()
    lengths_ref, ids_ref, hidden_ref, grad_ref, index_ref = held
    place = lax.axis_index(SHARD)
    swap = lax.axis_index("core") == 1
    limit = lengths_ref[place // (SEQ // ROWS)]
    spot = (place % (SEQ // ROWS)) * ROWS + lax.broadcasted_iota(I32, (ROWS, 1), 0)
    arrays = [hidden_ref[...].astype(F32), jnp.where(spot < limit, grad_ref[...].astype(F32), 0.0)]
    row = lax.broadcasted_iota(I32, (16, LANES), 0)
    lane = lax.broadcasted_iota(I32, (16, LANES), 1)
    digits = jnp.zeros((16, LANES), I32)
    for r in range(ROWS):
        digits = jnp.where(row == r, ids_ref[r], digits)
    digits = jnp.where(lane == 0, digits & 127, jnp.where(lane == 1, (digits >> 7) & 127, digits >> 14))
    digits = jnp.where(lane < 3, digits, 0).astype(F32).astype(BF16)
    spots[...] = jnp.zeros_like(spots)
    for tile in range(TILES):
        spots[2 * tile : 2 * tile + 2, :] = index_ref[:, tile * LANES : (tile + 1) * LANES].astype(F32)
    positions = spots[...].astype(BF16)
    for m in range(CHIPS):
        parts = []
        for array in arrays:
            pair = array[:, m * PAIR : (m + 1) * PAIR]
            other = jnp.concatenate([pair[:, COLS:], pair[:, :COLS]], axis=1)
            parts.append(jnp.where(swap, other, pair))
        out_ref[m, 0:IDS, :] = jnp.concatenate(parts, axis=0).astype(BF16)
        out_ref[m, IDS : IDS + 16, :] = digits
        out_ref[m, IDS + 16 :, :] = positions


def spread_body(got_ref, out_ref, block, sem):
    hidden = []
    cotangents = []
    digits = []
    for m in range(CHIPS):
        rows = got_ref[m, 0:IDS, :].astype(F32)
        hidden.append(rows[0:ROWS])
        cotangents.append(rows[ROWS:])
        digits.append(got_ref[m, IDS : IDS + 16, :].astype(F32)[0:ROWS])
    block[0:64, :] = jnp.concatenate(hidden, axis=0).astype(BF16)
    block[64:128, :] = jnp.concatenate(cotangents, axis=0).astype(BF16)
    digits = jnp.concatenate(digits + [jnp.zeros((64, LANES), F32)], axis=0).T
    block[128:144, :] = digits[0:16].astype(BF16)
    copies = [pltpu.make_async_copy(block, out_ref.at[s], sem.at[s]) for s in range(SHARDS)]
    for copy in copies:
        copy.start()
    for copy in copies:
        copy.wait()


def turn_body(rows_ref, keep_out, send_out):
    for two in range(CHIPS // 2):
        for h in range(2):
            rows = rows_ref[h * 16 : h * 16 + 16, two * 16 : two * 16 + 16, :].astype(F32)
            for s in range(2):
                p = (2 * two + s) * 2 + h
                turned = rows[:, s * ROWS : (s + 1) * ROWS, :].reshape(SEQ, PAIR).T.astype(BF16)
                keep_out[p, 0:COLS, :] = turned[:COLS]
                send_out[p, 0:COLS, :] = turned[COLS:]
    for pair in range(SHARDS // 2):
        rows = [rows_ref[2 * pair + s, 64:144, :].astype(F32) for s in range(2)]
        turned = jnp.concatenate([r[0:64] for r in rows], axis=0).T.astype(BF16)
        digits = jnp.concatenate([r[64:80, 0:64] for r in rows], axis=1).astype(BF16)
        for out, part in ((keep_out, turned[:COLS]), (send_out, turned[COLS:])):
            out[pair, COLS:PAIR, :] = part
            out[pair, PAIR:, :] = digits


def over_terms(step, one_chunk):
    full = VOC // step

    def loop(i, carry):
        one_chunk(pl.multiple_of(i * step, step), step)
        return carry

    lax.fori_loop(0, full, loop, 0)
    one_chunk(full * step, VOC - full * step)


def logits_body(
    rows_ref, got_ref, own_ref, other_ref, pooled_ref, out_ref, hidden_ref, embed_ref, spots
):
    here = lax.broadcasted_iota(I32, (SEQ, 1), 0)
    embed_ref[0:COLS, :] = own_ref[...]
    embed_ref[COLS:, :] = other_ref[...]
    load_spots(got_ref, spots)
    for two in range(CHIPS // 2):
        for h in range(2):
            rows = rows_ref[h * 16 : h * 16 + 16, two * 16 : two * 16 + 16, :].astype(F32)
            for s in range(2):
                p = (2 * two + s) * 2 + h
                tokens = rows[:, s * ROWS : (s + 1) * ROWS, :].reshape(SEQ, PAIR)
                hidden_ref[p * SEQ : (p + 1) * SEQ, :] = tokens.astype(BF16)

    def one_chunk(first, width):
        lanes = pl.ds(first, width)
        embed = embed_ref[:, lanes]
        for p in range(OWN):
            scores = jnp.dot(
                hidden_ref[p * SEQ : (p + 1) * SEQ, :], embed, preferred_element_type=F32
            )
            index = jnp.concatenate(
                [spot_row(spots, p, first // LANES + n) for n in range(width // LANES)], axis=1
            )
            picked = jnp.sum(jnp.where(index == here, scores, 0.0), axis=0, keepdims=True)
            for at in range(0, width, CHUNK):
                some = min(CHUNK, width - at)
                out_ref[first // CHUNK + at // CHUNK, p : p + 1, 0:some] = picked[:, at : at + some]
        for at in range(0, width, CHUNK):
            some = min(CHUNK, width - at)
            upstream = pooled_ref[:, pl.ds(first + at, some)]
            out_ref[first // CHUNK + at // CHUNK, OWN : OWN + 2, 0:some] = upstream

    over_terms(1024, one_chunk)
    out_ref[:, OWN + 2 :, :] = jnp.zeros((GROUPS, 6, CHUNK), F32)
    out_ref[GROUPS - 1, :, LANES:] = jnp.zeros((24, CHUNK - LANES), F32)


def slope_body(part_ref, bias_ref, out_ref):
    logits = []
    upstream = []
    for c in range(2):
        total = part_ref[c, 0:OWN, :]
        for m in range(1, CHIPS):
            total = total + part_ref[2 * m + c, 0:OWN, :]
        logits.append(total)
        upstream += [part_ref[2 * m + c, OWN : OWN + 2, :] for m in range(CHIPS)]
    logits = jnp.concatenate(logits, axis=0) + bias_ref[...]
    upstream = jnp.concatenate(upstream, axis=0)
    softened = jnp.maximum(logits, 0.0) + jnp.log1p(jnp.exp(-jnp.abs(logits)))
    pooled = jnp.log1p(softened)
    sigmoid = 1.0 / (1.0 + jnp.exp(-logits))
    slope = sigmoid / (1.0 + softened)
    mean_pooled = jnp.sum(pooled, axis=0, keepdims=True) / PASSAGES
    grad = ((upstream + mean_pooled) * slope).astype(BF16)
    for g in range(GROUPS):
        out_ref[g] = grad


def hidden_body(
    place_ref, grad_ref, got_ref, own_ref, other_ref, out_ref, total, left, embed_ref, grads, spots
):
    here = lax.broadcasted_iota(I32, (SEQ, LANES), 0).astype(I16)
    zero = jnp.zeros((), BF16)
    first_core = place_ref[1] == 0
    load_spots(got_ref, spots)
    embed_ref[0:COLS, :] = own_ref[...]
    embed_ref[COLS:, :] = other_ref[...]
    total[...] = jnp.zeros_like(total)

    def one_chunk(first, width):
        for at in range(0, width, CHUNK):
            both = grad_ref[first // CHUNK + at // CHUNK].astype(F32)
            grads[:, at : at + CHUNK] = jnp.where(first_core, both[0:OWN], both[OWN:])
        embed = embed_ref[:, pl.ds(first, width)]
        for group in range(0, OWN, 4):
            for p in range(group, group + 4):
                for tile in range(width // LANES):
                    lanes = slice(tile * LANES, (tile + 1) * LANES)
                    index = spot_row(spots, p, first // LANES + tile)
                    index = jnp.broadcast_to(index, (16, LANES)).astype(I16)
                    value = jnp.broadcast_to(grads[p : p + 1, lanes], (16, LANES)).astype(BF16)
                    index = jnp.concatenate([index] * 8, axis=0)
                    value = jnp.concatenate([value] * 8, axis=0)
                    left[p * SEQ : (p + 1) * SEQ, lanes] = jnp.where(index == here, value, zero)
            rows = slice(group * SEQ, (group + 4) * SEQ)
            total[rows, :] += lax.dot_general(
                left[rows, 0:width], embed, (((1,), (1,)), ((), ())), preferred_element_type=F32
            )

    over_terms(1024, one_chunk)
    out_ref[...] = total[...].astype(BF16)


def token_body(place_ref, keep_ref, got_ref, out_ref, left, right, total):
    base = place_ref[0] * VOC
    low_row = lax.broadcasted_iota(I32, (512, LANES), 0).astype(I16)
    zero = jnp.zeros((), BF16)
    one = jnp.ones((), BF16)
    total[...] = jnp.zeros_like(total)

    def token_block(table_ref, block):
        for s in range(8):
            p = block * 8 + s
            digits = table_ref[p, PAIR:, :].astype(F32).astype(I32)
            local = (digits[2:3] << 14) + (digits[1:2] << 7) + digits[0:1] - base
            inside = (local >= 0) & (local < VOC)
            high = jnp.where(inside, local >> 9, 15)
            high = jnp.broadcast_to(high, (16, LANES)).astype(I16)
            low = jnp.broadcast_to(local & 511, (16, LANES)).astype(I16)
            high = jnp.concatenate([high] * 4, axis=0)
            low = jnp.concatenate([low] * 32, axis=0)
            cotangents = table_ref[p, COLS:PAIR, :]
            lanes = slice(s * LANES, (s + 1) * LANES)
            for h in range(8):
                left[h * COLS : (h + 1) * COLS, lanes] = jnp.where(
                    high == jnp.int16(h), cotangents, zero
                )
            right[:, lanes] = jnp.where(low_row == low, one, zero)
        total[...] += lax.dot_general(
            left[...], right[...], (((1,), (1,)), ((), ())), preferred_element_type=F32
        )

    for table_ref in (keep_ref, got_ref):

        def one_block(block, carry, table_ref=table_ref):
            token_block(table_ref, block)
            return carry

        lax.fori_loop(0, 2, one_block, 0)
    for h in range(8):
        out_ref[:, h * 512 : (h + 1) * 512] = total[h * COLS : (h + 1) * COLS, :]


def embed_body(
    place_ref, token_ref, grad_ref, own_index, other_index, keep_ref, got_ref, out_ref, bias_ref, grads, own_spots, other_spots
):
    first_core = place_ref[1] == 0
    load_spots(own_index, own_spots)
    load_spots(other_index, other_spots)
    for g in range(GROUPS):
        both = grad_ref[g].astype(F32)
        grads[g] = jnp.where(first_core, both, jnp.concatenate([both[OWN:], both[:OWN]], axis=0))

    def one_tile(tile, carry):
        lanes = pl.ds(pl.multiple_of(tile * LANES, LANES), LANES)
        half = pl.ds(pl.multiple_of((tile % 2) * LANES, LANES), LANES)
        totals = [token_ref[d : d + 16, lanes] for d in range(0, COLS, 16)]
        for n, (table_ref, spots) in enumerate(((keep_ref, own_spots), (got_ref, other_spots))):
            for p in range(OWN):
                index = spot_row(spots, p, tile)
                index = jnp.broadcast_to(index, (16, LANES)).astype(I16)
                value = grads[tile // 2, n * OWN + p : n * OWN + p + 1, half]
                for d in range(COLS // 16):
                    picked = lane_gather(table_ref[p, d * 16 : d * 16 + 16, :], index).astype(F32)
                    totals[d] = totals[d] + picked * value
        for d in range(COLS // 16):
            out_ref[d * 16 : d * 16 + 16, lanes] = totals[d]
        bias_ref[:, lanes] = jnp.sum(grads[tile // 2, :, half], axis=0, keepdims=True)
        return carry

    lax.fori_loop(0, TILES, one_tile, 0)


def sum_body(place_ref, part_ref, out_ref):
    swap = place_ref[1] == 1
    for m in range(CHIPS):
        total = part_ref[m * SHARDS].astype(F32)
        for s in range(1, SHARDS):
            total = total + part_ref[m * SHARDS + s].astype(F32)
        other = jnp.concatenate([total[:, COLS:], total[:, :COLS]], axis=1)
        out_ref[:, m * PAIR : (m + 1) * PAIR] = jnp.where(swap, other, total).astype(BF16)


def call(body, name, out, scratch=(), specs=None, us=1, out_specs=None, room=24):
    extra = {} if out_specs is None else {"out_specs": out_specs}
    return pl.pallas_call(
        body,
        out_shape=out,
        in_specs=specs,
        scratch_shapes=scratch,
        compiler_params=pltpu.CompilerParams(vmem_limit_bytes=room * 1024 * 1024),
        cost_estimate=pl.CostEstimate(flops=0, bytes_accessed=3_700_000 * us, transcendentals=0),
        name=name,
        **extra,
    )


def shape(dims, dtype):
    return jax.ShapeDtypeStruct(dims, dtype)


def exchange(x, axis):
    return lax.all_to_all(x, axis, split_axis=0, concat_axis=0, tiled=True)


def swap_over(x, axis):
    return lax.ppermute(x, axis, [(0, 1), (1, 0)])


def on_device(
    hidden, embed_grad, token_ids, lengths, pool_index, embedding, head_bias, pooled_grad
):
    place = jnp.stack([lax.axis_index(name) for name in (SHARD, "core", "zl", "x")]).astype(I32)
    packed = call(
        pack_body,
        "pack",
        shape((CHIPS, IDS + 80, LANES), BF16),
        [
            pltpu.SMEM((2,), I32),
            pltpu.SMEM((ROWS,), I32),
            pltpu.VMEM((ROWS, WIDTH), BF16),
            pltpu.VMEM((ROWS, WIDTH), BF16),
            pltpu.VMEM((2, VOC), I32),
            pltpu.VMEM((64, LANES), F32),
            pltpu.SemaphoreType.DMA((5,)),
        ],
        [ANY] * 5,
        room=56,
    )(lengths, token_ids, hidden, embed_grad, pool_index)
    own_index = exchange(packed, ("zl", "x"))
    rows = call(
        spread_body,
        "spread",
        shape((SHARDS, 144, LANES), BF16),
        [pltpu.VMEM((144, LANES), BF16), pltpu.SemaphoreType.DMA((SHARDS,))],
        [VMEM],
        out_specs=ANY,
        room=8,
    )(own_index)
    all_rows = exchange(rows, SHARD)
    other_embed = swap_over(embedding, "core")
    partial = call(
        logits_body,
        "logits",
        shape((GROUPS, 24, CHUNK), F32),
        [
            pltpu.VMEM((OWN * SEQ, PAIR), BF16),
            pltpu.VMEM((PAIR, VOC), BF16),
            pltpu.VMEM((CHIPS, 64, LANES), I32),
        ],
        [VMEM] * 5,
        us=6,
    )(all_rows, own_index, embedding, other_embed, pooled_grad)
    keep, send = call(
        turn_body,
        "turn",
        (shape((OWN, PAIR + 16, SEQ), BF16), shape((OWN, PAIR + 16, SEQ), BF16)),
        specs=[VMEM],
        us=3,
    )(all_rows)
    got = swap_over(send, "core")
    other_index = swap_over(own_index, "core")
    parts = exchange(partial, GROUP)
    bias = jnp.pad(head_bias, (0, GROUPS * CHUNK - VOC)).reshape(GROUPS, 1, CHUNK)
    bias = lax.dynamic_index_in_dim(bias, lax.axis_index(GROUP), 0, keepdims=False)
    grad_block = call(
        slope_body, "slope", shape((GROUPS, PASSAGES, CHUNK), BF16), specs=[VMEM, VMEM], room=8
    )(parts, bias)
    all_grad = exchange(grad_block, GROUP)
    token_grad = call(
        token_body,
        "token_grad",
        shape((COLS, 4096), F32),
        [
            pltpu.VMEM((512, 1024), BF16),
            pltpu.VMEM((512, 1024), BF16),
            pltpu.VMEM((512, 512), F32),
        ],
        [SMEM, VMEM, VMEM],
        us=5,
        room=24,
    )(place, keep, got)
    all_grad, token_grad, other_index = lax.optimization_barrier((all_grad, token_grad, other_index))
    hidden_parts = call(
        hidden_body,
        "hidden_grad",
        shape((OWN * SEQ, PAIR), BF16),
        [
            pltpu.VMEM((OWN * SEQ, PAIR), F32),
            pltpu.VMEM((OWN * SEQ, 1024), BF16),
            pltpu.VMEM((PAIR, VOC), BF16),
            pltpu.VMEM((OWN, 1024), F32),
            pltpu.VMEM((CHIPS, 64, LANES), I32),
        ],
        [SMEM] + [VMEM] * 4,
        us=6,
    )(place, all_grad, own_index, embedding, other_embed)
    hidden_got = exchange(hidden_parts.reshape(CHIPS * SHARDS, ROWS, PAIR), HOME)
    embedding_grad, bias_grad = call(
        embed_body,
        "embedding_grad",
        (shape((COLS, VOC), F32), shape((1, VOC), F32)),
        [
            pltpu.VMEM((GROUPS, PASSAGES, CHUNK), F32),
            pltpu.VMEM((CHIPS, 64, LANES), I32),
            pltpu.VMEM((CHIPS, 64, LANES), I32),
        ],
        [SMEM] + [VMEM] * 6,
        us=11,
        room=24,
    )(place, token_grad, all_grad, own_index, other_index, keep, got)
    hidden_grad = call(
        sum_body, "sum_shards", shape((ROWS, WIDTH), BF16), specs=[SMEM, VMEM], room=8
    )(place, hidden_got)
    return hidden_grad, embedding_grad, bias_grad.reshape(VOC)


def solution(mesh):
    fine = Mesh(mesh.devices.reshape(2, 4, 2, 4, 8), GROUP + SHARD)
    every = P(GROUP + SHARD, None)
    split = P(GROUP, SHARD)
    return jax.shard_map(
        on_device,
        mesh=fine,
        in_specs=(every, every, P(GROUP + SHARD), P(GROUP), split, split, P(SHARD), split),
        out_specs=(every, split, P(SHARD)),
        check_vma=False,
    )
```

```python
import jax
import jax.numpy as jnp
from jax import lax
from jax.experimental import pallas as pl
from jax.experimental.pallas import tpu as pltpu
from jax.sharding import Mesh, PartitionSpec as P

F32 = jnp.float32
BF16 = jnp.bfloat16
I16 = jnp.int16
I32 = jnp.int32
LANES = 128
SMEM = pl.BlockSpec(memory_space=pltpu.SMEM)
VMEM = pl.BlockSpec(memory_space=pltpu.VMEM)
ANY = pl.BlockSpec(memory_space=pl.ANY)

GROUP = ("zl", "x", "core")
SHARD = ("zh", "y")
HOME = ("zl", "x", "zh", "y")
GROUPS = 16
SHARDS = 32
CHIPS = 8
SEQ = 128
PASSAGES = 32
OWN = 16
COLS = 64
PAIR = 128
WIDTH = 8 * PAIR
ROWS = 8
TILES = 31
VOC = TILES * LANES
CHUNK = 256
IDS = 16
SLOTS = 24


def lane_gather(table, index):
    numbers = lax.GatherDimensionNumbers(
        offset_dims=(),
        collapsed_slice_dims=(1,),
        start_index_map=(1,),
        operand_batching_dims=(0,),
        start_indices_batching_dims=(0,),
    )
    return lax.gather(
        table,
        index[..., None],
        numbers,
        (1, 1),
        mode=lax.GatherScatterMode.PROMISE_IN_BOUNDS,
    )


def load_spots(got_ref, spots):
    for m in range(CHIPS):
        spots[m] = got_ref[m, IDS + 16 :, :].astype(F32).astype(I32)


def spot_row(spots, p, tile):
    return spots[p // 2, pl.ds(2 * tile + p % 2, 1), :]


def pack_body(lengths, ids, hidden, grad, index, out_ref, *scratch):
    held, spots, sem = scratch[:5], scratch[5], scratch[6]
    copies = [
        pltpu.make_async_copy(source, target, sem.at[n])
        for n, (source, target) in enumerate(zip((lengths, ids, hidden, grad, index), held))
    ]
    for copy in copies:
        copy.start()
    for copy in copies:
        copy.wait()
    lengths_ref, ids_ref, hidden_ref, grad_ref, index_ref = held
    place = lax.axis_index(SHARD)
    swap = lax.axis_index("core") == 1
    limit = lengths_ref[place // (SEQ // ROWS)]
    spot = (place % (SEQ // ROWS)) * ROWS + lax.broadcasted_iota(I32, (ROWS, 1), 0)
    arrays = [hidden_ref[...].astype(F32), jnp.where(spot < limit, grad_ref[...].astype(F32), 0.0)]
    row = lax.broadcasted_iota(I32, (16, LANES), 0)
    lane = lax.broadcasted_iota(I32, (16, LANES), 1)
    digits = jnp.zeros((16, LANES), I32)
    for r in range(ROWS):
        digits = jnp.where(row == r, ids_ref[r], digits)
    digits = jnp.where(lane == 0, digits & 127, jnp.where(lane == 1, (digits >> 7) & 127, digits >> 14))
    digits = jnp.where(lane < 3, digits, 0).astype(F32).astype(BF16)
    spots[...] = jnp.zeros_like(spots)
    for tile in range(TILES):
        spots[2 * tile : 2 * tile + 2, :] = index_ref[:, tile * LANES : (tile + 1) * LANES].astype(F32)
    positions = spots[...].astype(BF16)
    for m in range(CHIPS):
        parts = []
        for array in arrays:
            pair = array[:, m * PAIR : (m + 1) * PAIR]
            other = jnp.concatenate([pair[:, COLS:], pair[:, :COLS]], axis=1)
            parts.append(jnp.where(swap, other, pair))
        out_ref[m, 0:IDS, :] = jnp.concatenate(parts, axis=0).astype(BF16)
        out_ref[m, IDS : IDS + 16, :] = digits
        out_ref[m, IDS + 16 :, :] = positions


def spread_body(got_ref, out_ref, rest_ref):
    tokens = 64
    hidden = []
    cotangents = []
    digits = []
    for m in range(CHIPS):
        rows = got_ref[m, 0:IDS, :].astype(F32)
        hidden.append(rows[0:ROWS])
        cotangents.append(rows[ROWS:])
        digits.append(got_ref[m, IDS : IDS + 16, :].astype(F32)[0:ROWS])
    hidden = jnp.concatenate(hidden, axis=0).astype(BF16)
    blank = jnp.zeros((LANES - tokens, LANES), F32)
    cotangents = jnp.concatenate(cotangents + [blank], axis=0)
    digits = jnp.concatenate(digits + [blank], axis=0)
    across = digits.T[0:16]

    def owner(ids):
        return ((ids + 0.5) * (1.0 / VOC)).astype(I32)

    lane = lax.broadcasted_iota(I32, (LANES, LANES), 1)
    row = lax.broadcasted_iota(I32, (LANES, LANES), 0)
    across_owner = owner(across[0:1] + 128.0 * across[1:2] + 16384.0 * across[2:3])
    across_owner = jnp.where(lane[0:1] < tokens, across_owner, SHARDS)
    down_owner = owner(digits[:, 0:1] + 128.0 * digits[:, 1:2] + 16384.0 * digits[:, 2:3])
    down_owner = jnp.where(row < tokens, down_owner, SHARDS + 1)
    same = down_owner == across_owner
    across_rank = jnp.sum(jnp.where(same & (row < lane), 1.0, 0.0), axis=0, keepdims=True).astype(I32)
    down_rank = jnp.sum(jnp.where(same & (lane < row), 1.0, 0.0), axis=1, keepdims=True).astype(I32)
    more = jnp.max(jnp.where(lane[0:1] < tokens, across_rank, 0), axis=1, keepdims=True) >= SLOTS
    rest = jnp.where(down_rank >= SLOTS, cotangents, 0.0)[0:tokens]
    rest_ref[...] = jnp.concatenate([rest, across], axis=0).astype(BF16)
    flag = jnp.where(more, 1.0, 0.0) + jnp.zeros((1, LANES), F32)
    packed = cotangents.astype(BF16)
    across = across.astype(BF16)
    slot = lax.broadcasted_iota(I32, (32, 1), 0)
    slot = jnp.where(slot < SLOTS, slot, -1)
    for s in range(SHARDS):
        place = jnp.where((across_owner == s) & (across_rank == slot), 1.0, 0.0).astype(BF16)
        rows = jnp.dot(place, packed, preferred_element_type=F32)
        codes = lax.dot_general(
            across, place, (((1,), (1,)), ((), ())), preferred_element_type=F32
        )
        codes = jnp.concatenate([codes[0:7], jnp.zeros((7, LANES - 32), F32)], axis=1)
        out_ref[s, 0:64, :] = hidden
        out_ref[s, 64:96, :] = jnp.concatenate([rows[0:SLOTS], codes, flag], axis=0).astype(BF16)


def turn_body(rows_ref, keep_out, send_out):
    for two in range(CHIPS // 2):
        for h in range(2):
            rows = rows_ref[h * 16 : h * 16 + 16, two * 16 : two * 16 + 16, :].astype(F32)
            for s in range(2):
                p = (2 * two + s) * 2 + h
                turned = rows[:, s * ROWS : (s + 1) * ROWS, :].reshape(SEQ, PAIR).T.astype(BF16)
                keep_out[p, 0:COLS, :] = turned[:COLS]
                send_out[p, 0:COLS, :] = turned[COLS:]
    keep = lax.broadcasted_iota(I32, (32, 1), 0) < SLOTS
    for four in range(SHARDS // 4):
        rows = [rows_ref[4 * four + s, 64:96, :].astype(F32) for s in range(4)]
        turned = jnp.concatenate([jnp.where(keep, r, 0.0) for r in rows], axis=0).T.astype(BF16)
        digits = jnp.concatenate([r[24:32, 0:32] for r in rows], axis=1)
        digits = jnp.concatenate([digits, jnp.zeros((8, LANES), F32)], axis=0).astype(BF16)
        for n, out in enumerate((keep_out, send_out)):
            for part in range(2):
                at = n * COLS + part * 32
                out[2 * four + part, COLS : COLS + 32, :] = turned[at : at + 32]
                out[2 * four + part, COLS + 32 :, :] = digits


def over_terms(step, one_chunk):
    full = VOC // step

    def loop(i, carry):
        one_chunk(pl.multiple_of(i * step, step), step)
        return carry

    lax.fori_loop(0, full, loop, 0)
    one_chunk(full * step, VOC - full * step)


def logits_body(
    rows_ref, got_ref, own_ref, other_ref, pooled_ref, out_ref, hidden_ref, embed_ref, spots
):
    here = lax.broadcasted_iota(I32, (SEQ, 1), 0)
    embed_ref[0:COLS, :] = own_ref[...]
    embed_ref[COLS:, :] = other_ref[...]
    load_spots(got_ref, spots)
    for two in range(CHIPS // 2):
        for h in range(2):
            rows = rows_ref[h * 16 : h * 16 + 16, two * 16 : two * 16 + 16, :].astype(F32)
            for s in range(2):
                p = (2 * two + s) * 2 + h
                tokens = rows[:, s * ROWS : (s + 1) * ROWS, :].reshape(SEQ, PAIR)
                hidden_ref[p * SEQ : (p + 1) * SEQ, :] = tokens.astype(BF16)

    def one_chunk(first, width):
        lanes = pl.ds(first, width)
        embed = embed_ref[:, lanes]
        for p in range(OWN):
            scores = jnp.dot(
                hidden_ref[p * SEQ : (p + 1) * SEQ, :], embed, preferred_element_type=F32
            )
            index = jnp.concatenate(
                [spot_row(spots, p, first // LANES + n) for n in range(width // LANES)], axis=1
            )
            picked = jnp.sum(jnp.where(index == here, scores, 0.0), axis=0, keepdims=True)
            for at in range(0, width, CHUNK):
                some = min(CHUNK, width - at)
                out_ref[first // CHUNK + at // CHUNK, p : p + 1, 0:some] = picked[:, at : at + some]
        for at in range(0, width, CHUNK):
            some = min(CHUNK, width - at)
            upstream = pooled_ref[:, pl.ds(first + at, some)]
            out_ref[first // CHUNK + at // CHUNK, OWN : OWN + 2, 0:some] = upstream

    over_terms(1024, one_chunk)
    more = rows_ref[0, 80:96, :].astype(F32)
    for s in range(1, SHARDS):
        more = jnp.maximum(more, rows_ref[s, 80:96, :].astype(F32))
    more = jnp.concatenate([more[15:16], more[15:16]], axis=1)
    tail = jnp.concatenate([more, jnp.zeros((5, CHUNK), F32)], axis=0)
    for g in range(GROUPS):
        out_ref[g, OWN + 2 :, :] = tail
    out_ref[GROUPS - 1, 0 : OWN + 2, LANES:] = jnp.zeros((OWN + 2, CHUNK - LANES), F32)


def slope_body(part_ref, bias_ref, out_ref, more_ref):
    logits = []
    upstream = []
    for c in range(2):
        total = part_ref[c, 0:OWN, :]
        for m in range(1, CHIPS):
            total = total + part_ref[2 * m + c, 0:OWN, :]
        logits.append(total)
        upstream += [part_ref[2 * m + c, OWN : OWN + 2, :] for m in range(CHIPS)]
    logits = jnp.concatenate(logits, axis=0) + bias_ref[...]
    upstream = jnp.concatenate(upstream, axis=0)
    softened = jnp.maximum(logits, 0.0) + jnp.log1p(jnp.exp(-jnp.abs(logits)))
    pooled = jnp.log1p(softened)
    sigmoid = 1.0 / (1.0 + jnp.exp(-logits))
    slope = sigmoid / (1.0 + softened)
    mean_pooled = jnp.sum(pooled, axis=0, keepdims=True) / PASSAGES
    grad = ((upstream + mean_pooled) * slope).astype(BF16)
    more = part_ref[0, OWN : OWN + 8, 0:LANES]
    for g in range(1, GROUPS):
        more = jnp.maximum(more, part_ref[g, OWN : OWN + 8, 0:LANES])
    more_ref[...] = more[2:3]
    for g in range(GROUPS):
        out_ref[g] = grad


def hidden_body(
    place_ref, grad_ref, got_ref, own_ref, other_ref, out_ref, total, left, embed_ref, grads, spots
):
    here = lax.broadcasted_iota(I32, (SEQ, LANES), 0).astype(I16)
    zero = jnp.zeros((), BF16)
    first_core = place_ref[1] == 0
    load_spots(got_ref, spots)
    embed_ref[0:COLS, :] = own_ref[...]
    embed_ref[COLS:, :] = other_ref[...]
    total[...] = jnp.zeros_like(total)

    def one_chunk(first, width):
        for at in range(0, width, CHUNK):
            both = grad_ref[first // CHUNK + at // CHUNK].astype(F32)
            grads[:, at : at + CHUNK] = jnp.where(first_core, both[0:OWN], both[OWN:])
        embed = embed_ref[:, pl.ds(first, width)]
        for group in range(0, OWN, 4):
            for p in range(group, group + 4):
                for tile in range(width // LANES):
                    lanes = slice(tile * LANES, (tile + 1) * LANES)
                    index = spot_row(spots, p, first // LANES + tile)
                    index = jnp.broadcast_to(index, (16, LANES)).astype(I16)
                    value = jnp.broadcast_to(grads[p : p + 1, lanes], (16, LANES)).astype(BF16)
                    index = jnp.concatenate([index] * 8, axis=0)
                    value = jnp.concatenate([value] * 8, axis=0)
                    left[p * SEQ : (p + 1) * SEQ, lanes] = jnp.where(index == here, value, zero)
            rows = slice(group * SEQ, (group + 4) * SEQ)
            total[rows, :] += lax.dot_general(
                left[rows, 0:width], embed, (((1,), (1,)), ((), ())), preferred_element_type=F32
            )

    over_terms(1024, one_chunk)
    out_ref[...] = total[...].astype(BF16)


def rest_body(place_ref, every_ref, swapped_ref, total_ref, out_ref, total):
    base = place_ref[0] * VOC
    low_row = lax.broadcasted_iota(I32, (512, LANES), 0)
    total[...] = jnp.zeros_like(total)
    for n, ref in enumerate((every_ref, swapped_ref)):

        def pair(k, carry, n=n, ref=ref):
            rows = [ref[2 * k + part].astype(F32) for part in range(2)]
            digits = jnp.concatenate([r[64:72, 0:64] for r in rows], axis=1).astype(I32)
            local = (digits[2:3] << 14) + (digits[1:2] << 7) + digits[0:1] - base
            inside = (local >= 0) & (local < VOC)
            high = jnp.where(inside, local >> 9, 15)
            turned = jnp.concatenate([r[0:64] for r in rows], axis=0).T[n * COLS : (n + 1) * COLS]
            left = [jnp.where(high == h, turned, 0.0) for h in range(8)]
            right = jnp.where(low_row == (local & 511), 1.0, 0.0)
            total[...] += lax.dot_general(
                jnp.concatenate(left, axis=0).astype(BF16),
                right.astype(BF16),
                (((1,), (1,)), ((), ())),
                preferred_element_type=F32,
            )
            return carry

        lax.fori_loop(0, SHARDS // 2, pair, 0)
    for h in range(8):
        lanes = slice(h * 512, (h + 1) * 512)
        out_ref[:, lanes] = total_ref[:, lanes] + total[h * COLS : (h + 1) * COLS, :]


def token_body(place_ref, keep_ref, got_ref, out_ref, left, right, total):
    base = place_ref[0] * VOC
    low_row = lax.broadcasted_iota(I32, (512, LANES), 0).astype(I16)
    zero = jnp.zeros((), BF16)
    one = jnp.ones((), BF16)
    total[...] = jnp.zeros_like(total)

    def token_block(table_ref):
        for group in range(8):
            digits = table_ref[2 * group, COLS + 32 :, :].astype(F32).astype(I32)
            local = (digits[2:3] << 14) + (digits[1:2] << 7) + digits[0:1] - base
            inside = (local >= 0) & (local < VOC)
            high = jnp.where(inside, local >> 9, 15)
            high = jnp.broadcast_to(high, (16, LANES)).astype(I16)
            low = jnp.broadcast_to(local & 511, (16, LANES)).astype(I16)
            high = jnp.concatenate([high] * 4, axis=0)
            low = jnp.concatenate([low] * 32, axis=0)
            cotangents = jnp.concatenate(
                [table_ref[2 * group + part, COLS : COLS + 32, :] for part in range(2)], axis=0
            )
            lanes = slice(group * LANES, (group + 1) * LANES)
            for h in range(8):
                left[h * COLS : (h + 1) * COLS, lanes] = jnp.where(
                    high == jnp.int16(h), cotangents, zero
                )
            right[:, lanes] = jnp.where(low_row == low, one, zero)
        total[...] += lax.dot_general(
            left[...], right[...], (((1,), (1,)), ((), ())), preferred_element_type=F32
        )

    for table_ref in (keep_ref, got_ref):
        token_block(table_ref)
    for h in range(8):
        out_ref[:, h * 512 : (h + 1) * 512] = total[h * COLS : (h + 1) * COLS, :]


def embed_body(
    place_ref, token_ref, grad_ref, own_index, other_index, keep_ref, got_ref, out_ref, bias_ref, grads, own_spots, other_spots
):
    first_core = place_ref[1] == 0
    load_spots(own_index, own_spots)
    load_spots(other_index, other_spots)
    for g in range(GROUPS):
        both = grad_ref[g].astype(F32)
        grads[g] = jnp.where(first_core, both, jnp.concatenate([both[OWN:], both[:OWN]], axis=0))

    def one_tile(tile, carry):
        lanes = pl.ds(pl.multiple_of(tile * LANES, LANES), LANES)
        half = pl.ds(pl.multiple_of((tile % 2) * LANES, LANES), LANES)
        totals = [token_ref[d : d + 16, lanes] for d in range(0, COLS, 16)]
        for n, (table_ref, spots) in enumerate(((keep_ref, own_spots), (got_ref, other_spots))):
            for p in range(OWN):
                index = spot_row(spots, p, tile)
                index = jnp.broadcast_to(index, (16, LANES)).astype(I16)
                value = grads[tile // 2, n * OWN + p : n * OWN + p + 1, half]
                for d in range(COLS // 16):
                    picked = lane_gather(table_ref[p, d * 16 : d * 16 + 16, :], index).astype(F32)
                    totals[d] = totals[d] + picked * value
        for d in range(COLS // 16):
            out_ref[d * 16 : d * 16 + 16, lanes] = totals[d]
        bias_ref[:, lanes] = jnp.sum(grads[tile // 2, :, half], axis=0, keepdims=True)
        return carry

    lax.fori_loop(0, TILES, one_tile, 0)


def sum_body(place_ref, part_ref, out_ref):
    swap = place_ref[1] == 1
    for m in range(CHIPS):
        total = part_ref[m * SHARDS].astype(F32)
        for s in range(1, SHARDS):
            total = total + part_ref[m * SHARDS + s].astype(F32)
        other = jnp.concatenate([total[:, COLS:], total[:, :COLS]], axis=1)
        out_ref[:, m * PAIR : (m + 1) * PAIR] = jnp.where(swap, other, total).astype(BF16)


def call(body, name, out, scratch=(), specs=None, us=1, out_specs=None, room=24):
    extra = {} if out_specs is None else {"out_specs": out_specs}
    return pl.pallas_call(
        body,
        out_shape=out,
        in_specs=specs,
        scratch_shapes=scratch,
        compiler_params=pltpu.CompilerParams(vmem_limit_bytes=room * 1024 * 1024),
        cost_estimate=pl.CostEstimate(flops=0, bytes_accessed=3_700_000 * us, transcendentals=0),
        name=name,
        **extra,
    )


def shape(dims, dtype):
    return jax.ShapeDtypeStruct(dims, dtype)


def exchange(x, axis):
    return lax.all_to_all(x, axis, split_axis=0, concat_axis=0, tiled=True)


def swap_over(x, axis):
    return lax.ppermute(x, axis, [(0, 1), (1, 0)])


def add_rest(total, rest):
    ring = [(k, (k + 1) % SHARDS) for k in range(SHARDS)]

    def step(k, carry):
        held, every = carry
        held = lax.ppermute(held, SHARD, ring)
        return held, lax.dynamic_update_index_in_dim(every, held, k, 0)

    every = jnp.zeros((SHARDS,) + rest.shape, BF16).at[0].set(rest)
    every = lax.fori_loop(1, SHARDS, step, (rest, every))[1]
    place = jnp.stack([lax.axis_index(SHARD)]).astype(I32)
    return call(
        rest_body,
        "rest",
        shape(total.shape, F32),
        [pltpu.VMEM((512, 512), F32)],
        [SMEM, VMEM, VMEM, VMEM],
    )(place, every, swap_over(every, "core"), total)


def on_device(
    hidden, embed_grad, token_ids, lengths, pool_index, embedding, head_bias, pooled_grad
):
    place = jnp.stack([lax.axis_index(name) for name in (SHARD, "core", "zl", "x")]).astype(I32)
    packed = call(
        pack_body,
        "pack",
        shape((CHIPS, IDS + 80, LANES), BF16),
        [
            pltpu.SMEM((2,), I32),
            pltpu.SMEM((ROWS,), I32),
            pltpu.VMEM((ROWS, WIDTH), BF16),
            pltpu.VMEM((ROWS, WIDTH), BF16),
            pltpu.VMEM((2, VOC), I32),
            pltpu.VMEM((64, LANES), F32),
            pltpu.SemaphoreType.DMA((5,)),
        ],
        [ANY] * 5,
        room=56,
    )(lengths, token_ids, hidden, embed_grad, pool_index)
    own_index = exchange(packed, ("zl", "x"))
    rows, rest = call(
        spread_body,
        "spread",
        (shape((SHARDS, 96, LANES), BF16), shape((80, LANES), BF16)),
        specs=[VMEM],
        room=8,
    )(own_index)
    all_rows = exchange(rows, SHARD)
    other_embed = swap_over(embedding, "core")
    partial = call(
        logits_body,
        "logits",
        shape((GROUPS, 24, CHUNK), F32),
        [
            pltpu.VMEM((OWN * SEQ, PAIR), BF16),
            pltpu.VMEM((PAIR, VOC), BF16),
            pltpu.VMEM((CHIPS, 64, LANES), I32),
        ],
        [VMEM] * 5,
        us=6,
    )(all_rows, own_index, embedding, other_embed, pooled_grad)
    keep, send = call(
        turn_body,
        "turn",
        (shape((OWN, COLS + 48, SEQ), BF16),) * 2,
        specs=[VMEM],
        us=3,
    )(all_rows)
    got = swap_over(send, "core")
    other_index = swap_over(own_index, "core")
    parts = exchange(partial, GROUP)
    bias = jnp.pad(head_bias, (0, GROUPS * CHUNK - VOC)).reshape(GROUPS, 1, CHUNK)
    bias = lax.dynamic_index_in_dim(bias, lax.axis_index(GROUP), 0, keepdims=False)
    grad_block, more = call(
        slope_body,
        "slope",
        (shape((GROUPS, PASSAGES, CHUNK), BF16), shape((1, LANES), F32)),
        specs=[VMEM, VMEM],
        room=8,
    )(parts, bias)
    all_grad = exchange(grad_block, GROUP)
    token_grad = call(
        token_body,
        "token_grad",
        shape((COLS, 4096), F32),
        [
            pltpu.VMEM((512, 1024), BF16),
            pltpu.VMEM((512, 1024), BF16),
            pltpu.VMEM((512, 512), F32),
        ],
        [SMEM, VMEM, VMEM],
        us=5,
        room=24,
    )(place, keep, got)
    all_grad, token_grad, other_index = lax.optimization_barrier((all_grad, token_grad, other_index))
    hidden_parts = call(
        hidden_body,
        "hidden_grad",
        shape((OWN * SEQ, PAIR), BF16),
        [
            pltpu.VMEM((OWN * SEQ, PAIR), F32),
            pltpu.VMEM((OWN * SEQ, 1024), BF16),
            pltpu.VMEM((PAIR, VOC), BF16),
            pltpu.VMEM((OWN, 1024), F32),
            pltpu.VMEM((CHIPS, 64, LANES), I32),
        ],
        [SMEM] + [VMEM] * 4,
        us=6,
    )(place, all_grad, own_index, embedding, other_embed)
    token_grad = lax.cond(more[0, 0] > 0.0, add_rest, lambda total, rest: total, token_grad, rest)
    hidden_got = exchange(hidden_parts.reshape(CHIPS * SHARDS, ROWS, PAIR), HOME)
    embedding_grad, bias_grad = call(
        embed_body,
        "embedding_grad",
        (shape((COLS, VOC), F32), shape((1, VOC), F32)),
        [
            pltpu.VMEM((GROUPS, PASSAGES, CHUNK), F32),
            pltpu.VMEM((CHIPS, 64, LANES), I32),
            pltpu.VMEM((CHIPS, 64, LANES), I32),
        ],
        [SMEM] + [VMEM] * 6,
        us=11,
        room=24,
    )(place, token_grad, all_grad, own_index, other_index, keep, got)
    hidden_grad = call(
        sum_body, "sum_shards", shape((ROWS, WIDTH), BF16), specs=[SMEM, VMEM], room=8
    )(place, hidden_got)
    return hidden_grad, embedding_grad, bias_grad.reshape(VOC)


def solution(mesh):
    fine = Mesh(mesh.devices.reshape(2, 4, 2, 4, 8), GROUP + SHARD)
    every = P(GROUP + SHARD, None)
    split = P(GROUP, SHARD)
    return jax.shard_map(
        on_device,
        mesh=fine,
        in_specs=(every, every, P(GROUP + SHARD), P(GROUP), split, split, P(SHARD), split),
        out_specs=(every, split, P(SHARD)),
        check_vma=False,
    )
```

```python
import jax
import jax.numpy as jnp
from jax import lax
from jax.experimental import pallas as pl
from jax.experimental.pallas import tpu as pltpu
from jax.sharding import Mesh, PartitionSpec as P

F32 = jnp.float32
BF16 = jnp.bfloat16
I16 = jnp.int16
I32 = jnp.int32
LANES = 128
SMEM = pl.BlockSpec(memory_space=pltpu.SMEM)
VMEM = pl.BlockSpec(memory_space=pltpu.VMEM)
ANY = pl.BlockSpec(memory_space=pl.ANY)

GROUP = ("zl", "x", "core")
SHARD = ("zh", "y")
HOME = ("zl", "x", "zh", "y")
GROUPS = 16
SHARDS = 32
CHIPS = 8
SEQ = 128
PASSAGES = 32
OWN = 16
COLS = 64
PAIR = 128
WIDTH = 8 * PAIR
ROWS = 8
TILES = 31
VOC = TILES * LANES
CHUNK = 256
IDS = 16
SLOTS = 24


def lane_gather(table, index):
    numbers = lax.GatherDimensionNumbers(
        offset_dims=(),
        collapsed_slice_dims=(1,),
        start_index_map=(1,),
        operand_batching_dims=(0,),
        start_indices_batching_dims=(0,),
    )
    return lax.gather(
        table,
        index[..., None],
        numbers,
        (1, 1),
        mode=lax.GatherScatterMode.PROMISE_IN_BOUNDS,
    )


def load_spots(got_ref, spots):
    for m in range(CHIPS):
        spots[m] = got_ref[m, IDS + 16 :, :].astype(F32).astype(I32)


def spot_row(spots, p, tile):
    return spots[p // 2, pl.ds(2 * tile + p % 2, 1), :]


def pack_body(lengths, ids, hidden, grad, index, out_ref, *scratch):
    held, spots, sem = scratch[:5], scratch[5], scratch[6]
    copies = [
        pltpu.make_async_copy(source, target, sem.at[n])
        for n, (source, target) in enumerate(zip((lengths, ids, hidden, grad, index), held))
    ]
    for copy in copies:
        copy.start()
    for copy in copies:
        copy.wait()
    lengths_ref, ids_ref, hidden_ref, grad_ref, index_ref = held
    place = lax.axis_index(SHARD)
    swap = lax.axis_index("core") == 1
    limit = lengths_ref[place // (SEQ // ROWS)]
    spot = (place % (SEQ // ROWS)) * ROWS + lax.broadcasted_iota(I32, (ROWS, 1), 0)
    arrays = [hidden_ref[...].astype(F32), jnp.where(spot < limit, grad_ref[...].astype(F32), 0.0)]
    row = lax.broadcasted_iota(I32, (16, LANES), 0)
    lane = lax.broadcasted_iota(I32, (16, LANES), 1)
    digits = jnp.zeros((16, LANES), I32)
    for r in range(ROWS):
        digits = jnp.where(row == r, ids_ref[r], digits)
    digits = jnp.where(lane == 0, digits & 127, jnp.where(lane == 1, (digits >> 7) & 127, digits >> 14))
    digits = jnp.where(lane < 3, digits, 0).astype(F32).astype(BF16)
    spots[...] = jnp.zeros_like(spots)
    for tile in range(TILES):
        spots[2 * tile : 2 * tile + 2, :] = index_ref[:, tile * LANES : (tile + 1) * LANES].astype(F32)
    positions = spots[...].astype(BF16)
    for m in range(CHIPS):
        parts = []
        for array in arrays:
            pair = array[:, m * PAIR : (m + 1) * PAIR]
            other = jnp.concatenate([pair[:, COLS:], pair[:, :COLS]], axis=1)
            parts.append(jnp.where(swap, other, pair))
        out_ref[m, 0:IDS, :] = jnp.concatenate(parts, axis=0).astype(BF16)
        out_ref[m, IDS : IDS + 16, :] = digits
        out_ref[m, IDS + 16 :, :] = positions


def spread_body(got_ref, out_ref, rest_ref):
    tokens = 64
    hidden = []
    cotangents = []
    digits = []
    for m in range(CHIPS):
        rows = got_ref[m, 0:IDS, :].astype(F32)
        hidden.append(rows[0:ROWS])
        cotangents.append(rows[ROWS:])
        digits.append(got_ref[m, IDS : IDS + 16, :].astype(F32)[0:ROWS])
    hidden = jnp.concatenate(hidden, axis=0).astype(BF16)
    blank = jnp.zeros((LANES - tokens, LANES), F32)
    cotangents = jnp.concatenate(cotangents + [blank], axis=0)
    digits = jnp.concatenate(digits + [blank], axis=0)
    across = digits.T[0:16]

    def owner(ids):
        return ((ids + 0.5) * (1.0 / VOC)).astype(I32)

    lane = lax.broadcasted_iota(I32, (LANES, LANES), 1)
    row = lax.broadcasted_iota(I32, (LANES, LANES), 0)
    across_owner = owner(across[0:1] + 128.0 * across[1:2] + 16384.0 * across[2:3])
    across_owner = jnp.where(lane[0:1] < tokens, across_owner, SHARDS)
    down_owner = owner(digits[:, 0:1] + 128.0 * digits[:, 1:2] + 16384.0 * digits[:, 2:3])
    down_owner = jnp.where(row < tokens, down_owner, SHARDS + 1)
    same = down_owner == across_owner
    across_rank = jnp.sum(jnp.where(same & (row < lane), 1.0, 0.0), axis=0, keepdims=True).astype(I32)
    down_rank = jnp.sum(jnp.where(same & (lane < row), 1.0, 0.0), axis=1, keepdims=True).astype(I32)
    more = jnp.max(jnp.where(lane[0:1] < tokens, across_rank, 0), axis=1, keepdims=True) >= SLOTS
    rest = jnp.where(down_rank >= SLOTS, cotangents, 0.0)[0:tokens]
    rest_ref[...] = jnp.concatenate([rest, across], axis=0).astype(BF16)
    flag = jnp.where(more, 1.0, 0.0) + jnp.zeros((1, LANES), F32)
    packed = cotangents.astype(BF16)
    across = across.astype(BF16)
    slot = lax.broadcasted_iota(I32, (32, 1), 0)
    slot = jnp.where(slot < SLOTS, slot, -1)
    for s in range(SHARDS):
        place = jnp.where((across_owner == s) & (across_rank == slot), 1.0, 0.0).astype(BF16)
        rows = jnp.dot(place, packed, preferred_element_type=F32)
        codes = lax.dot_general(
            across, place, (((1,), (1,)), ((), ())), preferred_element_type=F32
        )
        codes = jnp.concatenate([codes[0:7], jnp.zeros((7, LANES - 32), F32)], axis=1)
        out_ref[s, 0:64, :] = hidden
        out_ref[s, 64:96, :] = jnp.concatenate([rows[0:SLOTS], codes, flag], axis=0).astype(BF16)


def turn_body(rows_ref, keep_out, send_out):
    for two in range(CHIPS // 2):
        for h in range(2):
            rows = rows_ref[h * 16 : h * 16 + 16, two * 16 : two * 16 + 16, :].astype(F32)
            for s in range(2):
                p = (2 * two + s) * 2 + h
                turned = rows[:, s * ROWS : (s + 1) * ROWS, :].reshape(SEQ, PAIR).T.astype(BF16)
                keep_out[p, 0:COLS, :] = turned[:COLS]
                send_out[p, 0:COLS, :] = turned[COLS:]
    keep = lax.broadcasted_iota(I32, (32, 1), 0) < SLOTS
    for four in range(SHARDS // 4):
        rows = [rows_ref[4 * four + s, 64:96, :].astype(F32) for s in range(4)]
        turned = jnp.concatenate([jnp.where(keep, r, 0.0) for r in rows], axis=0).T.astype(BF16)
        digits = jnp.concatenate([r[24:32, 0:32] for r in rows], axis=1)
        digits = jnp.concatenate([digits, jnp.zeros((8, LANES), F32)], axis=0).astype(BF16)
        for n, out in enumerate((keep_out, send_out)):
            for part in range(2):
                at = n * COLS + part * 32
                out[2 * four + part, COLS : COLS + 32, :] = turned[at : at + 32]
                out[2 * four + part, COLS + 32 :, :] = digits


def over_terms(step, one_chunk):
    full = VOC // step

    def loop(i, carry):
        one_chunk(pl.multiple_of(i * step, step), step)
        return carry

    lax.fori_loop(0, full, loop, 0)
    one_chunk(full * step, VOC - full * step)


def logits_body(
    rows_ref, got_ref, own_ref, other_ref, pooled_ref, out_ref, hidden_ref, embed_ref, spots
):
    here = lax.broadcasted_iota(I32, (8, 1), 0)
    embed_ref[0:COLS, :] = own_ref[...]
    embed_ref[COLS:, :] = other_ref[...]
    load_spots(got_ref, spots)
    for two in range(CHIPS // 2):
        for h in range(2):
            rows = rows_ref[h * 16 : h * 16 + 16, two * 16 : two * 16 + 16, :].astype(F32)
            for s in range(2):
                p = (2 * two + s) * 2 + h
                tokens = rows[:, s * ROWS : (s + 1) * ROWS, :].reshape(SEQ, PAIR)
                hidden_ref[p * SEQ : (p + 1) * SEQ, :] = tokens.astype(BF16)

    def one_chunk(first, width):
        lanes = pl.ds(first, width)
        embed = embed_ref[:, lanes]
        for p in range(OWN):
            scores = jnp.dot(
                hidden_ref[p * SEQ : (p + 1) * SEQ, :], embed, preferred_element_type=F32
            )
            index = jnp.concatenate(
                [spot_row(spots, p, first // LANES + n) for n in range(width // LANES)], axis=1
            )
            high = jnp.broadcast_to(index >> 3, (8, width))
            rows = scores[0:8]
            for n in range(1, SEQ // 8):
                rows = jnp.where(high == n, scores[8 * n : 8 * n + 8], rows)
            picked = jnp.sum(jnp.where((index & 7) == here, rows, 0.0), axis=0, keepdims=True)
            for at in range(0, width, CHUNK):
                some = min(CHUNK, width - at)
                out_ref[first // CHUNK + at // CHUNK, p : p + 1, 0:some] = picked[:, at : at + some]
        for at in range(0, width, CHUNK):
            some = min(CHUNK, width - at)
            upstream = pooled_ref[:, pl.ds(first + at, some)]
            out_ref[first // CHUNK + at // CHUNK, OWN : OWN + 2, 0:some] = upstream

    over_terms(2048, one_chunk)
    more = rows_ref[0, 80:96, :].astype(F32)
    for s in range(1, SHARDS):
        more = jnp.maximum(more, rows_ref[s, 80:96, :].astype(F32))
    more = jnp.concatenate([more[15:16], more[15:16]], axis=1)
    tail = jnp.concatenate([more, jnp.zeros((5, CHUNK), F32)], axis=0)
    for g in range(GROUPS):
        out_ref[g, OWN + 2 :, :] = tail
    out_ref[GROUPS - 1, 0 : OWN + 2, LANES:] = jnp.zeros((OWN + 2, CHUNK - LANES), F32)


def slope_body(part_ref, bias_ref, out_ref, more_ref):
    logits = []
    upstream = []
    for c in range(2):
        total = part_ref[c, 0:OWN, :]
        for m in range(1, CHIPS):
            total = total + part_ref[2 * m + c, 0:OWN, :]
        logits.append(total)
        upstream += [part_ref[2 * m + c, OWN : OWN + 2, :] for m in range(CHIPS)]
    logits = jnp.concatenate(logits, axis=0) + bias_ref[...]
    upstream = jnp.concatenate(upstream, axis=0)
    softened = jnp.maximum(logits, 0.0) + jnp.log1p(jnp.exp(-jnp.abs(logits)))
    pooled = jnp.log1p(softened)
    sigmoid = 1.0 / (1.0 + jnp.exp(-logits))
    slope = sigmoid / (1.0 + softened)
    mean_pooled = jnp.sum(pooled, axis=0, keepdims=True) / PASSAGES
    grad = ((upstream + mean_pooled) * slope).astype(BF16)
    more = part_ref[0, OWN : OWN + 8, 0:LANES]
    for g in range(1, GROUPS):
        more = jnp.maximum(more, part_ref[g, OWN : OWN + 8, 0:LANES])
    more_ref[...] = more[2:3]
    for g in range(GROUPS):
        out_ref[g] = grad[g % 2 * OWN : g % 2 * OWN + OWN]


def hidden_body(
    grad_ref, got_ref, own_ref, other_ref, out_ref, total, left, embed_ref, grads, spots
):
    here = lax.broadcasted_iota(I32, (SEQ, LANES), 0).astype(I16)
    zero = jnp.zeros((), BF16)
    load_spots(got_ref, spots)
    embed_ref[0:COLS, :] = own_ref[...]
    embed_ref[COLS:, :] = other_ref[...]
    total[...] = jnp.zeros_like(total)

    def one_chunk(first, width):
        for at in range(0, width, CHUNK):
            grads[:, at : at + CHUNK] = grad_ref[first // CHUNK + at // CHUNK].astype(F32)
        embed = embed_ref[:, pl.ds(first, width)]
        for group in range(0, OWN, 4):
            for p in range(group, group + 4):
                for tile in range(width // LANES):
                    lanes = slice(tile * LANES, (tile + 1) * LANES)
                    index = spot_row(spots, p, first // LANES + tile)
                    index = jnp.broadcast_to(index, (16, LANES)).astype(I16)
                    value = jnp.broadcast_to(grads[p : p + 1, lanes], (16, LANES)).astype(BF16)
                    index = jnp.concatenate([index] * 8, axis=0)
                    value = jnp.concatenate([value] * 8, axis=0)
                    left[p * SEQ : (p + 1) * SEQ, lanes] = jnp.where(index == here, value, zero)
            rows = slice(group * SEQ, (group + 4) * SEQ)
            total[rows, :] += lax.dot_general(
                left[rows, 0:width], embed, (((1,), (1,)), ((), ())), preferred_element_type=F32
            )

    over_terms(1024, one_chunk)
    out_ref[...] = total[...].astype(BF16)


def rest_body(place_ref, every_ref, swapped_ref, total_ref, out_ref, total):
    base = place_ref[0] * VOC
    low_row = lax.broadcasted_iota(I32, (512, LANES), 0)
    total[...] = jnp.zeros_like(total)
    for n, ref in enumerate((every_ref, swapped_ref)):

        def pair(k, carry, n=n, ref=ref):
            rows = [ref[2 * k + part].astype(F32) for part in range(2)]
            digits = jnp.concatenate([r[64:72, 0:64] for r in rows], axis=1).astype(I32)
            local = (digits[2:3] << 14) + (digits[1:2] << 7) + digits[0:1] - base
            inside = (local >= 0) & (local < VOC)
            high = jnp.where(inside, local >> 9, 15)
            turned = jnp.concatenate([r[0:64] for r in rows], axis=0).T[n * COLS : (n + 1) * COLS]
            left = [jnp.where(high == h, turned, 0.0) for h in range(8)]
            right = jnp.where(low_row == (local & 511), 1.0, 0.0)
            total[...] += lax.dot_general(
                jnp.concatenate(left, axis=0).astype(BF16),
                right.astype(BF16),
                (((1,), (1,)), ((), ())),
                preferred_element_type=F32,
            )
            return carry

        lax.fori_loop(0, SHARDS // 2, pair, 0)
    for h in range(8):
        lanes = slice(h * 512, (h + 1) * 512)
        out_ref[:, lanes] = total_ref[:, lanes] + total[h * COLS : (h + 1) * COLS, :]


def token_body(place_ref, keep_ref, got_ref, out_ref, left, right, total):
    base = place_ref[0] * VOC
    low_row = lax.broadcasted_iota(I32, (512, LANES), 0).astype(I16)
    zero = jnp.zeros((), BF16)
    one = jnp.ones((), BF16)
    total[...] = jnp.zeros_like(total)

    def token_block(table_ref):
        for group in range(8):
            digits = table_ref[2 * group, COLS + 32 :, :].astype(F32).astype(I32)
            local = (digits[2:3] << 14) + (digits[1:2] << 7) + digits[0:1] - base
            inside = (local >= 0) & (local < VOC)
            high = jnp.where(inside, local >> 9, 15)
            high = jnp.broadcast_to(high, (16, LANES)).astype(I16)
            low = jnp.broadcast_to(local & 511, (16, LANES)).astype(I16)
            high = jnp.concatenate([high] * 4, axis=0)
            low = jnp.concatenate([low] * 32, axis=0)
            cotangents = jnp.concatenate(
                [table_ref[2 * group + part, COLS : COLS + 32, :] for part in range(2)], axis=0
            )
            lanes = slice(group * LANES, (group + 1) * LANES)
            for h in range(8):
                left[h * COLS : (h + 1) * COLS, lanes] = jnp.where(
                    high == jnp.int16(h), cotangents, zero
                )
            right[:, lanes] = jnp.where(low_row == low, one, zero)
        total[...] += lax.dot_general(
            left[...], right[...], (((1,), (1,)), ((), ())), preferred_element_type=F32
        )

    for table_ref in (keep_ref, got_ref):
        token_block(table_ref)
    for h in range(8):
        out_ref[:, h * 512 : (h + 1) * 512] = total[h * COLS : (h + 1) * COLS, :]


def embed_body(
    token_ref, own_grad, other_grad, own_index, other_index, keep_ref, got_ref, out_ref, bias_ref, grads, own_spots, other_spots
):
    load_spots(own_index, own_spots)
    load_spots(other_index, other_spots)
    for g in range(GROUPS):
        grads[g, 0:OWN, :] = own_grad[g].astype(F32)
        grads[g, OWN:, :] = other_grad[g].astype(F32)

    def one_tile(tile, carry):
        lanes = pl.ds(pl.multiple_of(tile * LANES, LANES), LANES)
        half = pl.ds(pl.multiple_of((tile % 2) * LANES, LANES), LANES)
        totals = [token_ref[d : d + 16, lanes] for d in range(0, COLS, 16)]
        for n, (table_ref, spots) in enumerate(((keep_ref, own_spots), (got_ref, other_spots))):
            for p in range(OWN):
                index = spot_row(spots, p, tile)
                index = jnp.broadcast_to(index, (16, LANES)).astype(I16)
                value = grads[tile // 2, n * OWN + p : n * OWN + p + 1, half]
                for d in range(COLS // 16):
                    picked = lane_gather(table_ref[p, d * 16 : d * 16 + 16, :], index).astype(F32)
                    totals[d] = totals[d] + picked * value
        for d in range(COLS // 16):
            out_ref[d * 16 : d * 16 + 16, lanes] = totals[d]
        bias_ref[:, lanes] = jnp.sum(grads[tile // 2, :, half], axis=0, keepdims=True)
        return carry

    lax.fori_loop(0, TILES, one_tile, 0)


def sum_body(place_ref, part_ref, out_ref):
    swap = place_ref[1] == 1
    for m in range(CHIPS):
        total = part_ref[m * SHARDS].astype(F32)
        for s in range(1, SHARDS):
            total = total + part_ref[m * SHARDS + s].astype(F32)
        other = jnp.concatenate([total[:, COLS:], total[:, :COLS]], axis=1)
        out_ref[:, m * PAIR : (m + 1) * PAIR] = jnp.where(swap, other, total).astype(BF16)


def call(body, name, out, scratch=(), specs=None, us=1, out_specs=None, room=24):
    extra = {} if out_specs is None else {"out_specs": out_specs}
    return pl.pallas_call(
        body,
        out_shape=out,
        in_specs=specs,
        scratch_shapes=scratch,
        compiler_params=pltpu.CompilerParams(vmem_limit_bytes=room * 1024 * 1024),
        cost_estimate=pl.CostEstimate(flops=0, bytes_accessed=3_700_000 * us, transcendentals=0),
        name=name,
        **extra,
    )


def shape(dims, dtype):
    return jax.ShapeDtypeStruct(dims, dtype)


def exchange(x, axis):
    return lax.all_to_all(x, axis, split_axis=0, concat_axis=0, tiled=True)


def swap_over(x, axis):
    return lax.ppermute(x, axis, [(0, 1), (1, 0)])


def add_rest(total, rest):
    ring = [(k, (k + 1) % SHARDS) for k in range(SHARDS)]

    def step(k, carry):
        held, every = carry
        held = lax.ppermute(held, SHARD, ring)
        return held, lax.dynamic_update_index_in_dim(every, held, k, 0)

    every = jnp.zeros((SHARDS,) + rest.shape, BF16).at[0].set(rest)
    every = lax.fori_loop(1, SHARDS, step, (rest, every))[1]
    place = jnp.stack([lax.axis_index(SHARD)]).astype(I32)
    return call(
        rest_body,
        "rest",
        shape(total.shape, F32),
        [pltpu.VMEM((512, 512), F32)],
        [SMEM, VMEM, VMEM, VMEM],
    )(place, every, swap_over(every, "core"), total)


def on_device(
    hidden, embed_grad, token_ids, lengths, pool_index, embedding, head_bias, pooled_grad
):
    place = jnp.stack([lax.axis_index(name) for name in (SHARD, "core", "zl", "x")]).astype(I32)
    packed = call(
        pack_body,
        "pack",
        shape((CHIPS, IDS + 80, LANES), BF16),
        [
            pltpu.SMEM((2,), I32),
            pltpu.SMEM((ROWS,), I32),
            pltpu.VMEM((ROWS, WIDTH), BF16),
            pltpu.VMEM((ROWS, WIDTH), BF16),
            pltpu.VMEM((2, VOC), I32),
            pltpu.VMEM((64, LANES), F32),
            pltpu.SemaphoreType.DMA((5,)),
        ],
        [ANY] * 5,
        room=56,
    )(lengths, token_ids, hidden, embed_grad, pool_index)
    own_index = exchange(packed, ("zl", "x"))
    rows, rest = call(
        spread_body,
        "spread",
        (shape((SHARDS, 96, LANES), BF16), shape((80, LANES), BF16)),
        specs=[VMEM],
        room=8,
    )(own_index)
    all_rows = exchange(rows, SHARD)
    other_embed = swap_over(embedding, "core")
    partial = call(
        logits_body,
        "logits",
        shape((GROUPS, 24, CHUNK), F32),
        [
            pltpu.VMEM((OWN * SEQ, PAIR), BF16),
            pltpu.VMEM((PAIR, VOC), BF16),
            pltpu.VMEM((CHIPS, 64, LANES), I32),
        ],
        [VMEM] * 5,
        us=6,
    )(all_rows, own_index, embedding, other_embed, pooled_grad)
    keep, send = call(
        turn_body,
        "turn",
        (shape((OWN, COLS + 48, SEQ), BF16),) * 2,
        specs=[VMEM],
        us=3,
    )(all_rows)
    got = swap_over(send, "core")
    other_index = swap_over(own_index, "core")
    parts = exchange(partial, GROUP)
    parts, keep = lax.optimization_barrier((parts, keep))
    bias = jnp.pad(head_bias, (0, GROUPS * CHUNK - VOC)).reshape(GROUPS, 1, CHUNK)
    bias = lax.dynamic_index_in_dim(bias, lax.axis_index(GROUP), 0, keepdims=False)
    grad_block, more = call(
        slope_body,
        "slope",
        (shape((GROUPS, OWN, CHUNK), BF16), shape((1, LANES), F32)),
        specs=[VMEM, VMEM],
        room=8,
    )(parts, bias)
    all_grad = exchange(grad_block, GROUP)
    token_grad = call(
        token_body,
        "token_grad",
        shape((COLS, 4096), F32),
        [
            pltpu.VMEM((512, 1024), BF16),
            pltpu.VMEM((512, 1024), BF16),
            pltpu.VMEM((512, 512), F32),
        ],
        [SMEM, VMEM, VMEM],
        us=5,
        room=24,
    )(place, keep, got)
    all_grad, token_grad, other_index = lax.optimization_barrier((all_grad, token_grad, other_index))
    hidden_parts = call(
        hidden_body,
        "hidden_grad",
        shape((OWN * SEQ, PAIR), BF16),
        [
            pltpu.VMEM((OWN * SEQ, PAIR), F32),
            pltpu.VMEM((OWN * SEQ, 1024), BF16),
            pltpu.VMEM((PAIR, VOC), BF16),
            pltpu.VMEM((OWN, 1024), F32),
            pltpu.VMEM((CHIPS, 64, LANES), I32),
        ],
        [VMEM] * 4,
        us=6,
    )(all_grad, own_index, embedding, other_embed)
    token_grad = lax.cond(more[0, 0] > 0.0, add_rest, lambda total, rest: total, token_grad, rest)
    hidden_got = exchange(hidden_parts.reshape(CHIPS * SHARDS, ROWS, PAIR), HOME)
    other_grad = swap_over(all_grad, "core")
    embedding_grad, bias_grad = call(
        embed_body,
        "embedding_grad",
        (shape((COLS, VOC), F32), shape((1, VOC), F32)),
        [
            pltpu.VMEM((GROUPS, PASSAGES, CHUNK), F32),
            pltpu.VMEM((CHIPS, 64, LANES), I32),
            pltpu.VMEM((CHIPS, 64, LANES), I32),
        ],
        [VMEM] * 7,
        us=11,
        room=24,
    )(token_grad, all_grad, other_grad, own_index, other_index, keep, got)
    hidden_grad = call(
        sum_body, "sum_shards", shape((ROWS, WIDTH), BF16), specs=[SMEM, VMEM], room=8
    )(place, hidden_got)
    return hidden_grad, embedding_grad, bias_grad.reshape(VOC)


def solution(mesh):
    fine = Mesh(mesh.devices.reshape(2, 4, 2, 4, 8), GROUP + SHARD)
    every = P(GROUP + SHARD, None)
    split = P(GROUP, SHARD)
    return jax.shard_map(
        on_device,
        mesh=fine,
        in_specs=(every, every, P(GROUP + SHARD), P(GROUP), split, split, P(SHARD), split),
        out_specs=(every, split, P(SHARD)),
        check_vma=False,
    )
```

```python
import jax
import jax.numpy as jnp
from jax import lax
from jax.experimental import pallas as pl
from jax.experimental.pallas import tpu as pltpu
from jax.sharding import Mesh, PartitionSpec as P

F32 = jnp.float32
BF16 = jnp.bfloat16
I16 = jnp.int16
I32 = jnp.int32
LANES = 128
SMEM = pl.BlockSpec(memory_space=pltpu.SMEM)
VMEM = pl.BlockSpec(memory_space=pltpu.VMEM)
ANY = pl.BlockSpec(memory_space=pl.ANY)

GROUP = ("zl", "x", "core")
SHARD = ("zh", "y")
PLANES = ("x", "zh", "y")
GROUPS = 16
SHARDS = 32
CHIPS = 8
SEQ = 128
PASSAGES = 32
OWN = 16
COLS = 64
PAIR = 128
WIDTH = 8 * PAIR
ROWS = 8
TILES = 31
VOC = TILES * LANES
CHUNK = 256
IDS = 16
SLOTS = 24


def lane_gather(table, index):
    numbers = lax.GatherDimensionNumbers(
        offset_dims=(),
        collapsed_slice_dims=(1,),
        start_index_map=(1,),
        operand_batching_dims=(0,),
        start_indices_batching_dims=(0,),
    )
    return lax.gather(
        table,
        index[..., None],
        numbers,
        (1, 1),
        mode=lax.GatherScatterMode.PROMISE_IN_BOUNDS,
    )


def load_spots(got_ref, spots):
    for m in range(CHIPS):
        spots[m] = got_ref[m, IDS + 16 :, :].astype(F32).astype(I32)


def spot_row(spots, p, tile):
    return spots[p // 2, pl.ds(2 * tile + p % 2, 1), :]


def pack_body(lengths, ids, hidden, grad, index, out_ref, *scratch):
    held, spots, sem = scratch[:5], scratch[5], scratch[6]
    copies = [
        pltpu.make_async_copy(source, target, sem.at[n])
        for n, (source, target) in enumerate(zip((lengths, ids, hidden, grad, index), held))
    ]
    for copy in copies:
        copy.start()
    for copy in copies:
        copy.wait()
    lengths_ref, ids_ref, hidden_ref, grad_ref, index_ref = held
    place = lax.axis_index(SHARD)
    swap = lax.axis_index("core") == 1
    limit = lengths_ref[place // (SEQ // ROWS)]
    spot = (place % (SEQ // ROWS)) * ROWS + lax.broadcasted_iota(I32, (ROWS, 1), 0)
    arrays = [hidden_ref[...].astype(F32), jnp.where(spot < limit, grad_ref[...].astype(F32), 0.0)]
    row = lax.broadcasted_iota(I32, (16, LANES), 0)
    lane = lax.broadcasted_iota(I32, (16, LANES), 1)
    digits = jnp.zeros((16, LANES), I32)
    for r in range(ROWS):
        digits = jnp.where(row == r, ids_ref[r], digits)
    digits = jnp.where(lane == 0, digits & 127, jnp.where(lane == 1, (digits >> 7) & 127, digits >> 14))
    digits = jnp.where(lane < 3, digits, 0).astype(F32).astype(BF16)
    spots[...] = jnp.zeros_like(spots)
    for tile in range(TILES):
        spots[2 * tile : 2 * tile + 2, :] = index_ref[:, tile * LANES : (tile + 1) * LANES].astype(F32)
    positions = spots[...].astype(BF16)
    for m in range(CHIPS):
        parts = []
        for array in arrays:
            pair = array[:, m * PAIR : (m + 1) * PAIR]
            other = jnp.concatenate([pair[:, COLS:], pair[:, :COLS]], axis=1)
            parts.append(jnp.where(swap, other, pair))
        out_ref[m, 0:IDS, :] = jnp.concatenate(parts, axis=0).astype(BF16)
        out_ref[m, IDS : IDS + 16, :] = digits
        out_ref[m, IDS + 16 :, :] = positions


def spread_body(got_ref, out_ref, rest_ref):
    tokens = 64
    hidden = []
    cotangents = []
    digits = []
    for m in range(CHIPS):
        rows = got_ref[m, 0:IDS, :].astype(F32)
        hidden.append(rows[0:ROWS])
        cotangents.append(rows[ROWS:])
        digits.append(got_ref[m, IDS : IDS + 16, :].astype(F32)[0:ROWS])
    hidden = jnp.concatenate(hidden, axis=0).astype(BF16)
    blank = jnp.zeros((LANES - tokens, LANES), F32)
    cotangents = jnp.concatenate(cotangents + [blank], axis=0)
    digits = jnp.concatenate(digits + [blank], axis=0)
    across = digits.T[0:16]

    def owner(ids):
        return ((ids + 0.5) * (1.0 / VOC)).astype(I32)

    lane = lax.broadcasted_iota(I32, (LANES, LANES), 1)
    row = lax.broadcasted_iota(I32, (LANES, LANES), 0)
    across_owner = owner(across[0:1] + 128.0 * across[1:2] + 16384.0 * across[2:3])
    across_owner = jnp.where(lane[0:1] < tokens, across_owner, SHARDS)
    down_owner = owner(digits[:, 0:1] + 128.0 * digits[:, 1:2] + 16384.0 * digits[:, 2:3])
    down_owner = jnp.where(row < tokens, down_owner, SHARDS + 1)
    same = down_owner == across_owner
    across_rank = jnp.sum(jnp.where(same & (row < lane), 1.0, 0.0), axis=0, keepdims=True).astype(I32)
    down_rank = jnp.sum(jnp.where(same & (lane < row), 1.0, 0.0), axis=1, keepdims=True).astype(I32)
    more = jnp.max(jnp.where(lane[0:1] < tokens, across_rank, 0), axis=1, keepdims=True) >= SLOTS
    rest = jnp.where(down_rank >= SLOTS, cotangents, 0.0)[0:tokens]
    rest_ref[...] = jnp.concatenate([rest, across], axis=0).astype(BF16)
    flag = jnp.where(more, 1.0, 0.0) + jnp.zeros((1, LANES), F32)
    packed = cotangents.astype(BF16)
    across = across.astype(BF16)
    slot = lax.broadcasted_iota(I32, (32, 1), 0)
    slot = jnp.where(slot < SLOTS, slot, -1)
    for s in range(SHARDS):
        place = jnp.where((across_owner == s) & (across_rank == slot), 1.0, 0.0).astype(BF16)
        rows = jnp.dot(place, packed, preferred_element_type=F32)
        codes = lax.dot_general(
            across, place, (((1,), (1,)), ((), ())), preferred_element_type=F32
        )
        codes = jnp.concatenate([codes[0:7], jnp.zeros((7, LANES - 32), F32)], axis=1)
        out_ref[s, 0:64, :] = hidden
        out_ref[s, 64:96, :] = jnp.concatenate([rows[0:SLOTS], codes, flag], axis=0).astype(BF16)


def turn_body(rows_ref, keep_out, send_out):
    for two in range(CHIPS // 2):
        for h in range(2):
            rows = rows_ref[h * 16 : h * 16 + 16, two * 16 : two * 16 + 16, :].astype(F32)
            for s in range(2):
                p = (2 * two + s) * 2 + h
                turned = rows[:, s * ROWS : (s + 1) * ROWS, :].reshape(SEQ, PAIR).T.astype(BF16)
                keep_out[p, 0:COLS, :] = turned[:COLS]
                send_out[p, 0:COLS, :] = turned[COLS:]
    keep = lax.broadcasted_iota(I32, (32, 1), 0) < SLOTS
    for four in range(SHARDS // 4):
        rows = [rows_ref[4 * four + s, 64:96, :].astype(F32) for s in range(4)]
        turned = jnp.concatenate([jnp.where(keep, r, 0.0) for r in rows], axis=0).T.astype(BF16)
        digits = jnp.concatenate([r[24:32, 0:32] for r in rows], axis=1)
        digits = jnp.concatenate([digits, jnp.zeros((8, LANES), F32)], axis=0).astype(BF16)
        for n, out in enumerate((keep_out, send_out)):
            for part in range(2):
                at = n * COLS + part * 32
                out[2 * four + part, COLS : COLS + 32, :] = turned[at : at + 32]
                out[2 * four + part, COLS + 32 :, :] = digits


def over_terms(step, one_chunk):
    full = VOC // step

    def loop(i, carry):
        one_chunk(pl.multiple_of(i * step, step), step)
        return carry

    lax.fori_loop(0, full, loop, 0)
    one_chunk(full * step, VOC - full * step)


def logits_body(
    rows_ref, got_ref, own_ref, other_ref, pooled_ref, out_ref, hidden_ref, embed_ref, spots
):
    here = lax.broadcasted_iota(I32, (8, 1), 0)
    embed_ref[0:COLS, :] = own_ref[...]
    embed_ref[COLS:, :] = other_ref[...]
    load_spots(got_ref, spots)
    for two in range(CHIPS // 2):
        for h in range(2):
            rows = rows_ref[h * 16 : h * 16 + 16, two * 16 : two * 16 + 16, :].astype(F32)
            for s in range(2):
                p = (2 * two + s) * 2 + h
                tokens = rows[:, s * ROWS : (s + 1) * ROWS, :].reshape(SEQ, PAIR)
                hidden_ref[p * SEQ : (p + 1) * SEQ, :] = tokens.astype(BF16)

    def one_chunk(first, width):
        lanes = pl.ds(first, width)
        embed = embed_ref[:, lanes]
        for p in range(OWN):
            scores = jnp.dot(
                hidden_ref[p * SEQ : (p + 1) * SEQ, :], embed, preferred_element_type=F32
            )
            index = jnp.concatenate(
                [spot_row(spots, p, first // LANES + n) for n in range(width // LANES)], axis=1
            )
            high = jnp.broadcast_to(index >> 3, (8, width))
            rows = scores[0:8]
            for n in range(1, SEQ // 8):
                rows = jnp.where(high == n, scores[8 * n : 8 * n + 8], rows)
            picked = jnp.sum(jnp.where((index & 7) == here, rows, 0.0), axis=0, keepdims=True)
            for at in range(0, width, CHUNK):
                some = min(CHUNK, width - at)
                left = p // 8 * CHUNK
                out_ref[first // CHUNK + at // CHUNK, p % 8 : p % 8 + 1, left : left + some] = picked[
                    :, at : at + some
                ]
        for at in range(0, width, CHUNK):
            some = min(CHUNK, width - at)
            for half in range(some // LANES):
                upstream = pooled_ref[:, pl.ds(first + at + half * LANES, LANES)]
                out_ref[first // CHUNK + at // CHUNK, 2 * half : 2 * half + 2, 2 * CHUNK :] = upstream

    over_terms(2048, one_chunk)
    more = rows_ref[0, 80:96, :].astype(F32)
    for s in range(1, SHARDS):
        more = jnp.maximum(more, rows_ref[s, 80:96, :].astype(F32))
    tail = jnp.concatenate([more[15:16], jnp.zeros((3, LANES), F32)], axis=0)
    for g in range(GROUPS):
        out_ref[g, 4:8, 2 * CHUNK :] = tail
    for left in range(LANES, 2 * CHUNK, CHUNK):
        out_ref[GROUPS - 1, :, left : left + LANES] = jnp.zeros((8, LANES), F32)
    out_ref[GROUPS - 1, 2:4, 2 * CHUNK :] = jnp.zeros((2, LANES), F32)


def slope_body(part_ref, bias_ref, out_ref, more_ref):
    logits = []
    upstream = []
    for c in range(2):
        total = part_ref[c, :, 0 : 2 * CHUNK]
        for m in range(1, CHIPS):
            total = total + part_ref[2 * m + c, :, 0 : 2 * CHUNK]
        logits += [total[:, :CHUNK], total[:, CHUNK:]]
        for m in range(CHIPS):
            halves = part_ref[2 * m + c, :, 2 * CHUNK :]
            upstream.append(jnp.concatenate([halves[0:2], halves[2:4]], axis=1))
    logits = jnp.concatenate(logits, axis=0) + bias_ref[...]
    upstream = jnp.concatenate(upstream, axis=0)
    softened = jnp.maximum(logits, 0.0) + jnp.log1p(jnp.exp(-jnp.abs(logits)))
    pooled = jnp.log1p(softened)
    sigmoid = 1.0 / (1.0 + jnp.exp(-logits))
    slope = sigmoid / (1.0 + softened)
    mean_pooled = jnp.sum(pooled, axis=0, keepdims=True) / PASSAGES
    grad = ((upstream + mean_pooled) * slope).astype(BF16)
    more = part_ref[0, :, 2 * CHUNK :]
    for g in range(1, GROUPS):
        more = jnp.maximum(more, part_ref[g, :, 2 * CHUNK :])
    more_ref[...] = more[4:5]
    for g in range(GROUPS):
        out_ref[g] = grad[g % 2 * OWN : g % 2 * OWN + OWN]


def hidden_body(
    grad_ref, got_ref, own_ref, other_ref, out_ref, total, left, embed_ref, grads, spots
):
    here = lax.broadcasted_iota(I32, (SEQ, LANES), 0).astype(I16)
    zero = jnp.zeros((), BF16)
    load_spots(got_ref, spots)
    embed_ref[0:COLS, :] = own_ref[...]
    embed_ref[COLS:, :] = other_ref[...]
    total[...] = jnp.zeros_like(total)

    def one_chunk(first, width):
        for at in range(0, width, CHUNK):
            grads[:, at : at + CHUNK] = grad_ref[first // CHUNK + at // CHUNK].astype(F32)
        embed = embed_ref[:, pl.ds(first, width)]
        for group in range(0, OWN, 4):
            for p in range(group, group + 4):
                for tile in range(width // LANES):
                    lanes = slice(tile * LANES, (tile + 1) * LANES)
                    index = spot_row(spots, p, first // LANES + tile)
                    index = jnp.broadcast_to(index, (16, LANES)).astype(I16)
                    value = jnp.broadcast_to(grads[p : p + 1, lanes], (16, LANES)).astype(BF16)
                    index = jnp.concatenate([index] * 8, axis=0)
                    value = jnp.concatenate([value] * 8, axis=0)
                    left[p * SEQ : (p + 1) * SEQ, lanes] = jnp.where(index == here, value, zero)
            rows = slice(group * SEQ, (group + 4) * SEQ)
            total[rows, :] += lax.dot_general(
                left[rows, 0:width], embed, (((1,), (1,)), ((), ())), preferred_element_type=F32
            )

    over_terms(1024, one_chunk)
    for x in range(4):
        for h in range(2):
            halves = []
            for z in range(2):
                p = 2 * (4 * z + x) + h
                halves.append(total[p * SEQ : (p + 1) * SEQ, :].reshape(16, ROWS, PAIR))
            at = x * SHARDS + h * 16
            out_ref[at : at + 16] = jnp.concatenate(halves, axis=1).astype(BF16)


def rest_body(place_ref, every_ref, swapped_ref, total_ref, out_ref, total):
    base = place_ref[0] * VOC
    low_row = lax.broadcasted_iota(I32, (512, LANES), 0)
    total[...] = jnp.zeros_like(total)
    for n, ref in enumerate((every_ref, swapped_ref)):

        def pair(k, carry, n=n, ref=ref):
            rows = [ref[2 * k + part].astype(F32) for part in range(2)]
            digits = jnp.concatenate([r[64:72, 0:64] for r in rows], axis=1).astype(I32)
            local = (digits[2:3] << 14) + (digits[1:2] << 7) + digits[0:1] - base
            inside = (local >= 0) & (local < VOC)
            high = jnp.where(inside, local >> 9, 15)
            turned = jnp.concatenate([r[0:64] for r in rows], axis=0).T[n * COLS : (n + 1) * COLS]
            left = [jnp.where(high == h, turned, 0.0) for h in range(8)]
            right = jnp.where(low_row == (local & 511), 1.0, 0.0)
            total[...] += lax.dot_general(
                jnp.concatenate(left, axis=0).astype(BF16),
                right.astype(BF16),
                (((1,), (1,)), ((), ())),
                preferred_element_type=F32,
            )
            return carry

        lax.fori_loop(0, SHARDS // 2, pair, 0)
    for h in range(8):
        lanes = slice(h * 512, (h + 1) * 512)
        out_ref[:, lanes] = total_ref[:, lanes] + total[h * COLS : (h + 1) * COLS, :]


def token_body(place_ref, keep_ref, got_ref, out_ref, left, right, total):
    base = place_ref[0] * VOC
    low_row = lax.broadcasted_iota(I32, (512, LANES), 0).astype(I16)
    zero = jnp.zeros((), BF16)
    one = jnp.ones((), BF16)
    total[...] = jnp.zeros_like(total)

    def token_block(table_ref):
        for group in range(8):
            digits = table_ref[2 * group, COLS + 32 :, :].astype(F32).astype(I32)
            local = (digits[2:3] << 14) + (digits[1:2] << 7) + digits[0:1] - base
            inside = (local >= 0) & (local < VOC)
            high = jnp.where(inside, local >> 9, 15)
            high = jnp.broadcast_to(high, (16, LANES)).astype(I16)
            low = jnp.broadcast_to(local & 511, (16, LANES)).astype(I16)
            high = jnp.concatenate([high] * 4, axis=0)
            low = jnp.concatenate([low] * 32, axis=0)
            cotangents = jnp.concatenate(
                [table_ref[2 * group + part, COLS : COLS + 32, :] for part in range(2)], axis=0
            )
            lanes = slice(group * LANES, (group + 1) * LANES)
            for h in range(8):
                left[h * COLS : (h + 1) * COLS, lanes] = jnp.where(
                    high == jnp.int16(h), cotangents, zero
                )
            right[:, lanes] = jnp.where(low_row == low, one, zero)
        total[...] += lax.dot_general(
            left[...], right[...], (((1,), (1,)), ((), ())), preferred_element_type=F32
        )

    for table_ref in (keep_ref, got_ref):
        token_block(table_ref)
    for h in range(8):
        out_ref[:, h * 512 : (h + 1) * 512] = total[h * COLS : (h + 1) * COLS, :]


def embed_body(
    token_ref, own_grad, other_grad, own_index, other_index, keep_ref, got_ref, out_ref, bias_ref, grads, own_spots, other_spots
):
    load_spots(own_index, own_spots)
    load_spots(other_index, other_spots)
    for g in range(GROUPS):
        grads[g, 0:OWN, :] = own_grad[g].astype(F32)
        grads[g, OWN:, :] = other_grad[g].astype(F32)

    def one_tile(tile, carry):
        lanes = pl.ds(pl.multiple_of(tile * LANES, LANES), LANES)
        half = pl.ds(pl.multiple_of((tile % 2) * LANES, LANES), LANES)
        totals = [token_ref[d : d + 16, lanes] for d in range(0, COLS, 16)]
        for n, (table_ref, spots) in enumerate(((keep_ref, own_spots), (got_ref, other_spots))):
            for p in range(OWN):
                index = spot_row(spots, p, tile)
                index = jnp.broadcast_to(index, (16, LANES)).astype(I16)
                value = grads[tile // 2, n * OWN + p : n * OWN + p + 1, half]
                for d in range(COLS // 16):
                    picked = lane_gather(table_ref[p, d * 16 : d * 16 + 16, :], index).astype(F32)
                    totals[d] = totals[d] + picked * value
        for d in range(COLS // 16):
            out_ref[d * 16 : d * 16 + 16, lanes] = totals[d]
        bias_ref[:, lanes] = jnp.sum(grads[tile // 2, :, half], axis=0, keepdims=True)
        return carry

    lax.fori_loop(0, TILES, one_tile, 0)


def sum_body(place_ref, part_ref, keep_out, send_out):
    upper = place_ref[2] == 1
    for x in range(4):
        total = part_ref[x * SHARDS].astype(F32)
        for s in range(1, SHARDS):
            total = total + part_ref[x * SHARDS + s].astype(F32)
        keep_out[x] = jnp.where(upper, total[ROWS:], total[:ROWS])
        send_out[x] = jnp.where(upper, total[:ROWS], total[ROWS:])


def join_body(place_ref, keep_ref, got_ref, out_ref):
    swap = place_ref[1] == 1
    upper = place_ref[2] == 1
    for m in range(CHIPS):
        x = m % 4
        pair = jnp.where(upper == (m >= 4), keep_ref[x], got_ref[x])
        other = jnp.concatenate([pair[:, COLS:], pair[:, :COLS]], axis=1)
        out_ref[:, m * PAIR : (m + 1) * PAIR] = jnp.where(swap, other, pair).astype(BF16)


def call(body, name, out, scratch=(), specs=None, us=1, out_specs=None, room=24):
    extra = {} if out_specs is None else {"out_specs": out_specs}
    return pl.pallas_call(
        body,
        out_shape=out,
        in_specs=specs,
        scratch_shapes=scratch,
        compiler_params=pltpu.CompilerParams(vmem_limit_bytes=room * 1024 * 1024),
        cost_estimate=pl.CostEstimate(flops=0, bytes_accessed=3_700_000 * us, transcendentals=0),
        name=name,
        **extra,
    )


def shape(dims, dtype):
    return jax.ShapeDtypeStruct(dims, dtype)


def exchange(x, axis):
    return lax.all_to_all(x, axis, split_axis=0, concat_axis=0, tiled=True)


def swap_over(x, axis):
    return lax.ppermute(x, axis, [(0, 1), (1, 0)])


def add_rest(total, rest):
    ring = [(k, (k + 1) % SHARDS) for k in range(SHARDS)]

    def step(k, carry):
        held, every = carry
        held = lax.ppermute(held, SHARD, ring)
        return held, lax.dynamic_update_index_in_dim(every, held, k, 0)

    every = jnp.zeros((SHARDS,) + rest.shape, BF16).at[0].set(rest)
    every = lax.fori_loop(1, SHARDS, step, (rest, every))[1]
    place = jnp.stack([lax.axis_index(SHARD)]).astype(I32)
    return call(
        rest_body,
        "rest",
        shape(total.shape, F32),
        [pltpu.VMEM((512, 512), F32)],
        [SMEM, VMEM, VMEM, VMEM],
    )(place, every, swap_over(every, "core"), total)


def on_device(
    hidden, embed_grad, token_ids, lengths, pool_index, embedding, head_bias, pooled_grad
):
    place = jnp.stack([lax.axis_index(name) for name in (SHARD, "core", "zl", "x")]).astype(I32)
    packed = call(
        pack_body,
        "pack",
        shape((CHIPS, IDS + 80, LANES), BF16),
        [
            pltpu.SMEM((2,), I32),
            pltpu.SMEM((ROWS,), I32),
            pltpu.VMEM((ROWS, WIDTH), BF16),
            pltpu.VMEM((ROWS, WIDTH), BF16),
            pltpu.VMEM((2, VOC), I32),
            pltpu.VMEM((64, LANES), F32),
            pltpu.SemaphoreType.DMA((5,)),
        ],
        [ANY] * 5,
        room=56,
    )(lengths, token_ids, hidden, embed_grad, pool_index)
    own_index = exchange(packed, ("zl", "x"))
    rows, rest = call(
        spread_body,
        "spread",
        (shape((SHARDS, 96, LANES), BF16), shape((80, LANES), BF16)),
        specs=[VMEM],
        room=8,
    )(own_index)
    all_rows = exchange(rows, SHARD)
    other_embed = swap_over(embedding, "core")
    partial = call(
        logits_body,
        "logits",
        shape((GROUPS, 8, 2 * CHUNK + LANES), F32),
        [
            pltpu.VMEM((OWN * SEQ, PAIR), BF16),
            pltpu.VMEM((PAIR, VOC), BF16),
            pltpu.VMEM((CHIPS, 64, LANES), I32),
        ],
        [VMEM] * 5,
        us=6,
    )(all_rows, own_index, embedding, other_embed, pooled_grad)
    keep, send = call(
        turn_body,
        "turn",
        (shape((OWN, COLS + 48, SEQ), BF16),) * 2,
        specs=[VMEM],
        us=3,
    )(all_rows)
    got = swap_over(send, "core")
    other_index = swap_over(own_index, "core")
    parts = exchange(partial, GROUP)
    parts, keep = lax.optimization_barrier((parts, keep))
    bias = jnp.pad(head_bias, (0, GROUPS * CHUNK - VOC)).reshape(GROUPS, 1, CHUNK)
    bias = lax.dynamic_index_in_dim(bias, lax.axis_index(GROUP), 0, keepdims=False)
    grad_block, more = call(
        slope_body,
        "slope",
        (shape((GROUPS, OWN, CHUNK), BF16), shape((1, LANES), F32)),
        specs=[VMEM, VMEM],
        room=8,
    )(parts, bias)
    all_grad = exchange(grad_block, GROUP)
    token_grad = call(
        token_body,
        "token_grad",
        shape((COLS, 4096), F32),
        [
            pltpu.VMEM((512, 1024), BF16),
            pltpu.VMEM((512, 1024), BF16),
            pltpu.VMEM((512, 512), F32),
        ],
        [SMEM, VMEM, VMEM],
        us=5,
        room=24,
    )(place, keep, got)
    all_grad, token_grad, other_index = lax.optimization_barrier((all_grad, token_grad, other_index))
    hidden_parts = call(
        hidden_body,
        "hidden_grad",
        shape((4 * SHARDS, 2 * ROWS, PAIR), BF16),
        [
            pltpu.VMEM((OWN * SEQ, PAIR), F32),
            pltpu.VMEM((OWN * SEQ, 1024), BF16),
            pltpu.VMEM((PAIR, VOC), BF16),
            pltpu.VMEM((OWN, 1024), F32),
            pltpu.VMEM((CHIPS, 64, LANES), I32),
        ],
        [VMEM] * 4,
        us=6,
    )(all_grad, own_index, embedding, other_embed)
    token_grad = lax.cond(more[0, 0] > 0.0, add_rest, lambda total, rest: total, token_grad, rest)
    hidden_got = exchange(hidden_parts, PLANES)
    other_grad = swap_over(all_grad, "core")
    embedding_grad, bias_grad = call(
        embed_body,
        "embedding_grad",
        (shape((COLS, VOC), F32), shape((1, VOC), F32)),
        [
            pltpu.VMEM((GROUPS, PASSAGES, CHUNK), F32),
            pltpu.VMEM((CHIPS, 64, LANES), I32),
            pltpu.VMEM((CHIPS, 64, LANES), I32),
        ],
        [VMEM] * 7,
        us=11,
        room=24,
    )(token_grad, all_grad, other_grad, own_index, other_index, keep, got)
    summed, send = call(
        sum_body,
        "sum_shards",
        (shape((4, ROWS, PAIR), F32),) * 2,
        specs=[SMEM, VMEM],
        room=8,
    )(place, hidden_got)
    hidden_grad = call(
        join_body, "join", shape((ROWS, WIDTH), BF16), specs=[SMEM, VMEM, VMEM], room=8
    )(place, summed, swap_over(send, "zl"))
    return hidden_grad, embedding_grad, bias_grad.reshape(VOC)


def solution(mesh):
    fine = Mesh(mesh.devices.reshape(2, 4, 2, 4, 8), GROUP + SHARD)
    every = P(GROUP + SHARD, None)
    split = P(GROUP, SHARD)
    return jax.shard_map(
        on_device,
        mesh=fine,
        in_specs=(every, every, P(GROUP + SHARD), P(GROUP), split, split, P(SHARD), split),
        out_specs=(every, split, P(SHARD)),
        check_vma=False,
    )
```

```python
import jax
import jax.numpy as jnp
from jax import lax
from jax.experimental import pallas as pl
from jax.experimental.pallas import tpu as pltpu
from jax.sharding import Mesh, PartitionSpec as P

F32 = jnp.float32
BF16 = jnp.bfloat16
I16 = jnp.int16
I32 = jnp.int32
LANES = 128
SMEM = pl.BlockSpec(memory_space=pltpu.SMEM)
VMEM = pl.BlockSpec(memory_space=pltpu.VMEM)
ANY = pl.BlockSpec(memory_space=pl.ANY)

GROUP = ("zl", "x", "core")
SHARD = ("zh", "y")
HOME = ("zl", "x", "zh", "y")
GROUPS = 16
SHARDS = 32
CHIPS = 8
SEQ = 128
PASSAGES = 32
OWN = 16
COLS = 64
PAIR = 128
WIDTH = 8 * PAIR
ROWS = 8
TILES = 31
VOC = TILES * LANES
CHUNK = 256
IDS = 16
SLOTS = 24


def lane_gather(table, index):
    numbers = lax.GatherDimensionNumbers(
        offset_dims=(),
        collapsed_slice_dims=(1,),
        start_index_map=(1,),
        operand_batching_dims=(0,),
        start_indices_batching_dims=(0,),
    )
    return lax.gather(
        table,
        index[..., None],
        numbers,
        (1, 1),
        mode=lax.GatherScatterMode.PROMISE_IN_BOUNDS,
    )


def load_spots(got_ref, spots):
    for m in range(CHIPS):
        spots[m] = got_ref[m, IDS + 16 :, :].astype(F32).astype(I32)


def spot_row(spots, p, tile):
    return spots[p // 2, pl.ds(2 * tile + p % 2, 1), :]


def pack_body(lengths, ids, hidden, grad, index, out_ref, *scratch):
    held, spots, sem = scratch[:5], scratch[5], scratch[6]
    copies = [
        pltpu.make_async_copy(source, target, sem.at[n])
        for n, (source, target) in enumerate(zip((lengths, ids, hidden, grad, index), held))
    ]
    for copy in copies:
        copy.start()
    for copy in copies:
        copy.wait()
    lengths_ref, ids_ref, hidden_ref, grad_ref, index_ref = held
    place = lax.axis_index(SHARD)
    swap = lax.axis_index("core") == 1
    limit = lengths_ref[place // (SEQ // ROWS)]
    spot = (place % (SEQ // ROWS)) * ROWS + lax.broadcasted_iota(I32, (ROWS, 1), 0)
    arrays = [hidden_ref[...].astype(F32), jnp.where(spot < limit, grad_ref[...].astype(F32), 0.0)]
    row = lax.broadcasted_iota(I32, (16, LANES), 0)
    lane = lax.broadcasted_iota(I32, (16, LANES), 1)
    digits = jnp.zeros((16, LANES), I32)
    for r in range(ROWS):
        digits = jnp.where(row == r, ids_ref[r], digits)
    digits = jnp.where(lane == 0, digits & 127, jnp.where(lane == 1, (digits >> 7) & 127, digits >> 14))
    digits = jnp.where(lane < 3, digits, 0).astype(F32).astype(BF16)
    spots[...] = jnp.zeros_like(spots)
    for tile in range(TILES):
        spots[2 * tile : 2 * tile + 2, :] = index_ref[:, tile * LANES : (tile + 1) * LANES].astype(F32)
    positions = spots[...].astype(BF16)
    for m in range(CHIPS):
        parts = []
        for array in arrays:
            pair = array[:, m * PAIR : (m + 1) * PAIR]
            other = jnp.concatenate([pair[:, COLS:], pair[:, :COLS]], axis=1)
            parts.append(jnp.where(swap, other, pair))
        out_ref[m, 0:IDS, :] = jnp.concatenate(parts, axis=0).astype(BF16)
        out_ref[m, IDS : IDS + 16, :] = digits
        out_ref[m, IDS + 16 :, :] = positions


def spread_body(got_ref, out_ref, rest_ref):
    tokens = 64
    hidden = []
    cotangents = []
    digits = []
    for m in range(CHIPS):
        rows = got_ref[m, 0:IDS, :].astype(F32)
        hidden.append(rows[0:ROWS])
        cotangents.append(rows[ROWS:])
        digits.append(got_ref[m, IDS : IDS + 16, :].astype(F32)[0:ROWS])
    hidden = jnp.concatenate(hidden, axis=0).astype(BF16)
    blank = jnp.zeros((LANES - tokens, LANES), F32)
    cotangents = jnp.concatenate(cotangents + [blank], axis=0)
    digits = jnp.concatenate(digits + [blank], axis=0)
    across = digits.T[0:16]

    def owner(ids):
        return ((ids + 0.5) * (1.0 / VOC)).astype(I32)

    lane = lax.broadcasted_iota(I32, (LANES, LANES), 1)
    row = lax.broadcasted_iota(I32, (LANES, LANES), 0)
    across_owner = owner(across[0:1] + 128.0 * across[1:2] + 16384.0 * across[2:3])
    across_owner = jnp.where(lane[0:1] < tokens, across_owner, SHARDS)
    down_owner = owner(digits[:, 0:1] + 128.0 * digits[:, 1:2] + 16384.0 * digits[:, 2:3])
    down_owner = jnp.where(row < tokens, down_owner, SHARDS + 1)
    same = down_owner == across_owner
    across_rank = jnp.sum(jnp.where(same & (row < lane), 1.0, 0.0), axis=0, keepdims=True).astype(I32)
    down_rank = jnp.sum(jnp.where(same & (lane < row), 1.0, 0.0), axis=1, keepdims=True).astype(I32)
    more = jnp.max(jnp.where(lane[0:1] < tokens, across_rank, 0), axis=1, keepdims=True) >= SLOTS
    rest = jnp.where(down_rank >= SLOTS, cotangents, 0.0)[0:tokens]
    rest_ref[...] = jnp.concatenate([rest, across], axis=0).astype(BF16)
    flag = jnp.where(more, 1.0, 0.0) + jnp.zeros((1, LANES), F32)
    packed = cotangents.astype(BF16)
    across = across.astype(BF16)
    slot = lax.broadcasted_iota(I32, (32, 1), 0)
    slot = jnp.where(slot < SLOTS, slot, -1)
    for s in range(SHARDS):
        place = jnp.where((across_owner == s) & (across_rank == slot), 1.0, 0.0).astype(BF16)
        rows = jnp.dot(place, packed, preferred_element_type=F32)
        codes = lax.dot_general(
            across, place, (((1,), (1,)), ((), ())), preferred_element_type=F32
        )
        codes = jnp.concatenate([codes[0:7], jnp.zeros((7, LANES - 32), F32)], axis=1)
        out_ref[s, 0:64, :] = hidden
        out_ref[s, 64:96, :] = jnp.concatenate([rows[0:SLOTS], codes, flag], axis=0).astype(BF16)


def turn_body(rows_ref, keep_out, send_out):
    for two in range(CHIPS // 2):
        for h in range(2):
            rows = rows_ref[h * 16 : h * 16 + 16, two * 16 : two * 16 + 16, :].astype(F32)
            for s in range(2):
                p = (2 * two + s) * 2 + h
                turned = rows[:, s * ROWS : (s + 1) * ROWS, :].reshape(SEQ, PAIR).T.astype(BF16)
                keep_out[p, 0:COLS, :] = turned[:COLS]
                send_out[p, 0:COLS, :] = turned[COLS:]
    keep = lax.broadcasted_iota(I32, (32, 1), 0) < SLOTS
    for four in range(SHARDS // 4):
        rows = [rows_ref[4 * four + s, 64:96, :].astype(F32) for s in range(4)]
        turned = jnp.concatenate([jnp.where(keep, r, 0.0) for r in rows], axis=0).T.astype(BF16)
        digits = jnp.concatenate([r[24:32, 0:32] for r in rows], axis=1)
        digits = jnp.concatenate([digits, jnp.zeros((8, LANES), F32)], axis=0).astype(BF16)
        for n, out in enumerate((keep_out, send_out)):
            for part in range(2):
                at = n * COLS + part * 32
                out[2 * four + part, COLS : COLS + 32, :] = turned[at : at + 32]
                out[2 * four + part, COLS + 32 :, :] = digits


def over_terms(step, one_chunk):
    full = VOC // step

    def loop(i, carry):
        one_chunk(pl.multiple_of(i * step, step), step)
        return carry

    lax.fori_loop(0, full, loop, 0)
    one_chunk(full * step, VOC - full * step)


def logits_body(
    rows_ref, got_ref, own_ref, other_ref, pooled_ref, out_ref, hidden_ref, embed_ref, spots
):
    here = lax.broadcasted_iota(I32, (8, 1), 0)
    embed_ref[0:COLS, :] = own_ref[...]
    embed_ref[COLS:, :] = other_ref[...]
    load_spots(got_ref, spots)
    for two in range(CHIPS // 2):
        for h in range(2):
            rows = rows_ref[h * 16 : h * 16 + 16, two * 16 : two * 16 + 16, :].astype(F32)
            for s in range(2):
                p = (2 * two + s) * 2 + h
                tokens = rows[:, s * ROWS : (s + 1) * ROWS, :].reshape(SEQ, PAIR)
                hidden_ref[p * SEQ : (p + 1) * SEQ, :] = tokens.astype(BF16)

    def one_chunk(first, width):
        lanes = pl.ds(first, width)
        embed = embed_ref[:, lanes]
        for p in range(OWN):
            scores = jnp.dot(
                hidden_ref[p * SEQ : (p + 1) * SEQ, :], embed, preferred_element_type=F32
            )
            index = jnp.concatenate(
                [spot_row(spots, p, first // LANES + n) for n in range(width // LANES)], axis=1
            )
            high = jnp.broadcast_to(index >> 3, (8, width))
            rows = scores[0:8]
            for n in range(1, SEQ // 8):
                rows = jnp.where(high == n, scores[8 * n : 8 * n + 8], rows)
            picked = jnp.sum(jnp.where((index & 7) == here, rows, 0.0), axis=0, keepdims=True)
            for at in range(0, width, CHUNK):
                some = min(CHUNK, width - at)
                left = p // 8 * CHUNK
                out_ref[first // CHUNK + at // CHUNK, p % 8 : p % 8 + 1, left : left + some] = picked[
                    :, at : at + some
                ]
        for at in range(0, width, CHUNK):
            some = min(CHUNK, width - at)
            for half in range(some // LANES):
                upstream = pooled_ref[:, pl.ds(first + at + half * LANES, LANES)]
                out_ref[first // CHUNK + at // CHUNK, 2 * half : 2 * half + 2, 2 * CHUNK :] = upstream

    over_terms(2048, one_chunk)
    more = rows_ref[0, 80:96, :].astype(F32)
    for s in range(1, SHARDS):
        more = jnp.maximum(more, rows_ref[s, 80:96, :].astype(F32))
    tail = jnp.concatenate([more[15:16], jnp.zeros((3, LANES), F32)], axis=0)
    for g in range(GROUPS):
        out_ref[g, 4:8, 2 * CHUNK :] = tail
    for left in range(LANES, 2 * CHUNK, CHUNK):
        out_ref[GROUPS - 1, :, left : left + LANES] = jnp.zeros((8, LANES), F32)
    out_ref[GROUPS - 1, 2:4, 2 * CHUNK :] = jnp.zeros((2, LANES), F32)


def slope_body(part_ref, bias_ref, out_ref, more_ref):
    logits = []
    upstream = []
    for c in range(2):
        total = part_ref[c, :, 0 : 2 * CHUNK]
        for m in range(1, CHIPS):
            total = total + part_ref[2 * m + c, :, 0 : 2 * CHUNK]
        logits += [total[:, :CHUNK], total[:, CHUNK:]]
        for m in range(CHIPS):
            halves = part_ref[2 * m + c, :, 2 * CHUNK :]
            upstream.append(jnp.concatenate([halves[0:2], halves[2:4]], axis=1))
    logits = jnp.concatenate(logits, axis=0) + bias_ref[...]
    upstream = jnp.concatenate(upstream, axis=0)
    softened = jnp.maximum(logits, 0.0) + jnp.log1p(jnp.exp(-jnp.abs(logits)))
    pooled = jnp.log1p(softened)
    sigmoid = 1.0 / (1.0 + jnp.exp(-logits))
    slope = sigmoid / (1.0 + softened)
    mean_pooled = jnp.sum(pooled, axis=0, keepdims=True) / PASSAGES
    grad = ((upstream + mean_pooled) * slope).astype(BF16)
    more = part_ref[0, :, 2 * CHUNK :]
    for g in range(1, GROUPS):
        more = jnp.maximum(more, part_ref[g, :, 2 * CHUNK :])
    more_ref[...] = more[4:5]
    for g in range(GROUPS):
        out_ref[g] = grad[g % 2 * OWN : g % 2 * OWN + OWN]


def hidden_body(
    grad_ref, got_ref, own_ref, other_ref, out_ref, total, left, embed_ref, grads, spots
):
    here = lax.broadcasted_iota(I32, (SEQ, LANES), 0).astype(I16)
    zero = jnp.zeros((), BF16)
    load_spots(got_ref, spots)
    embed_ref[0:COLS, :] = own_ref[...]
    embed_ref[COLS:, :] = other_ref[...]
    total[...] = jnp.zeros_like(total)

    def one_chunk(first, width):
        for at in range(0, width, CHUNK):
            grads[:, at : at + CHUNK] = grad_ref[first // CHUNK + at // CHUNK].astype(F32)
        embed = embed_ref[:, pl.ds(first, width)]
        for group in range(0, OWN, 4):
            for p in range(group, group + 4):
                for tile in range(width // LANES):
                    lanes = slice(tile * LANES, (tile + 1) * LANES)
                    index = spot_row(spots, p, first // LANES + tile)
                    index = jnp.broadcast_to(index, (16, LANES)).astype(I16)
                    value = jnp.broadcast_to(grads[p : p + 1, lanes], (16, LANES)).astype(BF16)
                    index = jnp.concatenate([index] * 8, axis=0)
                    value = jnp.concatenate([value] * 8, axis=0)
                    left[p * SEQ : (p + 1) * SEQ, lanes] = jnp.where(index == here, value, zero)
            rows = slice(group * SEQ, (group + 4) * SEQ)
            total[rows, :] += lax.dot_general(
                left[rows, 0:width], embed, (((1,), (1,)), ((), ())), preferred_element_type=F32
            )

    over_terms(1024, one_chunk)
    out_ref[...] = total[...].astype(BF16)


def rest_body(place_ref, every_ref, swapped_ref, total_ref, out_ref, total):
    base = place_ref[0] * VOC
    low_row = lax.broadcasted_iota(I32, (512, LANES), 0)
    total[...] = jnp.zeros_like(total)
    for n, ref in enumerate((every_ref, swapped_ref)):

        def pair(k, carry, n=n, ref=ref):
            rows = [ref[2 * k + part].astype(F32) for part in range(2)]
            digits = jnp.concatenate([r[64:72, 0:64] for r in rows], axis=1).astype(I32)
            local = (digits[2:3] << 14) + (digits[1:2] << 7) + digits[0:1] - base
            inside = (local >= 0) & (local < VOC)
            high = jnp.where(inside, local >> 9, 15)
            turned = jnp.concatenate([r[0:64] for r in rows], axis=0).T[n * COLS : (n + 1) * COLS]
            left = [jnp.where(high == h, turned, 0.0) for h in range(8)]
            right = jnp.where(low_row == (local & 511), 1.0, 0.0)
            total[...] += lax.dot_general(
                jnp.concatenate(left, axis=0).astype(BF16),
                right.astype(BF16),
                (((1,), (1,)), ((), ())),
                preferred_element_type=F32,
            )
            return carry

        lax.fori_loop(0, SHARDS // 2, pair, 0)
    for h in range(8):
        lanes = slice(h * 512, (h + 1) * 512)
        out_ref[:, lanes] = total_ref[:, lanes] + total[h * COLS : (h + 1) * COLS, :]


def token_body(place_ref, keep_ref, got_ref, out_ref, left, right, total):
    base = place_ref[0] * VOC
    low_row = lax.broadcasted_iota(I32, (512, LANES), 0).astype(I16)
    zero = jnp.zeros((), BF16)
    one = jnp.ones((), BF16)
    total[...] = jnp.zeros_like(total)

    def token_block(table_ref):
        for group in range(8):
            digits = table_ref[2 * group, COLS + 32 :, :].astype(F32).astype(I32)
            local = (digits[2:3] << 14) + (digits[1:2] << 7) + digits[0:1] - base
            inside = (local >= 0) & (local < VOC)
            high = jnp.where(inside, local >> 9, 15)
            high = jnp.broadcast_to(high, (16, LANES)).astype(I16)
            low = jnp.broadcast_to(local & 511, (16, LANES)).astype(I16)
            high = jnp.concatenate([high] * 4, axis=0)
            low = jnp.concatenate([low] * 32, axis=0)
            cotangents = jnp.concatenate(
                [table_ref[2 * group + part, COLS : COLS + 32, :] for part in range(2)], axis=0
            )
            lanes = slice(group * LANES, (group + 1) * LANES)
            for h in range(8):
                left[h * COLS : (h + 1) * COLS, lanes] = jnp.where(
                    high == jnp.int16(h), cotangents, zero
                )
            right[:, lanes] = jnp.where(low_row == low, one, zero)
        total[...] += lax.dot_general(
            left[...], right[...], (((1,), (1,)), ((), ())), preferred_element_type=F32
        )

    for table_ref in (keep_ref, got_ref):
        token_block(table_ref)
    for h in range(8):
        out_ref[:, h * 512 : (h + 1) * 512] = total[h * COLS : (h + 1) * COLS, :]


def embed_body(
    token_ref, own_grad, other_grad, own_index, other_index, keep_ref, got_ref, out_ref, bias_ref, grads, own_spots, other_spots
):
    load_spots(own_index, own_spots)
    load_spots(other_index, other_spots)
    for g in range(GROUPS):
        grads[g, 0:OWN, :] = own_grad[g].astype(F32)
        grads[g, OWN:, :] = other_grad[g].astype(F32)

    def one_tile(tile, carry):
        lanes = pl.ds(pl.multiple_of(tile * LANES, LANES), LANES)
        half = pl.ds(pl.multiple_of((tile % 2) * LANES, LANES), LANES)
        totals = [token_ref[d : d + 16, lanes] for d in range(0, COLS, 16)]
        for n, (table_ref, spots) in enumerate(((keep_ref, own_spots), (got_ref, other_spots))):
            for p in range(OWN):
                index = spot_row(spots, p, tile)
                index = jnp.broadcast_to(index, (16, LANES)).astype(I16)
                value = grads[tile // 2, n * OWN + p : n * OWN + p + 1, half]
                for d in range(COLS // 16):
                    picked = lane_gather(table_ref[p, d * 16 : d * 16 + 16, :], index).astype(F32)
                    totals[d] = totals[d] + picked * value
        for d in range(COLS // 16):
            out_ref[d * 16 : d * 16 + 16, lanes] = totals[d]
        bias_ref[:, lanes] = jnp.sum(grads[tile // 2, :, half], axis=0, keepdims=True)
        return carry

    lax.fori_loop(0, TILES, one_tile, 0)


def sum_body(place_ref, part_ref, out_ref):
    swap = place_ref[1] == 1
    for m in range(CHIPS):
        total = part_ref[m * SHARDS // 2].astype(F32)
        for s in range(1, SHARDS // 2):
            total = total + part_ref[m * SHARDS // 2 + s].astype(F32)
        total = total[:ROWS] + total[ROWS:]
        other = jnp.concatenate([total[:, COLS:], total[:, :COLS]], axis=1)
        out_ref[:, m * PAIR : (m + 1) * PAIR] = jnp.where(swap, other, total).astype(BF16)


def call(body, name, out, scratch=(), specs=None, us=1, out_specs=None, room=24):
    extra = {} if out_specs is None else {"out_specs": out_specs}
    return pl.pallas_call(
        body,
        out_shape=out,
        in_specs=specs,
        scratch_shapes=scratch,
        compiler_params=pltpu.CompilerParams(vmem_limit_bytes=room * 1024 * 1024),
        cost_estimate=pl.CostEstimate(flops=0, bytes_accessed=3_700_000 * us, transcendentals=0),
        name=name,
        **extra,
    )


def shape(dims, dtype):
    return jax.ShapeDtypeStruct(dims, dtype)


def exchange(x, axis):
    return lax.all_to_all(x, axis, split_axis=0, concat_axis=0, tiled=True)


def swap_over(x, axis):
    return lax.ppermute(x, axis, [(0, 1), (1, 0)])


def add_rest(total, rest):
    ring = [(k, (k + 1) % SHARDS) for k in range(SHARDS)]

    def step(k, carry):
        held, every = carry
        held = lax.ppermute(held, SHARD, ring)
        return held, lax.dynamic_update_index_in_dim(every, held, k, 0)

    every = jnp.zeros((SHARDS,) + rest.shape, BF16).at[0].set(rest)
    every = lax.fori_loop(1, SHARDS, step, (rest, every))[1]
    place = jnp.stack([lax.axis_index(SHARD)]).astype(I32)
    return call(
        rest_body,
        "rest",
        shape(total.shape, F32),
        [pltpu.VMEM((512, 512), F32)],
        [SMEM, VMEM, VMEM, VMEM],
    )(place, every, swap_over(every, "core"), total)


def on_device(
    hidden, embed_grad, token_ids, lengths, pool_index, embedding, head_bias, pooled_grad
):
    place = jnp.stack([lax.axis_index(name) for name in (SHARD, "core", "zl", "x")]).astype(I32)
    packed = call(
        pack_body,
        "pack",
        shape((CHIPS, IDS + 80, LANES), BF16),
        [
            pltpu.SMEM((2,), I32),
            pltpu.SMEM((ROWS,), I32),
            pltpu.VMEM((ROWS, WIDTH), BF16),
            pltpu.VMEM((ROWS, WIDTH), BF16),
            pltpu.VMEM((2, VOC), I32),
            pltpu.VMEM((64, LANES), F32),
            pltpu.SemaphoreType.DMA((5,)),
        ],
        [ANY] * 5,
        room=56,
    )(lengths, token_ids, hidden, embed_grad, pool_index)
    own_index = exchange(packed, ("zl", "x"))
    rows, rest = call(
        spread_body,
        "spread",
        (shape((SHARDS, 96, LANES), BF16), shape((80, LANES), BF16)),
        specs=[VMEM],
        room=8,
    )(own_index)
    all_rows = exchange(rows, SHARD)
    other_embed = swap_over(embedding, "core")
    partial = call(
        logits_body,
        "logits",
        shape((GROUPS, 8, 2 * CHUNK + LANES), F32),
        [
            pltpu.VMEM((OWN * SEQ, PAIR), BF16),
            pltpu.VMEM((PAIR, VOC), BF16),
            pltpu.VMEM((CHIPS, 64, LANES), I32),
        ],
        [VMEM] * 5,
        us=6,
    )(all_rows, own_index, embedding, other_embed, pooled_grad)
    keep, send = call(
        turn_body,
        "turn",
        (shape((OWN, COLS + 48, SEQ), BF16),) * 2,
        specs=[VMEM],
        us=3,
    )(all_rows)
    got = swap_over(send, "core")
    other_index = swap_over(own_index, "core")
    parts = exchange(partial, GROUP)
    parts, keep = lax.optimization_barrier((parts, keep))
    bias = jnp.pad(head_bias, (0, GROUPS * CHUNK - VOC)).reshape(GROUPS, 1, CHUNK)
    bias = lax.dynamic_index_in_dim(bias, lax.axis_index(GROUP), 0, keepdims=False)
    grad_block, more = call(
        slope_body,
        "slope",
        (shape((GROUPS, OWN, CHUNK), BF16), shape((1, LANES), F32)),
        specs=[VMEM, VMEM],
        room=8,
    )(parts, bias)
    all_grad = exchange(grad_block, GROUP)
    token_grad = call(
        token_body,
        "token_grad",
        shape((COLS, 4096), F32),
        [
            pltpu.VMEM((512, 1024), BF16),
            pltpu.VMEM((512, 1024), BF16),
            pltpu.VMEM((512, 512), F32),
        ],
        [SMEM, VMEM, VMEM],
        us=5,
        room=24,
    )(place, keep, got)
    all_grad, token_grad, other_index = lax.optimization_barrier((all_grad, token_grad, other_index))
    hidden_parts = call(
        hidden_body,
        "hidden_grad",
        shape((OWN * SEQ, PAIR), BF16),
        [
            pltpu.VMEM((OWN * SEQ, PAIR), F32),
            pltpu.VMEM((OWN * SEQ, 1024), BF16),
            pltpu.VMEM((PAIR, VOC), BF16),
            pltpu.VMEM((OWN, 1024), F32),
            pltpu.VMEM((CHIPS, 64, LANES), I32),
        ],
        [VMEM] * 4,
        us=6,
    )(all_grad, own_index, embedding, other_embed)
    token_grad = lax.cond(more[0, 0] > 0.0, add_rest, lambda total, rest: total, token_grad, rest)
    hidden_got = exchange(hidden_parts.reshape(CHIPS * SHARDS, ROWS, PAIR), HOME)
    other_grad = swap_over(all_grad, "core")
    embedding_grad, bias_grad = call(
        embed_body,
        "embedding_grad",
        (shape((COLS, VOC), F32), shape((1, VOC), F32)),
        [
            pltpu.VMEM((GROUPS, PASSAGES, CHUNK), F32),
            pltpu.VMEM((CHIPS, 64, LANES), I32),
            pltpu.VMEM((CHIPS, 64, LANES), I32),
        ],
        [VMEM] * 7,
        us=11,
        room=24,
    )(token_grad, all_grad, other_grad, own_index, other_index, keep, got)
    hidden_grad = call(
        sum_body, "sum_shards", shape((ROWS, WIDTH), BF16), specs=[SMEM, VMEM], room=8
    )(place, hidden_got.reshape(CHIPS * SHARDS // 2, 2 * ROWS, PAIR))
    return hidden_grad, embedding_grad, bias_grad.reshape(VOC)


def solution(mesh):
    fine = Mesh(mesh.devices.reshape(2, 4, 2, 4, 8), GROUP + SHARD)
    every = P(GROUP + SHARD, None)
    split = P(GROUP, SHARD)
    return jax.shard_map(
        on_device,
        mesh=fine,
        in_specs=(every, every, P(GROUP + SHARD), P(GROUP), split, split, P(SHARD), split),
        out_specs=(every, split, P(SHARD)),
        check_vma=False,
    )
```

```python
import jax
import jax.numpy as jnp
from jax import lax
from jax.experimental import pallas as pl
from jax.experimental.pallas import tpu as pltpu
from jax.sharding import Mesh, PartitionSpec as P

F32 = jnp.float32
BF16 = jnp.bfloat16
I16 = jnp.int16
I32 = jnp.int32
LANES = 128
SMEM = pl.BlockSpec(memory_space=pltpu.SMEM)
VMEM = pl.BlockSpec(memory_space=pltpu.VMEM)
ANY = pl.BlockSpec(memory_space=pl.ANY)

GROUP = ("zl", "x", "core")
SHARD = ("zh", "y")
HOME = ("zl", "x", "zh", "y")
GROUPS = 16
SHARDS = 32
CHIPS = 8
SEQ = 128
PASSAGES = 32
OWN = 16
COLS = 64
PAIR = 128
WIDTH = 8 * PAIR
ROWS = 8
TILES = 31
VOC = TILES * LANES
CHUNK = 256
IDS = 16
SLOTS = 24


def lane_gather(table, index):
    numbers = lax.GatherDimensionNumbers(
        offset_dims=(),
        collapsed_slice_dims=(1,),
        start_index_map=(1,),
        operand_batching_dims=(0,),
        start_indices_batching_dims=(0,),
    )
    return lax.gather(
        table,
        index[..., None],
        numbers,
        (1, 1),
        mode=lax.GatherScatterMode.PROMISE_IN_BOUNDS,
    )


def load_spots(got_ref, spots):
    for m in range(CHIPS):
        spots[m] = got_ref[m, IDS + 16 :, :].astype(F32).astype(I32)


def spot_row(spots, p, tile):
    return spots[p // 2, pl.ds(2 * tile + p % 2, 1), :]


def pack_body(lengths, ids, hidden, grad, index, out_ref, *scratch):
    held, spots, sem = scratch[:5], scratch[5], scratch[6]
    copies = [
        pltpu.make_async_copy(source, target, sem.at[n])
        for n, (source, target) in enumerate(zip((lengths, ids, hidden, grad, index), held))
    ]
    for copy in copies:
        copy.start()
    for copy in copies:
        copy.wait()
    lengths_ref, ids_ref, hidden_ref, grad_ref, index_ref = held
    place = lax.axis_index(SHARD)
    swap = lax.axis_index("core") == 1
    limit = lengths_ref[place // (SEQ // ROWS)]
    spot = (place % (SEQ // ROWS)) * ROWS + lax.broadcasted_iota(I32, (ROWS, 1), 0)
    arrays = [hidden_ref[...].astype(F32), jnp.where(spot < limit, grad_ref[...].astype(F32), 0.0)]
    row = lax.broadcasted_iota(I32, (16, LANES), 0)
    lane = lax.broadcasted_iota(I32, (16, LANES), 1)
    digits = jnp.zeros((16, LANES), I32)
    for r in range(ROWS):
        digits = jnp.where(row == r, ids_ref[r], digits)
    digits = jnp.where(lane == 0, digits & 127, jnp.where(lane == 1, (digits >> 7) & 127, digits >> 14))
    digits = jnp.where(lane < 3, digits, 0).astype(F32).astype(BF16)
    spots[...] = jnp.zeros_like(spots)
    for tile in range(TILES):
        spots[2 * tile : 2 * tile + 2, :] = index_ref[:, tile * LANES : (tile + 1) * LANES].astype(F32)
    positions = spots[...].astype(BF16)
    for m in range(CHIPS):
        parts = []
        for array in arrays:
            pair = array[:, m * PAIR : (m + 1) * PAIR]
            other = jnp.concatenate([pair[:, COLS:], pair[:, :COLS]], axis=1)
            parts.append(jnp.where(swap, other, pair))
        out_ref[m, 0:IDS, :] = jnp.concatenate(parts, axis=0).astype(BF16)
        out_ref[m, IDS : IDS + 16, :] = digits
        out_ref[m, IDS + 16 :, :] = positions


def spread_body(got_ref, out_ref, rest_ref):
    tokens = 64
    hidden = []
    cotangents = []
    digits = []
    for m in range(CHIPS):
        rows = got_ref[m, 0:IDS, :].astype(F32)
        hidden.append(rows[0:ROWS])
        cotangents.append(rows[ROWS:])
        digits.append(got_ref[m, IDS : IDS + 16, :].astype(F32)[0:ROWS])
    hidden = jnp.concatenate(hidden, axis=0).astype(BF16)
    blank = jnp.zeros((LANES - tokens, LANES), F32)
    cotangents = jnp.concatenate(cotangents + [blank], axis=0)
    digits = jnp.concatenate(digits + [blank], axis=0)
    across = digits.T[0:16]

    def owner(ids):
        return ((ids + 0.5) * (1.0 / VOC)).astype(I32)

    lane = lax.broadcasted_iota(I32, (LANES, LANES), 1)
    row = lax.broadcasted_iota(I32, (LANES, LANES), 0)
    across_owner = owner(across[0:1] + 128.0 * across[1:2] + 16384.0 * across[2:3])
    across_owner = jnp.where(lane[0:1] < tokens, across_owner, SHARDS)
    down_owner = owner(digits[:, 0:1] + 128.0 * digits[:, 1:2] + 16384.0 * digits[:, 2:3])
    down_owner = jnp.where(row < tokens, down_owner, SHARDS + 1)
    same = down_owner == across_owner
    across_rank = jnp.sum(jnp.where(same & (row < lane), 1.0, 0.0), axis=0, keepdims=True).astype(I32)
    down_rank = jnp.sum(jnp.where(same & (lane < row), 1.0, 0.0), axis=1, keepdims=True).astype(I32)
    more = jnp.max(jnp.where(lane[0:1] < tokens, across_rank, 0), axis=1, keepdims=True) >= SLOTS
    rest = jnp.where(down_rank >= SLOTS, cotangents, 0.0)[0:tokens]
    rest_ref[...] = jnp.concatenate([rest, across], axis=0).astype(BF16)
    flag = jnp.where(more, 1.0, 0.0) + jnp.zeros((1, LANES), F32)
    packed = cotangents.astype(BF16)
    across = across.astype(BF16)
    slot = lax.broadcasted_iota(I32, (32, 1), 0)
    slot = jnp.where(slot < SLOTS, slot, -1)
    for s in range(SHARDS):
        place = jnp.where((across_owner == s) & (across_rank == slot), 1.0, 0.0).astype(BF16)
        rows = jnp.dot(place, packed, preferred_element_type=F32)
        codes = lax.dot_general(
            across, place, (((1,), (1,)), ((), ())), preferred_element_type=F32
        )
        codes = jnp.concatenate([codes[0:7], jnp.zeros((7, LANES - 32), F32)], axis=1)
        out_ref[s, 0:64, :] = hidden
        out_ref[s, 64:96, :] = jnp.concatenate([rows[0:SLOTS], codes, flag], axis=0).astype(BF16)


def turn_body(rows_ref, keep_out, send_out):
    for two in range(CHIPS // 2):
        for h in range(2):
            rows = rows_ref[h * 16 : h * 16 + 16, two * 16 : two * 16 + 16, :].astype(F32)
            for s in range(2):
                p = (2 * two + s) * 2 + h
                turned = rows[:, s * ROWS : (s + 1) * ROWS, :].reshape(SEQ, PAIR).T.astype(BF16)
                keep_out[p, 0:COLS, :] = turned[:COLS]
                send_out[p, 0:COLS, :] = turned[COLS:]
    keep = lax.broadcasted_iota(I32, (32, 1), 0) < SLOTS
    for four in range(SHARDS // 4):
        rows = [rows_ref[4 * four + s, 64:96, :].astype(F32) for s in range(4)]
        turned = jnp.concatenate([jnp.where(keep, r, 0.0) for r in rows], axis=0).T.astype(BF16)
        digits = jnp.concatenate([r[24:32, 0:32] for r in rows], axis=1)
        digits = jnp.concatenate([digits, jnp.zeros((8, LANES), F32)], axis=0).astype(BF16)
        for n, out in enumerate((keep_out, send_out)):
            for part in range(2):
                at = n * COLS + part * 32
                out[2 * four + part, COLS : COLS + 32, :] = turned[at : at + 32]
                out[2 * four + part, COLS + 32 :, :] = digits


def ready_body(got_ref, own_ref, other_ref, spots_ref, embed_ref):
    load_spots(got_ref, spots_ref)
    embed_ref[0:COLS, :] = own_ref[...]
    embed_ref[COLS:, :] = other_ref[...]


def over_terms(step, one_chunk):
    full = VOC // step

    def loop(i, carry):
        one_chunk(pl.multiple_of(i * step, step), step)
        return carry

    lax.fori_loop(0, full, loop, 0)
    one_chunk(full * step, VOC - full * step)


def logits_body(
    rows_ref, spots, embed_ref, pooled_ref, out_ref, hidden_ref
):
    here = lax.broadcasted_iota(I32, (8, 1), 0)
    for two in range(CHIPS // 2):
        for h in range(2):
            rows = rows_ref[h * 16 : h * 16 + 16, two * 16 : two * 16 + 16, :].astype(F32)
            for s in range(2):
                p = (2 * two + s) * 2 + h
                tokens = rows[:, s * ROWS : (s + 1) * ROWS, :].reshape(SEQ, PAIR)
                hidden_ref[p * SEQ : (p + 1) * SEQ, :] = tokens.astype(BF16)

    def one_chunk(first, width):
        lanes = pl.ds(first, width)
        embed = embed_ref[:, lanes]
        for p in range(OWN):
            scores = jnp.dot(
                hidden_ref[p * SEQ : (p + 1) * SEQ, :], embed, preferred_element_type=F32
            )
            index = jnp.concatenate(
                [spot_row(spots, p, first // LANES + n) for n in range(width // LANES)], axis=1
            )
            high = jnp.broadcast_to(index >> 3, (8, width))
            rows = scores[0:8]
            for n in range(1, SEQ // 8):
                rows = jnp.where(high == n, scores[8 * n : 8 * n + 8], rows)
            picked = jnp.sum(jnp.where((index & 7) == here, rows, 0.0), axis=0, keepdims=True)
            for at in range(0, width, CHUNK):
                some = min(CHUNK, width - at)
                left = p // 8 * CHUNK
                out_ref[first // CHUNK + at // CHUNK, p % 8 : p % 8 + 1, left : left + some] = picked[
                    :, at : at + some
                ]
        for at in range(0, width, CHUNK):
            some = min(CHUNK, width - at)
            for half in range(some // LANES):
                upstream = pooled_ref[:, pl.ds(first + at + half * LANES, LANES)]
                out_ref[first // CHUNK + at // CHUNK, 2 * half : 2 * half + 2, 2 * CHUNK :] = upstream

    over_terms(2048, one_chunk)
    more = rows_ref[0, 80:96, :].astype(F32)
    for s in range(1, SHARDS):
        more = jnp.maximum(more, rows_ref[s, 80:96, :].astype(F32))
    tail = jnp.concatenate([more[15:16], jnp.zeros((3, LANES), F32)], axis=0)
    for g in range(GROUPS):
        out_ref[g, 4:8, 2 * CHUNK :] = tail
    for left in range(LANES, 2 * CHUNK, CHUNK):
        out_ref[GROUPS - 1, :, left : left + LANES] = jnp.zeros((8, LANES), F32)
    out_ref[GROUPS - 1, 2:4, 2 * CHUNK :] = jnp.zeros((2, LANES), F32)


def slope_body(part_ref, bias_ref, out_ref, more_ref):
    logits = []
    upstream = []
    for c in range(2):
        total = part_ref[c, :, 0 : 2 * CHUNK]
        for m in range(1, CHIPS):
            total = total + part_ref[2 * m + c, :, 0 : 2 * CHUNK]
        logits += [total[:, :CHUNK], total[:, CHUNK:]]
        for m in range(CHIPS):
            halves = part_ref[2 * m + c, :, 2 * CHUNK :]
            upstream.append(jnp.concatenate([halves[0:2], halves[2:4]], axis=1))
    logits = jnp.concatenate(logits, axis=0) + bias_ref[...]
    upstream = jnp.concatenate(upstream, axis=0)
    softened = jnp.maximum(logits, 0.0) + jnp.log1p(jnp.exp(-jnp.abs(logits)))
    pooled = jnp.log1p(softened)
    sigmoid = 1.0 / (1.0 + jnp.exp(-logits))
    slope = sigmoid / (1.0 + softened)
    mean_pooled = jnp.sum(pooled, axis=0, keepdims=True) / PASSAGES
    grad = ((upstream + mean_pooled) * slope).astype(BF16)
    more = part_ref[0, :, 2 * CHUNK :]
    for g in range(1, GROUPS):
        more = jnp.maximum(more, part_ref[g, :, 2 * CHUNK :])
    more_ref[...] = more[4:5]
    for g in range(GROUPS):
        out_ref[g] = grad[g % 2 * OWN : g % 2 * OWN + OWN]


def hidden_body(
    grad_ref, spots, embed_ref, out_ref, total, left, grads
):
    here = lax.broadcasted_iota(I32, (SEQ, LANES), 0).astype(I16)
    zero = jnp.zeros((), BF16)
    total[...] = jnp.zeros_like(total)

    def one_chunk(first, width):
        for at in range(0, width, CHUNK):
            grads[:, at : at + CHUNK] = grad_ref[first // CHUNK + at // CHUNK].astype(F32)
        embed = embed_ref[:, pl.ds(first, width)]
        for group in range(0, OWN, 4):
            for p in range(group, group + 4):
                for tile in range(width // LANES):
                    lanes = slice(tile * LANES, (tile + 1) * LANES)
                    index = spot_row(spots, p, first // LANES + tile)
                    index = jnp.broadcast_to(index, (16, LANES)).astype(I16)
                    value = jnp.broadcast_to(grads[p : p + 1, lanes], (16, LANES)).astype(BF16)
                    index = jnp.concatenate([index] * 8, axis=0)
                    value = jnp.concatenate([value] * 8, axis=0)
                    left[p * SEQ : (p + 1) * SEQ, lanes] = jnp.where(index == here, value, zero)
            rows = slice(group * SEQ, (group + 4) * SEQ)
            total[rows, :] += lax.dot_general(
                left[rows, 0:width], embed, (((1,), (1,)), ((), ())), preferred_element_type=F32
            )

    over_terms(1024, one_chunk)
    out_ref[...] = total[...].astype(BF16)


def rest_body(place_ref, every_ref, swapped_ref, total_ref, out_ref, total):
    base = place_ref[0] * VOC
    low_row = lax.broadcasted_iota(I32, (512, LANES), 0)
    total[...] = jnp.zeros_like(total)
    for n, ref in enumerate((every_ref, swapped_ref)):

        def pair(k, carry, n=n, ref=ref):
            rows = [ref[2 * k + part].astype(F32) for part in range(2)]
            digits = jnp.concatenate([r[64:72, 0:64] for r in rows], axis=1).astype(I32)
            local = (digits[2:3] << 14) + (digits[1:2] << 7) + digits[0:1] - base
            inside = (local >= 0) & (local < VOC)
            high = jnp.where(inside, local >> 9, 15)
            turned = jnp.concatenate([r[0:64] for r in rows], axis=0).T[n * COLS : (n + 1) * COLS]
            left = [jnp.where(high == h, turned, 0.0) for h in range(8)]
            right = jnp.where(low_row == (local & 511), 1.0, 0.0)
            total[...] += lax.dot_general(
                jnp.concatenate(left, axis=0).astype(BF16),
                right.astype(BF16),
                (((1,), (1,)), ((), ())),
                preferred_element_type=F32,
            )
            return carry

        lax.fori_loop(0, SHARDS // 2, pair, 0)
    for h in range(8):
        lanes = slice(h * 512, (h + 1) * 512)
        out_ref[:, lanes] = total_ref[:, lanes] + total[h * COLS : (h + 1) * COLS, :]


def token_body(place_ref, keep_ref, got_ref, out_ref, left, right, total):
    base = place_ref[0] * VOC
    low_row = lax.broadcasted_iota(I32, (512, LANES), 0).astype(I16)
    zero = jnp.zeros((), BF16)
    one = jnp.ones((), BF16)
    total[...] = jnp.zeros_like(total)

    def token_block(table_ref):
        for group in range(8):
            digits = table_ref[2 * group, COLS + 32 :, :].astype(F32).astype(I32)
            local = (digits[2:3] << 14) + (digits[1:2] << 7) + digits[0:1] - base
            inside = (local >= 0) & (local < VOC)
            high = jnp.where(inside, local >> 9, 15)
            high = jnp.broadcast_to(high, (16, LANES)).astype(I16)
            low = jnp.broadcast_to(local & 511, (16, LANES)).astype(I16)
            high = jnp.concatenate([high] * 4, axis=0)
            low = jnp.concatenate([low] * 32, axis=0)
            cotangents = jnp.concatenate(
                [table_ref[2 * group + part, COLS : COLS + 32, :] for part in range(2)], axis=0
            )
            lanes = slice(group * LANES, (group + 1) * LANES)
            for h in range(8):
                left[h * COLS : (h + 1) * COLS, lanes] = jnp.where(
                    high == jnp.int16(h), cotangents, zero
                )
            right[:, lanes] = jnp.where(low_row == low, one, zero)
        total[...] += lax.dot_general(
            left[...], right[...], (((1,), (1,)), ((), ())), preferred_element_type=F32
        )

    for table_ref in (keep_ref, got_ref):
        token_block(table_ref)
    for h in range(8):
        out_ref[:, h * 512 : (h + 1) * 512] = total[h * COLS : (h + 1) * COLS, :]


def embed_body(
    token_ref, own_grad, other_grad, own_spots, other_index, keep_ref, got_ref, out_ref, bias_ref, grads, other_spots
):
    load_spots(other_index, other_spots)
    for g in range(GROUPS):
        grads[g, 0:OWN, :] = own_grad[g].astype(F32)
        grads[g, OWN:, :] = other_grad[g].astype(F32)

    def one_tile(tile, carry):
        lanes = pl.ds(pl.multiple_of(tile * LANES, LANES), LANES)
        half = pl.ds(pl.multiple_of((tile % 2) * LANES, LANES), LANES)
        totals = [token_ref[d : d + 16, lanes] for d in range(0, COLS, 16)]
        for n, (table_ref, spots) in enumerate(((keep_ref, own_spots), (got_ref, other_spots))):
            for p in range(OWN):
                index = spot_row(spots, p, tile)
                index = jnp.broadcast_to(index, (16, LANES)).astype(I16)
                value = grads[tile // 2, n * OWN + p : n * OWN + p + 1, half]
                for d in range(COLS // 16):
                    picked = lane_gather(table_ref[p, d * 16 : d * 16 + 16, :], index).astype(F32)
                    totals[d] = totals[d] + picked * value
        for d in range(COLS // 16):
            out_ref[d * 16 : d * 16 + 16, lanes] = totals[d]
        bias_ref[:, lanes] = jnp.sum(grads[tile // 2, :, half], axis=0, keepdims=True)
        return carry

    lax.fori_loop(0, TILES, one_tile, 0)


def sum_body(place_ref, part_ref, out_ref):
    swap = place_ref[1] == 1
    for m in range(CHIPS):
        total = part_ref[m * SHARDS // 2].astype(F32)
        for s in range(1, SHARDS // 2):
            total = total + part_ref[m * SHARDS // 2 + s].astype(F32)
        total = total[:ROWS] + total[ROWS:]
        other = jnp.concatenate([total[:, COLS:], total[:, :COLS]], axis=1)
        out_ref[:, m * PAIR : (m + 1) * PAIR] = jnp.where(swap, other, total).astype(BF16)


def call(body, name, out, scratch=(), specs=None, us=1, out_specs=None, room=24):
    extra = {} if out_specs is None else {"out_specs": out_specs}
    return pl.pallas_call(
        body,
        out_shape=out,
        in_specs=specs,
        scratch_shapes=scratch,
        compiler_params=pltpu.CompilerParams(vmem_limit_bytes=room * 1024 * 1024),
        cost_estimate=pl.CostEstimate(flops=0, bytes_accessed=3_700_000 * us, transcendentals=0),
        name=name,
        **extra,
    )


def shape(dims, dtype):
    return jax.ShapeDtypeStruct(dims, dtype)


def exchange(x, axis):
    return lax.all_to_all(x, axis, split_axis=0, concat_axis=0, tiled=True)


def swap_over(x, axis):
    return lax.ppermute(x, axis, [(0, 1), (1, 0)])


def add_rest(total, rest):
    ring = [(k, (k + 1) % SHARDS) for k in range(SHARDS)]

    def step(k, carry):
        held, every = carry
        held = lax.ppermute(held, SHARD, ring)
        return held, lax.dynamic_update_index_in_dim(every, held, k, 0)

    every = jnp.zeros((SHARDS,) + rest.shape, BF16).at[0].set(rest)
    every = lax.fori_loop(1, SHARDS, step, (rest, every))[1]
    place = jnp.stack([lax.axis_index(SHARD)]).astype(I32)
    return call(
        rest_body,
        "rest",
        shape(total.shape, F32),
        [pltpu.VMEM((512, 512), F32)],
        [SMEM, VMEM, VMEM, VMEM],
    )(place, every, swap_over(every, "core"), total)


def on_device(
    hidden, embed_grad, token_ids, lengths, pool_index, embedding, head_bias, pooled_grad
):
    place = jnp.stack([lax.axis_index(name) for name in (SHARD, "core", "zl", "x")]).astype(I32)
    packed = call(
        pack_body,
        "pack",
        shape((CHIPS, IDS + 80, LANES), BF16),
        [
            pltpu.SMEM((2,), I32),
            pltpu.SMEM((ROWS,), I32),
            pltpu.VMEM((ROWS, WIDTH), BF16),
            pltpu.VMEM((ROWS, WIDTH), BF16),
            pltpu.VMEM((2, VOC), I32),
            pltpu.VMEM((64, LANES), F32),
            pltpu.SemaphoreType.DMA((5,)),
        ],
        [ANY] * 5,
        room=56,
    )(lengths, token_ids, hidden, embed_grad, pool_index)
    own_index = exchange(packed, ("zl", "x"))
    rows, rest = call(
        spread_body,
        "spread",
        (shape((SHARDS, 96, LANES), BF16), shape((80, LANES), BF16)),
        specs=[VMEM],
        room=8,
    )(own_index)
    all_rows = exchange(rows, SHARD)
    other_embed = swap_over(embedding, "core")
    spots, embed = call(
        ready_body,
        "ready",
        (shape((CHIPS, 64, LANES), I32), shape((PAIR, VOC), BF16)),
        specs=[VMEM] * 3,
        us=2,
        room=8,
    )(own_index, embedding, other_embed)
    partial = call(
        logits_body,
        "logits",
        shape((GROUPS, 8, 2 * CHUNK + LANES), F32),
        [pltpu.VMEM((OWN * SEQ, PAIR), BF16)],
        [VMEM] * 4,
        us=6,
    )(all_rows, spots, embed, pooled_grad)
    keep, send = call(
        turn_body,
        "turn",
        (shape((OWN, COLS + 48, SEQ), BF16),) * 2,
        specs=[VMEM],
        us=3,
    )(all_rows)
    got = swap_over(send, "core")
    other_index = swap_over(own_index, "core")
    parts = exchange(partial, GROUP)
    parts, keep = lax.optimization_barrier((parts, keep))
    bias = jnp.pad(head_bias, (0, GROUPS * CHUNK - VOC)).reshape(GROUPS, 1, CHUNK)
    bias = lax.dynamic_index_in_dim(bias, lax.axis_index(GROUP), 0, keepdims=False)
    grad_block, more = call(
        slope_body,
        "slope",
        (shape((GROUPS, OWN, CHUNK), BF16), shape((1, LANES), F32)),
        specs=[VMEM, VMEM],
        room=8,
    )(parts, bias)
    all_grad = exchange(grad_block, GROUP)
    token_grad = call(
        token_body,
        "token_grad",
        shape((COLS, 4096), F32),
        [
            pltpu.VMEM((512, 1024), BF16),
            pltpu.VMEM((512, 1024), BF16),
            pltpu.VMEM((512, 512), F32),
        ],
        [SMEM, VMEM, VMEM],
        us=5,
        room=24,
    )(place, keep, got)
    all_grad, token_grad, other_index = lax.optimization_barrier((all_grad, token_grad, other_index))
    hidden_parts = call(
        hidden_body,
        "hidden_grad",
        shape((OWN * SEQ, PAIR), BF16),
        [
            pltpu.VMEM((OWN * SEQ, PAIR), F32),
            pltpu.VMEM((OWN * SEQ, 1024), BF16),
            pltpu.VMEM((OWN, 1024), F32),
        ],
        [VMEM] * 3,
        us=6,
    )(all_grad, spots, embed)
    token_grad = lax.cond(more[0, 0] > 0.0, add_rest, lambda total, rest: total, token_grad, rest)
    hidden_got = exchange(hidden_parts.reshape(CHIPS * SHARDS, ROWS, PAIR), HOME)
    other_grad = swap_over(all_grad, "core")
    embedding_grad, bias_grad = call(
        embed_body,
        "embedding_grad",
        (shape((COLS, VOC), F32), shape((1, VOC), F32)),
        [
            pltpu.VMEM((GROUPS, PASSAGES, CHUNK), F32),
            pltpu.VMEM((CHIPS, 64, LANES), I32),
        ],
        [VMEM] * 7,
        us=11,
        room=24,
    )(token_grad, all_grad, other_grad, spots, other_index, keep, got)
    hidden_grad = call(
        sum_body, "sum_shards", shape((ROWS, WIDTH), BF16), specs=[SMEM, VMEM], room=8
    )(place, hidden_got.reshape(CHIPS * SHARDS // 2, 2 * ROWS, PAIR))
    return hidden_grad, embedding_grad, bias_grad.reshape(VOC)


def solution(mesh):
    fine = Mesh(mesh.devices.reshape(2, 4, 2, 4, 8), GROUP + SHARD)
    every = P(GROUP + SHARD, None)
    split = P(GROUP, SHARD)
    return jax.shard_map(
        on_device,
        mesh=fine,
        in_specs=(every, every, P(GROUP + SHARD), P(GROUP), split, split, P(SHARD), split),
        out_specs=(every, split, P(SHARD)),
        check_vma=False,
    )
```

```python
import jax
import jax.numpy as jnp
from jax import lax
from jax.experimental import pallas as pl
from jax.experimental.pallas import tpu as pltpu
from jax.sharding import Mesh, PartitionSpec as P

F32 = jnp.float32
BF16 = jnp.bfloat16
I16 = jnp.int16
I32 = jnp.int32
LANES = 128
SMEM = pl.BlockSpec(memory_space=pltpu.SMEM)
VMEM = pl.BlockSpec(memory_space=pltpu.VMEM)
ANY = pl.BlockSpec(memory_space=pl.ANY)

GROUP = ("zl", "x", "core")
SHARD = ("zh", "y")
HOME = ("zh", "y", "zl", "x")
GROUPS = 16
SHARDS = 32
CHIPS = 8
SEQ = 128
PASSAGES = 32
OWN = 16
COLS = 64
PAIR = 128
WIDTH = 8 * PAIR
ROWS = 8
TILES = 31
VOC = TILES * LANES
CHUNK = 256
IDS = 16
SLOTS = 24


def lane_gather(table, index):
    numbers = lax.GatherDimensionNumbers(
        offset_dims=(),
        collapsed_slice_dims=(1,),
        start_index_map=(1,),
        operand_batching_dims=(0,),
        start_indices_batching_dims=(0,),
    )
    return lax.gather(
        table,
        index[..., None],
        numbers,
        (1, 1),
        mode=lax.GatherScatterMode.PROMISE_IN_BOUNDS,
    )


def load_spots(got_ref, spots):
    for m in range(CHIPS):
        spots[m] = got_ref[m, IDS + 16 :, :].astype(F32).astype(I32)


def spot_row(spots, p, tile):
    return spots[p // 2, pl.ds(2 * tile + p % 2, 1), :]


def pack_body(lengths, ids, hidden, grad, index, out_ref, *scratch):
    held, spots, sem = scratch[:5], scratch[5], scratch[6]
    copies = [
        pltpu.make_async_copy(source, target, sem.at[n])
        for n, (source, target) in enumerate(zip((lengths, ids, hidden, grad, index), held))
    ]
    for copy in copies:
        copy.start()
    for copy in copies:
        copy.wait()
    lengths_ref, ids_ref, hidden_ref, grad_ref, index_ref = held
    place = lax.axis_index(SHARD)
    swap = lax.axis_index("core") == 1
    limit = lengths_ref[place // (SEQ // ROWS)]
    spot = (place % (SEQ // ROWS)) * ROWS + lax.broadcasted_iota(I32, (ROWS, 1), 0)
    arrays = [hidden_ref[...].astype(F32), jnp.where(spot < limit, grad_ref[...].astype(F32), 0.0)]
    row = lax.broadcasted_iota(I32, (16, LANES), 0)
    lane = lax.broadcasted_iota(I32, (16, LANES), 1)
    digits = jnp.zeros((16, LANES), I32)
    for r in range(ROWS):
        digits = jnp.where(row == r, ids_ref[r], digits)
    digits = jnp.where(lane == 0, digits & 127, jnp.where(lane == 1, (digits >> 7) & 127, digits >> 14))
    digits = jnp.where(lane < 3, digits, 0).astype(F32).astype(BF16)
    spots[...] = jnp.zeros_like(spots)
    for tile in range(TILES):
        spots[2 * tile : 2 * tile + 2, :] = index_ref[:, tile * LANES : (tile + 1) * LANES].astype(F32)
    positions = spots[...].astype(BF16)
    for m in range(CHIPS):
        parts = []
        for array in arrays:
            pair = array[:, m * PAIR : (m + 1) * PAIR]
            other = jnp.concatenate([pair[:, COLS:], pair[:, :COLS]], axis=1)
            parts.append(jnp.where(swap, other, pair))
        out_ref[m, 0:IDS, :] = jnp.concatenate(parts, axis=0).astype(BF16)
        out_ref[m, IDS : IDS + 16, :] = digits
        out_ref[m, IDS + 16 :, :] = positions


def spread_body(got_ref, out_ref, rest_ref):
    tokens = 64
    hidden = []
    cotangents = []
    digits = []
    for m in range(CHIPS):
        rows = got_ref[m, 0:IDS, :].astype(F32)
        hidden.append(rows[0:ROWS])
        cotangents.append(rows[ROWS:])
        digits.append(got_ref[m, IDS : IDS + 16, :].astype(F32)[0:ROWS])
    hidden = jnp.concatenate(hidden, axis=0).astype(BF16)
    blank = jnp.zeros((LANES - tokens, LANES), F32)
    cotangents = jnp.concatenate(cotangents + [blank], axis=0)
    digits = jnp.concatenate(digits + [blank], axis=0)
    across = digits.T[0:16]

    def owner(ids):
        return ((ids + 0.5) * (1.0 / VOC)).astype(I32)

    lane = lax.broadcasted_iota(I32, (LANES, LANES), 1)
    row = lax.broadcasted_iota(I32, (LANES, LANES), 0)
    across_owner = owner(across[0:1] + 128.0 * across[1:2] + 16384.0 * across[2:3])
    across_owner = jnp.where(lane[0:1] < tokens, across_owner, SHARDS)
    down_owner = owner(digits[:, 0:1] + 128.0 * digits[:, 1:2] + 16384.0 * digits[:, 2:3])
    down_owner = jnp.where(row < tokens, down_owner, SHARDS + 1)
    same = down_owner == across_owner
    across_rank = jnp.sum(jnp.where(same & (row < lane), 1.0, 0.0), axis=0, keepdims=True).astype(I32)
    down_rank = jnp.sum(jnp.where(same & (lane < row), 1.0, 0.0), axis=1, keepdims=True).astype(I32)
    more = jnp.max(jnp.where(lane[0:1] < tokens, across_rank, 0), axis=1, keepdims=True) >= SLOTS
    rest = jnp.where(down_rank >= SLOTS, cotangents, 0.0)[0:tokens]
    rest_ref[...] = jnp.concatenate([rest, across], axis=0).astype(BF16)
    flag = jnp.where(more, 1.0, 0.0) + jnp.zeros((1, LANES), F32)
    packed = cotangents.astype(BF16)
    across = across.astype(BF16)
    slot = lax.broadcasted_iota(I32, (32, 1), 0)
    slot = jnp.where(slot < SLOTS, slot, -1)
    for s in range(SHARDS):
        place = jnp.where((across_owner == s) & (across_rank == slot), 1.0, 0.0).astype(BF16)
        rows = jnp.dot(place, packed, preferred_element_type=F32)
        codes = lax.dot_general(
            across, place, (((1,), (1,)), ((), ())), preferred_element_type=F32
        )
        codes = jnp.concatenate([codes[0:7], jnp.zeros((7, LANES - 32), F32)], axis=1)
        out_ref[s, 0:64, :] = hidden
        out_ref[s, 64:96, :] = jnp.concatenate([rows[0:SLOTS], codes, flag], axis=0).astype(BF16)


def turn_body(rows_ref, keep_out, send_out):
    for two in range(CHIPS // 2):
        for h in range(2):
            rows = rows_ref[h * 16 : h * 16 + 16, two * 16 : two * 16 + 16, :].astype(F32)
            for s in range(2):
                p = (2 * two + s) * 2 + h
                turned = rows[:, s * ROWS : (s + 1) * ROWS, :].reshape(SEQ, PAIR).T.astype(BF16)
                keep_out[p, 0:COLS, :] = turned[:COLS]
                send_out[p, 0:COLS, :] = turned[COLS:]
    keep = lax.broadcasted_iota(I32, (32, 1), 0) < SLOTS
    for four in range(SHARDS // 4):
        rows = [rows_ref[4 * four + s, 64:96, :].astype(F32) for s in range(4)]
        turned = jnp.concatenate([jnp.where(keep, r, 0.0) for r in rows], axis=0).T.astype(BF16)
        digits = jnp.concatenate([r[24:32, 0:32] for r in rows], axis=1)
        digits = jnp.concatenate([digits, jnp.zeros((8, LANES), F32)], axis=0).astype(BF16)
        for n, out in enumerate((keep_out, send_out)):
            for part in range(2):
                at = n * COLS + part * 32
                out[2 * four + part, COLS : COLS + 32, :] = turned[at : at + 32]
                out[2 * four + part, COLS + 32 :, :] = digits


def over_terms(step, one_chunk):
    full = VOC // step

    def loop(i, carry):
        one_chunk(pl.multiple_of(i * step, step), step)
        return carry

    lax.fori_loop(0, full, loop, 0)
    one_chunk(full * step, VOC - full * step)


def logits_body(
    rows_ref, got_ref, own_ref, other_ref, pooled_ref, out_ref, hidden_ref, embed_ref, spots
):
    here = lax.broadcasted_iota(I32, (8, 1), 0)
    embed_ref[0:COLS, :] = own_ref[...]
    embed_ref[COLS:, :] = other_ref[...]
    load_spots(got_ref, spots)
    for two in range(CHIPS // 2):
        for h in range(2):
            rows = rows_ref[h * 16 : h * 16 + 16, two * 16 : two * 16 + 16, :].astype(F32)
            for s in range(2):
                p = (2 * two + s) * 2 + h
                tokens = rows[:, s * ROWS : (s + 1) * ROWS, :].reshape(SEQ, PAIR)
                hidden_ref[p * SEQ : (p + 1) * SEQ, :] = tokens.astype(BF16)

    def one_chunk(first, width):
        lanes = pl.ds(first, width)
        embed = embed_ref[:, lanes]
        for p in range(OWN):
            scores = jnp.dot(
                hidden_ref[p * SEQ : (p + 1) * SEQ, :], embed, preferred_element_type=F32
            )
            index = jnp.concatenate(
                [spot_row(spots, p, first // LANES + n) for n in range(width // LANES)], axis=1
            )
            high = jnp.broadcast_to(index >> 3, (8, width))
            rows = scores[0:8]
            for n in range(1, SEQ // 8):
                rows = jnp.where(high == n, scores[8 * n : 8 * n + 8], rows)
            picked = jnp.sum(jnp.where((index & 7) == here, rows, 0.0), axis=0, keepdims=True)
            for at in range(0, width, CHUNK):
                some = min(CHUNK, width - at)
                left = p // 8 * CHUNK
                out_ref[first // CHUNK + at // CHUNK, p % 8 : p % 8 + 1, left : left + some] = picked[
                    :, at : at + some
                ]
        for at in range(0, width, CHUNK):
            some = min(CHUNK, width - at)
            for half in range(some // LANES):
                upstream = pooled_ref[:, pl.ds(first + at + half * LANES, LANES)]
                out_ref[first // CHUNK + at // CHUNK, 2 * half : 2 * half + 2, 2 * CHUNK :] = upstream

    over_terms(2048, one_chunk)
    more = rows_ref[0, 80:96, :].astype(F32)
    for s in range(1, SHARDS):
        more = jnp.maximum(more, rows_ref[s, 80:96, :].astype(F32))
    tail = jnp.concatenate([more[15:16], jnp.zeros((3, LANES), F32)], axis=0)
    for g in range(GROUPS):
        out_ref[g, 4:8, 2 * CHUNK :] = tail
    for left in range(LANES, 2 * CHUNK, CHUNK):
        out_ref[GROUPS - 1, :, left : left + LANES] = jnp.zeros((8, LANES), F32)
    out_ref[GROUPS - 1, 2:4, 2 * CHUNK :] = jnp.zeros((2, LANES), F32)


def slope_body(part_ref, bias_ref, out_ref, more_ref):
    logits = []
    upstream = []
    for c in range(2):
        total = part_ref[c, :, 0 : 2 * CHUNK]
        for m in range(1, CHIPS):
            total = total + part_ref[2 * m + c, :, 0 : 2 * CHUNK]
        logits += [total[:, :CHUNK], total[:, CHUNK:]]
        for m in range(CHIPS):
            halves = part_ref[2 * m + c, :, 2 * CHUNK :]
            upstream.append(jnp.concatenate([halves[0:2], halves[2:4]], axis=1))
    logits = jnp.concatenate(logits, axis=0) + bias_ref[...]
    upstream = jnp.concatenate(upstream, axis=0)
    softened = jnp.maximum(logits, 0.0) + jnp.log1p(jnp.exp(-jnp.abs(logits)))
    pooled = jnp.log1p(softened)
    sigmoid = 1.0 / (1.0 + jnp.exp(-logits))
    slope = sigmoid / (1.0 + softened)
    mean_pooled = jnp.sum(pooled, axis=0, keepdims=True) / PASSAGES
    grad = ((upstream + mean_pooled) * slope).astype(BF16)
    more = part_ref[0, :, 2 * CHUNK :]
    for g in range(1, GROUPS):
        more = jnp.maximum(more, part_ref[g, :, 2 * CHUNK :])
    more_ref[...] = more[4:5]
    for g in range(GROUPS):
        out_ref[g] = grad[g % 2 * OWN : g % 2 * OWN + OWN]


def hidden_body(
    grad_ref, got_ref, own_ref, other_ref, out_ref, total, left, embed_ref, grads, spots
):
    here = lax.broadcasted_iota(I32, (SEQ, LANES), 0).astype(I16)
    zero = jnp.zeros((), BF16)
    load_spots(got_ref, spots)
    embed_ref[0:COLS, :] = own_ref[...]
    embed_ref[COLS:, :] = other_ref[...]
    total[...] = jnp.zeros_like(total)

    def one_chunk(first, width):
        for at in range(0, width, CHUNK):
            grads[:, at : at + CHUNK] = grad_ref[first // CHUNK + at // CHUNK].astype(F32)
        embed = embed_ref[:, pl.ds(first, width)]
        for group in range(0, OWN, 4):
            for p in range(group, group + 4):
                for tile in range(width // LANES):
                    lanes = slice(tile * LANES, (tile + 1) * LANES)
                    index = spot_row(spots, p, first // LANES + tile)
                    index = jnp.broadcast_to(index, (16, LANES)).astype(I16)
                    value = jnp.broadcast_to(grads[p : p + 1, lanes], (16, LANES)).astype(BF16)
                    index = jnp.concatenate([index] * 8, axis=0)
                    value = jnp.concatenate([value] * 8, axis=0)
                    left[p * SEQ : (p + 1) * SEQ, lanes] = jnp.where(index == here, value, zero)
            rows = slice(group * SEQ, (group + 4) * SEQ)
            total[rows, :] += lax.dot_general(
                left[rows, 0:width], embed, (((1,), (1,)), ((), ())), preferred_element_type=F32
            )

    over_terms(1024, one_chunk)
    for two in range(CHIPS // 2):
        for h in range(2):
            halves = []
            for s in range(2):
                p = (2 * two + s) * 2 + h
                halves.append(total[p * SEQ : (p + 1) * SEQ, :].reshape(16, ROWS, PAIR))
            rows = jnp.concatenate(halves, axis=1).astype(BF16)
            out_ref[h * 16 : h * 16 + 16, two * 16 : two * 16 + 16, :] = rows


def rest_body(place_ref, every_ref, swapped_ref, total_ref, out_ref, total):
    base = place_ref[0] * VOC
    low_row = lax.broadcasted_iota(I32, (512, LANES), 0)
    total[...] = jnp.zeros_like(total)
    for n, ref in enumerate((every_ref, swapped_ref)):

        def pair(k, carry, n=n, ref=ref):
            rows = [ref[2 * k + part].astype(F32) for part in range(2)]
            digits = jnp.concatenate([r[64:72, 0:64] for r in rows], axis=1).astype(I32)
            local = (digits[2:3] << 14) + (digits[1:2] << 7) + digits[0:1] - base
            inside = (local >= 0) & (local < VOC)
            high = jnp.where(inside, local >> 9, 15)
            turned = jnp.concatenate([r[0:64] for r in rows], axis=0).T[n * COLS : (n + 1) * COLS]
            left = [jnp.where(high == h, turned, 0.0) for h in range(8)]
            right = jnp.where(low_row == (local & 511), 1.0, 0.0)
            total[...] += lax.dot_general(
                jnp.concatenate(left, axis=0).astype(BF16),
                right.astype(BF16),
                (((1,), (1,)), ((), ())),
                preferred_element_type=F32,
            )
            return carry

        lax.fori_loop(0, SHARDS // 2, pair, 0)
    for h in range(8):
        lanes = slice(h * 512, (h + 1) * 512)
        out_ref[:, lanes] = total_ref[:, lanes] + total[h * COLS : (h + 1) * COLS, :]


def token_body(place_ref, keep_ref, got_ref, out_ref, left, right, total):
    base = place_ref[0] * VOC
    low_row = lax.broadcasted_iota(I32, (512, LANES), 0).astype(I16)
    zero = jnp.zeros((), BF16)
    one = jnp.ones((), BF16)
    total[...] = jnp.zeros_like(total)

    def token_block(table_ref):
        for group in range(8):
            digits = table_ref[2 * group, COLS + 32 :, :].astype(F32).astype(I32)
            local = (digits[2:3] << 14) + (digits[1:2] << 7) + digits[0:1] - base
            inside = (local >= 0) & (local < VOC)
            high = jnp.where(inside, local >> 9, 15)
            high = jnp.broadcast_to(high, (16, LANES)).astype(I16)
            low = jnp.broadcast_to(local & 511, (16, LANES)).astype(I16)
            high = jnp.concatenate([high] * 4, axis=0)
            low = jnp.concatenate([low] * 32, axis=0)
            cotangents = jnp.concatenate(
                [table_ref[2 * group + part, COLS : COLS + 32, :] for part in range(2)], axis=0
            )
            lanes = slice(group * LANES, (group + 1) * LANES)
            for h in range(8):
                left[h * COLS : (h + 1) * COLS, lanes] = jnp.where(
                    high == jnp.int16(h), cotangents, zero
                )
            right[:, lanes] = jnp.where(low_row == low, one, zero)
        total[...] += lax.dot_general(
            left[...], right[...], (((1,), (1,)), ((), ())), preferred_element_type=F32
        )

    for table_ref in (keep_ref, got_ref):
        token_block(table_ref)
    for h in range(8):
        out_ref[:, h * 512 : (h + 1) * 512] = total[h * COLS : (h + 1) * COLS, :]


def embed_body(
    token_ref, own_grad, other_grad, own_index, other_index, keep_ref, got_ref, out_ref, bias_ref, grads, own_spots, other_spots
):
    load_spots(own_index, own_spots)
    load_spots(other_index, other_spots)
    for g in range(GROUPS):
        grads[g, 0:OWN, :] = own_grad[g].astype(F32)
        grads[g, OWN:, :] = other_grad[g].astype(F32)

    def one_tile(tile, carry):
        lanes = pl.ds(pl.multiple_of(tile * LANES, LANES), LANES)
        half = pl.ds(pl.multiple_of((tile % 2) * LANES, LANES), LANES)
        totals = [token_ref[d : d + 16, lanes] for d in range(0, COLS, 16)]
        for n, (table_ref, spots) in enumerate(((keep_ref, own_spots), (got_ref, other_spots))):
            for p in range(OWN):
                index = spot_row(spots, p, tile)
                index = jnp.broadcast_to(index, (16, LANES)).astype(I16)
                value = grads[tile // 2, n * OWN + p : n * OWN + p + 1, half]
                for d in range(COLS // 16):
                    picked = lane_gather(table_ref[p, d * 16 : d * 16 + 16, :], index).astype(F32)
                    totals[d] = totals[d] + picked * value
        for d in range(COLS // 16):
            out_ref[d * 16 : d * 16 + 16, lanes] = totals[d]
        bias_ref[:, lanes] = jnp.sum(grads[tile // 2, :, half], axis=0, keepdims=True)
        return carry

    lax.fori_loop(0, TILES, one_tile, 0)


def sum_body(place_ref, part_ref, out_ref):
    swap = place_ref[1] == 1
    total = part_ref[0].astype(F32)
    for s in range(1, SHARDS):
        total = total + part_ref[s].astype(F32)
    for m in range(CHIPS):
        pair = total[m * ROWS : (m + 1) * ROWS]
        other = jnp.concatenate([pair[:, COLS:], pair[:, :COLS]], axis=1)
        out_ref[:, m * PAIR : (m + 1) * PAIR] = jnp.where(swap, other, pair).astype(BF16)


def call(body, name, out, scratch=(), specs=None, us=1, out_specs=None, room=24):
    extra = {} if out_specs is None else {"out_specs": out_specs}
    return pl.pallas_call(
        body,
        out_shape=out,
        in_specs=specs,
        scratch_shapes=scratch,
        compiler_params=pltpu.CompilerParams(vmem_limit_bytes=room * 1024 * 1024),
        cost_estimate=pl.CostEstimate(flops=0, bytes_accessed=3_700_000 * us, transcendentals=0),
        name=name,
        **extra,
    )


def shape(dims, dtype):
    return jax.ShapeDtypeStruct(dims, dtype)


def exchange(x, axis):
    return lax.all_to_all(x, axis, split_axis=0, concat_axis=0, tiled=True)


def swap_over(x, axis):
    return lax.ppermute(x, axis, [(0, 1), (1, 0)])


def add_rest(total, rest):
    ring = [(k, (k + 1) % SHARDS) for k in range(SHARDS)]

    def step(k, carry):
        held, every = carry
        held = lax.ppermute(held, SHARD, ring)
        return held, lax.dynamic_update_index_in_dim(every, held, k, 0)

    every = jnp.zeros((SHARDS,) + rest.shape, BF16).at[0].set(rest)
    every = lax.fori_loop(1, SHARDS, step, (rest, every))[1]
    place = jnp.stack([lax.axis_index(SHARD)]).astype(I32)
    return call(
        rest_body,
        "rest",
        shape(total.shape, F32),
        [pltpu.VMEM((512, 512), F32)],
        [SMEM, VMEM, VMEM, VMEM],
    )(place, every, swap_over(every, "core"), total)


def on_device(
    hidden, embed_grad, token_ids, lengths, pool_index, embedding, head_bias, pooled_grad
):
    place = jnp.stack([lax.axis_index(name) for name in (SHARD, "core", "zl", "x")]).astype(I32)
    packed = call(
        pack_body,
        "pack",
        shape((CHIPS, IDS + 80, LANES), BF16),
        [
            pltpu.SMEM((2,), I32),
            pltpu.SMEM((ROWS,), I32),
            pltpu.VMEM((ROWS, WIDTH), BF16),
            pltpu.VMEM((ROWS, WIDTH), BF16),
            pltpu.VMEM((2, VOC), I32),
            pltpu.VMEM((64, LANES), F32),
            pltpu.SemaphoreType.DMA((5,)),
        ],
        [ANY] * 5,
        room=56,
    )(lengths, token_ids, hidden, embed_grad, pool_index)
    own_index = exchange(packed, ("zl", "x"))
    rows, rest = call(
        spread_body,
        "spread",
        (shape((SHARDS, 96, LANES), BF16), shape((80, LANES), BF16)),
        specs=[VMEM],
        room=8,
    )(own_index)
    all_rows = exchange(rows, SHARD)
    other_embed = swap_over(embedding, "core")
    partial = call(
        logits_body,
        "logits",
        shape((GROUPS, 8, 2 * CHUNK + LANES), F32),
        [
            pltpu.VMEM((OWN * SEQ, PAIR), BF16),
            pltpu.VMEM((PAIR, VOC), BF16),
            pltpu.VMEM((CHIPS, 64, LANES), I32),
        ],
        [VMEM] * 5,
        us=6,
    )(all_rows, own_index, embedding, other_embed, pooled_grad)
    keep, send = call(
        turn_body,
        "turn",
        (shape((OWN, COLS + 48, SEQ), BF16),) * 2,
        specs=[VMEM],
        us=3,
    )(all_rows)
    got = swap_over(send, "core")
    other_index = swap_over(own_index, "core")
    parts = exchange(partial, GROUP)
    parts, keep = lax.optimization_barrier((parts, keep))
    bias = jnp.pad(head_bias, (0, GROUPS * CHUNK - VOC)).reshape(GROUPS, 1, CHUNK)
    bias = lax.dynamic_index_in_dim(bias, lax.axis_index(GROUP), 0, keepdims=False)
    grad_block, more = call(
        slope_body,
        "slope",
        (shape((GROUPS, OWN, CHUNK), BF16), shape((1, LANES), F32)),
        specs=[VMEM, VMEM],
        room=8,
    )(parts, bias)
    all_grad = exchange(grad_block, GROUP)
    token_grad = call(
        token_body,
        "token_grad",
        shape((COLS, 4096), F32),
        [
            pltpu.VMEM((512, 1024), BF16),
            pltpu.VMEM((512, 1024), BF16),
            pltpu.VMEM((512, 512), F32),
        ],
        [SMEM, VMEM, VMEM],
        us=5,
        room=24,
    )(place, keep, got)
    all_grad, token_grad, other_index = lax.optimization_barrier((all_grad, token_grad, other_index))
    hidden_parts = call(
        hidden_body,
        "hidden_grad",
        shape((SHARDS, CHIPS * ROWS, PAIR), BF16),
        [
            pltpu.VMEM((OWN * SEQ, PAIR), F32),
            pltpu.VMEM((OWN * SEQ, 1024), BF16),
            pltpu.VMEM((PAIR, VOC), BF16),
            pltpu.VMEM((OWN, 1024), F32),
            pltpu.VMEM((CHIPS, 64, LANES), I32),
        ],
        [VMEM] * 4,
        us=6,
    )(all_grad, own_index, embedding, other_embed)
    token_grad = lax.cond(more[0, 0] > 0.0, add_rest, lambda total, rest: total, token_grad, rest)
    hidden_got = exchange(hidden_parts.reshape(CHIPS * SHARDS, ROWS, PAIR), HOME)
    other_grad = swap_over(all_grad, "core")
    embedding_grad, bias_grad = call(
        embed_body,
        "embedding_grad",
        (shape((COLS, VOC), F32), shape((1, VOC), F32)),
        [
            pltpu.VMEM((GROUPS, PASSAGES, CHUNK), F32),
            pltpu.VMEM((CHIPS, 64, LANES), I32),
            pltpu.VMEM((CHIPS, 64, LANES), I32),
        ],
        [VMEM] * 7,
        us=11,
        room=24,
    )(token_grad, all_grad, other_grad, own_index, other_index, keep, got)
    hidden_grad = call(
        sum_body, "sum_shards", shape((ROWS, WIDTH), BF16), specs=[SMEM, VMEM], room=8
    )(place, hidden_got.reshape(SHARDS, CHIPS * ROWS, PAIR))
    return hidden_grad, embedding_grad, bias_grad.reshape(VOC)


def solution(mesh):
    fine = Mesh(mesh.devices.reshape(2, 4, 2, 4, 8), GROUP + SHARD)
    every = P(GROUP + SHARD, None)
    split = P(GROUP, SHARD)
    return jax.shard_map(
        on_device,
        mesh=fine,
        in_specs=(every, every, P(GROUP + SHARD), P(GROUP), split, split, P(SHARD), split),
        out_specs=(every, split, P(SHARD)),
        check_vma=False,
    )
```
